32 devices in a mesh: src: 2 (over core), dp: 8 (over z, y), seq: 2 (over x).
Axes of the slice: x: 2, y: 2, z: 4, core: 2. Of those that a mesh axis runs over, the one named last changes fastest.
Arguments:
- inputs: bfloat16 [2, 8, 2, 256, 768], P('src', 'dp', None, 'seq'), may hold values from -6 to 6
- cotangent: bfloat16 [2, 8, 2, 256, 768], P('src', 'dp', None, 'seq'), may hold values from -6 to 6
- row_counts: int32 [2, 8], P('src', 'dp'), may hold values from 0 to 2
- response_mask: int32 [2, 8, 2, 256], P('src', 'dp', None, 'seq'), may hold values 0 or 1
- norm1_gain: bfloat16 [768], replicated, may hold values from 0.5 to 1.5
- norm1_bias: bfloat16 [768], replicated, may hold values from -1.5 to 1.5
- qkv_weight: bfloat16 [768, 2304], replicated, may hold values from -0.21875 to 0.21875
- qv_bias: bfloat16 [2, 768], replicated, may hold values from -1.5 to 1.5
- out_weight: bfloat16 [768, 768], replicated, may hold values from -3 to 3
- out_bias: bfloat16 [768], replicated, may hold values from -1.5 to 1.5
- norm2_gain: bfloat16 [768], replicated, may hold values from 0.5 to 1.5
- norm2_bias: bfloat16 [768], replicated, may hold values from -1.5 to 1.5
- up_weight: bfloat16 [768, 3072], replicated, may hold values from -0.21875 to 0.21875
- up_bias: bfloat16 [3072], replicated, may hold values from -1.5 to 1.5
- down_weight: bfloat16 [3072, 768], replicated, may hold values from -0.109375 to 0.109375
- down_bias: bfloat16 [768], replicated, may hold values from -1.5 to 1.5
Outputs:
- output: bfloat16 [2, 8, 2, 256, 768], P('src', 'dp', None, 'seq')
- input_grad: bfloat16 [2, 8, 2, 256, 768], P('src', 'dp', None, 'seq')
- source_counts: int32 [2], replicated
- grad_norm1_gain: float32 [768], P('dp')
- grad_norm1_bias: float32 [768], P('dp')
- grad_qkv_weight: float32 [768, 2304], P('dp')
- grad_qv_bias: float32 [2, 768], P(None, 'dp')
- grad_out_weight: float32 [768, 768], P('dp')
- grad_out_bias: float32 [768], P('dp')
- grad_norm2_gain: float32 [768], P('dp')
- grad_norm2_bias: float32 [768], P('dp')
- grad_up_weight: float32 [768, 3072], P('dp')
- grad_up_bias: float32 [3072], P('dp')
- grad_down_weight: float32 [3072, 768], P('dp')
- grad_down_bias: float32 [768], P('dp')
The draws below stay inside these ranges and needn't reach their ends.
Inputs may be any that keep to these rules, and one draw needn't show every extreme that they name: `row_counts`: rows held by a data group; slots numbered 2 - 1 down to the count are padding.
All inputs are finite; a program needn't handle non-finite values. No bound on the sum of `response_mask` on one device may be relied on, other than what follows from the above.
Results may differ from the reference program's by a relative error of at most 0.018.
Values may be sent and summed in bfloat16 or wider, within the bound.
No kernel may reach another device: no remote copies, remote signals or barrier semaphores. Data moves between devices by JAX's collectives and lax.ppermute only.
A program may use at most 128 MiB of HBM per device.

```python
import jax
import jax.numpy as jnp
from jax import lax

D = 768
H = 12
HD = 64
FF = 3072
RCAP = 2
LEN = 256
N_SRC = 2
N_DP = 8


def with_ends(entries, key, least, largest):
    longest = entries.shape.index(max(entries.shape))
    spots = []
    for shift in (0, 1):
        where = [jax.random.randint(jax.random.fold_in(key, axis), (), 0, length) for axis, length in enumerate(entries.shape)]
        where[longest] = (where[longest] + shift) % entries.shape[longest]
        spots.append(tuple(where))
    return entries.at[spots[0]].set(least).at[spots[1]].set(largest)


def block_scale(own_key, dims, shards, low, high):
    def one(axis_at, parts):
        heights = jax.random.uniform(jax.random.fold_in(jax.random.fold_in(own_key, 6), axis_at), (parts,), jnp.float32, low / len(shards), high / len(shards))
        return jnp.repeat(jnp.exp(heights), dims[axis_at] // parts).reshape((-1,) + (1,) * (len(dims) - axis_at - 1))

    factor_of = one(*shards[0])
    for cut in shards[1:]:
        factor_of = factor_of * one(*cut)
    return factor_of


def noise(stream_key, dims, deviation, reach, shards=(), held_as=jnp.bfloat16):
    values = deviation * jax.random.normal(stream_key, dims, jnp.float32)
    if shards:
        values = values * block_scale(stream_key, dims, shards, -0.22, 0.18)
    return jnp.clip(values, -reach, reach).astype(held_as)


def setup_inputs(seed: int = 0) -> dict:
    key_list = jax.random.split(jax.random.key(seed), 17)
    return {
        "inputs": noise(key_list[0], (N_SRC, N_DP, RCAP, LEN, D), 1.0, 6.0, ((0, 2), (1, 8), (3, 2))),
        "cotangent": noise(key_list[1], (N_SRC, N_DP, RCAP, LEN, D), 1.0, 6.0, ((0, 2), (1, 8), (3, 2))),
        "row_counts": with_ends(jax.random.randint(key_list[2], (N_SRC, N_DP), 0, RCAP + 1), jax.random.fold_in(key_list[2], 1), 0, RCAP).astype(jnp.int32),
        "response_mask": with_ends((jax.random.randint(key_list[3], (N_SRC, N_DP, RCAP, LEN), 0, 4) < 3).astype(jnp.int32), jax.random.fold_in(key_list[3], 1), 0, 1),
        "norm1_gain": jnp.clip(1.0 + 0.1 * jax.random.normal(key_list[4], (D,), jnp.float32), 0.5, 1.5).astype(jnp.bfloat16),
        "norm1_bias": noise(key_list[5], (D,), 0.3, 1.5),
        "qkv_weight": noise(key_list[6], (D, 3 * D), D ** -0.5, 0.21875),
        "qv_bias": noise(key_list[7], (2, D), 0.3, 1.5),
        "out_weight": noise(key_list[8], (D, D), 4 ** -0.5, 3.0),
        "out_bias": noise(key_list[9], (D,), 0.3, 1.5),
        "norm2_gain": jnp.clip(1.0 + 0.1 * jax.random.normal(key_list[10], (D,), jnp.float32), 0.5, 1.5).astype(jnp.bfloat16),
        "norm2_bias": noise(key_list[11], (D,), 0.3, 1.5),
        "up_weight": noise(key_list[12], (D, FF), D ** -0.5, 0.21875),
        "up_bias": noise(key_list[13], (FF,), 0.3, 1.5),
        "down_weight": noise(key_list[14], (FF, D), FF ** -0.5, 0.109375),
        "down_bias": noise(key_list[15], (D,), 0.3, 1.5),
    }


@jax.custom_vjp
def low(v):
    return lax.optimization_barrier(v.astype(jnp.bfloat16)).astype(jnp.float32)

@jax.custom_vjp
def low_back(v):
    return v

def low_keep(v):
    return (low(v), None)

def low_pass(kept, grad):
    return (grad,)

def back_keep(v):
    return (v, None)

def back_low(kept, grad):
    return (low(grad),)
low.defvjp(low_keep, low_pass)
low_back.defvjp(back_keep, back_low)
EPS = 1e-05
HIGH = lax.Precision.HIGHEST

def norm_apply(values, scaling, offset):
    centre = lax.optimization_barrier(jnp.mean(values, axis=-1, keepdims=True))
    centered = values - centre
    spread = lax.optimization_barrier(jnp.mean(centered * centered, axis=-1, keepdims=True))
    return centered * lax.rsqrt(spread + EPS) * scaling + offset

def layer_row(source, params):
    norm1_gain, norm1_bias, qkv_weight, qv_bias, out_weight, out_bias, norm2_gain, norm2_bias, up_weight, up_bias, down_weight, down_bias = params
    length = source.shape[0]
    normed = low(norm_apply(source, norm1_gain, norm1_bias))
    joined = jnp.concatenate([qv_bias[0], jnp.zeros_like(qv_bias[0]), qv_bias[1]])
    projected = low_back(jnp.dot(normed, qkv_weight, precision=HIGH) + joined)
    query = low(projected[:, :D]).reshape(length, H, HD)
    keys = low(projected[:, D:2 * D]).reshape(length, H, HD)
    values = low(projected[:, 2 * D:]).reshape(length, H, HD)
    allowed = jnp.arange(length)[:, None] >= jnp.arange(length)[None, :]
    scores = jnp.einsum('qhd,khd->hqk', query, keys, precision=HIGH) * HD ** (-0.5)
    scores = low_back(jnp.where(allowed[None], scores, -1e+30))
    probs = low(jax.nn.softmax(scores, axis=-1))
    attended = jnp.einsum('hqk,khd->qhd', probs, values, precision=HIGH).reshape(length, D)
    attended = low(low_back(attended))
    branch = low_back(jnp.dot(attended, out_weight, precision=HIGH) + out_bias)
    middle = source + branch
    normed_two = low(norm_apply(middle, norm2_gain, norm2_bias))
    hidden = low_back(jnp.dot(normed_two, up_weight, precision=HIGH) + up_bias)
    active = low(jax.nn.gelu(hidden, approximate=True))
    branch_two = low_back(jnp.dot(active, down_weight, precision=HIGH) + down_bias)
    return middle + branch_two

def reference(inputs, cotangent, row_counts, response_mask, norm1_gain, norm1_bias, qkv_weight, qv_bias, out_weight, out_bias, norm2_gain, norm2_bias, up_weight, up_bias, down_weight, down_bias):
    params = tuple((p.astype(jnp.float32) for p in (norm1_gain, norm1_bias, qkv_weight, qv_bias, out_weight, out_bias, norm2_gain, norm2_bias, up_weight, up_bias, down_weight, down_bias)))
    present = (jnp.arange(RCAP)[None, None, :] < row_counts[:, :, None]).astype(jnp.int32)
    rows_in = inputs.astype(jnp.float32).reshape(-1, LEN, D)
    rows_cot = cotangent.astype(jnp.float32).reshape(-1, LEN, D)
    rows_mask = response_mask.reshape(-1, LEN)
    rows_present = present.reshape(-1)

    def step(totals, item):
        row_in, row_cot, row_mask, row_present = item
        weight = (row_mask * row_present).astype(jnp.float32)

        def compute(unused):
            result, pull = jax.vjp(layer_row, row_in, params)
            grad_in, grad_params = pull(row_cot * weight[:, None])
            return (result, grad_in, grad_params)

        def padding(unused):
            return (jnp.zeros_like(row_in), jnp.zeros_like(row_in), jax.tree.map(jnp.zeros_like, params))
        result, grad_in, grad_params = lax.cond(row_present > 0, compute, padding, 0)
        totals = jax.tree.map(lambda a, b: a + b, totals, grad_params)
        return (totals, (result, grad_in))
    start = jax.tree.map(jnp.zeros_like, params)
    totals, (results, grads_in) = lax.scan(step, start, (rows_in, rows_cot, rows_mask, rows_present))
    source_counts = lax.optimization_barrier(jnp.sum(response_mask * present[..., None], axis=(1, 2, 3))).astype(jnp.int32)
    whole = jnp.sum(source_counts).astype(jnp.float32)
    g = [t / whole for t in totals]
    output = results.reshape(inputs.shape).astype(jnp.bfloat16)
    input_grad = grads_in.reshape(inputs.shape).astype(jnp.bfloat16)
    return (output, input_grad, source_counts, g[0], g[1], g[2], g[3], g[4], g[5], g[6], g[7], g[8], g[9], g[10], g[11])
```

```python
import functools
import math

import jax
import jax.numpy as jnp
from jax import lax
from jax.sharding import PartitionSpec as P

H = 12
HD = 64


EPS = 1e-05
NEGATIVE = -1e30


def norm_apply(values, scaling, offset):
    centre = jnp.mean(values, axis=-1, keepdims=True)
    centered = values - centre
    spread = jnp.mean(centered * centered, axis=-1, keepdims=True)
    return centered * lax.rsqrt(spread + EPS) * scaling + offset


def causal_scores(query_part, keys_part, allowed):
    scores = jnp.einsum(
        "rqhd,rkhd->rhqk", query_part, keys_part, preferred_element_type=jnp.float32
    )
    scores = scores * HD ** (-0.5)
    return jnp.where(allowed, scores, NEGATIVE)


def attend_forward(query_part, keys_part, values_part, allowed):
    scores = causal_scores(query_part, keys_part, allowed)
    highest = jnp.max(scores, axis=-1, keepdims=True)
    powers = jnp.exp(scores - highest)
    totals = jnp.sum(powers, axis=-1, keepdims=True)
    probs_low = (powers / totals).astype(jnp.bfloat16)
    mixed = jnp.einsum(
        "rhqk,rkhd->rqhd", probs_low, values_part, preferred_element_type=jnp.float32
    )
    return (mixed, highest, totals)


def attend_backward(query_part, keys_part, values_part, grad_part, highest, totals, allowed):
    scores = causal_scores(query_part, keys_part, allowed)
    probs = jnp.exp(scores - highest) / totals
    probs_low = probs.astype(jnp.bfloat16)
    grad_probs = jnp.einsum(
        "rqhd,rkhd->rhqk", grad_part, values_part, preferred_element_type=jnp.float32
    )
    inner = jnp.sum(probs * grad_probs, axis=-1, keepdims=True)
    grad_scores = (probs * (grad_probs - inner)).astype(jnp.bfloat16)
    factor = HD ** (-0.5)
    grad_query = (
        jnp.einsum("rhqk,rkhd->rqhd", grad_scores, keys_part, preferred_element_type=jnp.float32)
        * factor
    )
    grad_keys = (
        jnp.einsum("rhqk,rqhd->rkhd", grad_scores, query_part, preferred_element_type=jnp.float32)
        * factor
    )
    grad_values = jnp.einsum(
        "rhqk,rqhd->rkhd", probs_low, grad_part, preferred_element_type=jnp.float32
    )
    return (grad_query, grad_keys, grad_values)


def body_generic(
    inputs,
    cotangent,
    row_counts,
    response_mask,
    norm1_gain,
    norm1_bias,
    qkv_weight,
    qv_bias,
    out_weight,
    out_bias,
    norm2_gain,
    norm2_bias,
    up_weight,
    up_bias,
    down_weight,
    down_bias,
):
    slots = inputs.shape[2]
    piece_len = inputs.shape[3]
    features = inputs.shape[4]
    tokens = slots * piece_len
    blocks_seq = lax.axis_size("seq")
    row_len = piece_len * blocks_seq
    group_heads = math.gcd(H, 4)
    bfloat = jnp.bfloat16
    single = jnp.float32
    present_int = (jnp.arange(slots) < row_counts[0, 0]).astype(jnp.int32)
    weight = (response_mask[0, 0] * present_int[:, None]).astype(single)
    local_count = jnp.sum(response_mask[0, 0] * present_int[:, None])
    picked = jnp.where(jnp.arange(lax.axis_size("src")) == lax.axis_index("src"), local_count, 0)
    source_counts = lax.psum(picked, ("src", "dp", "seq"))
    whole = jnp.sum(source_counts).astype(single)
    source = inputs.reshape(tokens, features).astype(single)
    normed, norm1_pull = jax.vjp(
        norm_apply, source, norm1_gain.astype(single), norm1_bias.astype(single)
    )
    normed_low = normed.astype(bfloat)
    bias_query = qv_bias[0].astype(single)
    joined = jnp.concatenate([bias_query, jnp.zeros_like(bias_query), qv_bias[1].astype(single)])
    projected = jnp.dot(normed_low, qkv_weight, preferred_element_type=single) + joined
    proj_low = projected.astype(bfloat)
    query = proj_low[:, :features].reshape(slots, piece_len, H, HD)
    keys_own = proj_low[:, features : 2 * features].reshape(slots, piece_len, features)
    values_own = proj_low[:, 2 * features :].reshape(slots, piece_len, features)
    keys_all, values_all = (
        lax.all_gather(keys_own, "seq", axis=1, tiled=True),
        lax.all_gather(values_own, "seq", axis=1, tiled=True),
    )
    query_pos = lax.axis_index("seq") * piece_len + jnp.arange(piece_len)
    allowed = query_pos[:, None] >= jnp.arange(row_len)[None, :]
    keys_heads = keys_all.reshape(slots, row_len, H, HD)
    values_heads = values_all.reshape(slots, row_len, H, HD)
    mixed_parts = []
    kept_stats = []
    for group in range(H // group_heads):
        first = group * group_heads
        last = first + group_heads
        mixed, highest, totals = attend_forward(
            query[:, :, first:last],
            keys_heads[:, :, first:last],
            values_heads[:, :, first:last],
            allowed,
        )
        mixed_parts.append(mixed)
        kept_stats.append((highest, totals))
    attended = jnp.concatenate(mixed_parts, axis=2).reshape(tokens, features)
    attended_low = attended.astype(bfloat)
    branch = jnp.dot(attended_low, out_weight, preferred_element_type=single) + out_bias.astype(
        single
    )
    middle = source + branch
    normed_two, norm2_pull = jax.vjp(
        norm_apply, middle, norm2_gain.astype(single), norm2_bias.astype(single)
    )
    normed_two_low = normed_two.astype(bfloat)
    hidden = jnp.dot(normed_two_low, up_weight, preferred_element_type=single) + up_bias.astype(
        single
    )
    active, gelu_pull = jax.vjp(functools.partial(jax.nn.gelu, approximate=True), hidden)
    active_low = active.astype(bfloat)
    branch_two = jnp.dot(active_low, down_weight, preferred_element_type=single) + down_bias.astype(
        single
    )
    result = middle + branch_two
    present_tok = jnp.repeat(present_int.astype(single), piece_len)
    output = (result * present_tok[:, None]).astype(bfloat).reshape(inputs.shape)
    incoming = cotangent.reshape(tokens, features).astype(single) * weight.reshape(tokens)[:, None]
    grad_branch_two = incoming.astype(bfloat)
    grad_down_weight = jnp.einsum(
        "tf,td->fd", active_low, grad_branch_two, preferred_element_type=single
    )
    grad_down_bias = jnp.sum(grad_branch_two.astype(single), axis=0)
    grad_active = jnp.einsum(
        "td,fd->tf", grad_branch_two, down_weight, preferred_element_type=single
    )
    grad_hidden = gelu_pull(grad_active)[0].astype(bfloat)
    grad_up_weight = jnp.einsum(
        "tm,tf->mf", normed_two_low, grad_hidden, preferred_element_type=single
    )
    grad_up_bias = jnp.sum(grad_hidden.astype(single), axis=0)
    grad_normed_two = jnp.einsum("tf,mf->tm", grad_hidden, up_weight, preferred_element_type=single)
    grad_mid_norm, grad_norm2_gain, grad_norm2_bias = norm2_pull(grad_normed_two)
    grad_middle = incoming + grad_mid_norm
    grad_branch = grad_middle.astype(bfloat)
    grad_out_weight = jnp.einsum(
        "tm,td->md", attended_low, grad_branch, preferred_element_type=single
    )
    grad_out_bias = jnp.sum(grad_branch.astype(single), axis=0)
    grad_attended = jnp.einsum("td,md->tm", grad_branch, out_weight, preferred_element_type=single)
    grad_heads = grad_attended.astype(bfloat).reshape(slots, piece_len, H, HD)
    query_grads = []
    key_grads = []
    value_grads = []
    for group in range(H // group_heads):
        first = group * group_heads
        last = first + group_heads
        highest, totals = kept_stats[group]
        grad_query, grad_keys, grad_values = attend_backward(
            query[:, :, first:last],
            keys_heads[:, :, first:last],
            values_heads[:, :, first:last],
            grad_heads[:, :, first:last],
            highest,
            totals,
            allowed,
        )
        query_grads.append(grad_query)
        key_grads.append(grad_keys)
        value_grads.append(grad_values)
    grad_query_all = jnp.concatenate(query_grads, axis=2).reshape(tokens, features)
    grad_keys_all = jnp.concatenate(key_grads, axis=2).reshape(slots, row_len, features)
    grad_values_all = jnp.concatenate(value_grads, axis=2).reshape(slots, row_len, features)
    grad_keys_own, grad_values_own = (
        lax.psum_scatter(
            grad_keys_all.astype(jnp.bfloat16), "seq", scatter_dimension=1, tiled=True
        ).astype(jnp.float32),
        lax.psum_scatter(
            grad_values_all.astype(jnp.bfloat16), "seq", scatter_dimension=1, tiled=True
        ).astype(jnp.float32),
    )
    grad_projected = jnp.concatenate(
        [
            grad_query_all,
            grad_keys_own.reshape(tokens, features),
            grad_values_own.reshape(tokens, features),
        ],
        axis=1,
    ).astype(bfloat)
    grad_qkv_weight = jnp.einsum(
        "tm,tn->mn", normed_low, grad_projected, preferred_element_type=single
    )
    column_sums = jnp.sum(grad_projected.astype(single), axis=0)
    grad_qv_bias = jnp.stack([column_sums[:features], column_sums[2 * features :]])
    grad_normed = jnp.einsum("tn,mn->tm", grad_projected, qkv_weight, preferred_element_type=single)
    grad_src_norm, grad_norm1_gain, grad_norm1_bias = norm1_pull(grad_normed)
    input_grad = (grad_middle + grad_src_norm).astype(bfloat).reshape(inputs.shape)
    grads = (
        grad_norm1_gain,
        grad_norm1_bias,
        grad_qkv_weight,
        grad_qv_bias,
        grad_out_weight,
        grad_out_bias,
        grad_norm2_gain,
        grad_norm2_bias,
        grad_up_weight,
        grad_up_bias,
        grad_down_weight,
        grad_down_bias,
    )
    summed = (
        lax.psum_scatter(
            grads[0].astype(jnp.bfloat16), "dp", scatter_dimension=0, tiled=True
        ).astype(jnp.float32),
        lax.psum_scatter(
            grads[1].astype(jnp.bfloat16), "dp", scatter_dimension=0, tiled=True
        ).astype(jnp.float32),
        lax.psum_scatter(
            grads[2].astype(jnp.bfloat16), "dp", scatter_dimension=0, tiled=True
        ).astype(jnp.float32),
        lax.psum_scatter(
            grads[3].astype(jnp.bfloat16), "dp", scatter_dimension=1, tiled=True
        ).astype(jnp.float32),
        lax.psum_scatter(
            grads[4].astype(jnp.bfloat16), "dp", scatter_dimension=0, tiled=True
        ).astype(jnp.float32),
        lax.psum_scatter(
            grads[5].astype(jnp.bfloat16), "dp", scatter_dimension=0, tiled=True
        ).astype(jnp.float32),
        lax.psum_scatter(
            grads[6].astype(jnp.bfloat16), "dp", scatter_dimension=0, tiled=True
        ).astype(jnp.float32),
        lax.psum_scatter(
            grads[7].astype(jnp.bfloat16), "dp", scatter_dimension=0, tiled=True
        ).astype(jnp.float32),
        lax.psum_scatter(
            grads[8].astype(jnp.bfloat16), "dp", scatter_dimension=0, tiled=True
        ).astype(jnp.float32),
        lax.psum_scatter(
            grads[9].astype(jnp.bfloat16), "dp", scatter_dimension=0, tiled=True
        ).astype(jnp.float32),
        lax.psum_scatter(
            grads[10].astype(jnp.bfloat16), "dp", scatter_dimension=0, tiled=True
        ).astype(jnp.float32),
        lax.psum_scatter(
            grads[11].astype(jnp.bfloat16), "dp", scatter_dimension=0, tiled=True
        ).astype(jnp.float32),
    )
    summed = (
        lax.psum(summed[0].astype(jnp.bfloat16), ("src", "seq")).astype(jnp.float32),
        lax.psum(summed[1].astype(jnp.bfloat16), ("src", "seq")).astype(jnp.float32),
        lax.psum(summed[2].astype(jnp.bfloat16), ("src", "seq")).astype(jnp.float32),
        lax.psum(summed[3].astype(jnp.bfloat16), ("src", "seq")).astype(jnp.float32),
        lax.psum(summed[4].astype(jnp.bfloat16), ("src", "seq")).astype(jnp.float32),
        lax.psum(summed[5].astype(jnp.bfloat16), ("src", "seq")).astype(jnp.float32),
        lax.psum(summed[6].astype(jnp.bfloat16), ("src", "seq")).astype(jnp.float32),
        lax.psum(summed[7].astype(jnp.bfloat16), ("src", "seq")).astype(jnp.float32),
        lax.psum(summed[8].astype(jnp.bfloat16), ("src", "seq")).astype(jnp.float32),
        lax.psum(summed[9].astype(jnp.bfloat16), ("src", "seq")).astype(jnp.float32),
        lax.psum(summed[10].astype(jnp.bfloat16), ("src", "seq")).astype(jnp.float32),
        lax.psum(summed[11].astype(jnp.bfloat16), ("src", "seq")).astype(jnp.float32),
    )
    final = [g / whole for g in summed]
    return (
        output,
        input_grad,
        source_counts,
        final[0],
        final[1],
        final[2],
        final[3],
        final[4],
        final[5],
        final[6],
        final[7],
        final[8],
        final[9],
        final[10],
        final[11],
    )


def swap_pairs(size, bit):
    return [(i, i ^ bit) for i in range(size)]


def relative(chunks, own):
    count = chunks.shape[0]
    return chunks[jnp.arange(count) ^ own]


def scatter_sum(chunks, order):
    count = chunks.shape[0]
    depth = count.bit_length() - 1
    left = list(range(depth - 1, -1, -1))
    held = chunks.reshape((2,) * depth + chunks.shape[1:])
    for stage in order:
        if stage == "seq":
            other = lax.ppermute(held, "seq", swap_pairs(2, 1))
            total = held.astype(jnp.float32) + other.astype(jnp.float32)
        else:
            at = left.index(stage)
            left.pop(at)
            keep = lax.index_in_dim(held, 0, at, keepdims=False)
            send = lax.index_in_dim(held, 1, at, keepdims=False)
            other = lax.ppermute(send, "dp", swap_pairs(count, 1 << stage))
            total = keep.astype(jnp.float32) + other.astype(jnp.float32)
        held = total.astype(jnp.bfloat16)
    return total


def body_fast(
    inputs,
    cotangent,
    row_counts,
    response_mask,
    norm1_gain,
    norm1_bias,
    qkv_weight,
    qv_bias,
    out_weight,
    out_bias,
    norm2_gain,
    norm2_bias,
    up_weight,
    up_bias,
    down_weight,
    down_bias,
):
    slots = inputs.shape[2]
    piece_len = inputs.shape[3]
    features = inputs.shape[4]
    length = 2 * piece_len
    groups = lax.axis_size("dp")
    bfloat = jnp.bfloat16
    single = jnp.float32
    core = lax.axis_index("src")
    own = lax.axis_index("dp")
    place = lax.axis_index("seq")
    pair = swap_pairs(2, 1)

    present = jnp.arange(slots) < row_counts[0, 0]
    mask = response_mask[0, 0] * present.astype(jnp.int32)[:, None]
    cot = cotangent[0, 0] * mask.astype(bfloat)[..., None]
    local_count = jnp.sum(mask)
    row_present = (place < row_counts[0, 0]).astype(single)

    def row_of(both):
        mine = lax.dynamic_index_in_dim(both, place, 0, keepdims=False)
        theirs = lax.dynamic_index_in_dim(both, 1 - place, 0, keepdims=False)
        other = lax.ppermute(theirs, "seq", pair)
        return jnp.where(
            place == 0, jnp.concatenate([mine, other]), jnp.concatenate([other, mine])
        )

    def row_back(row):
        mine = lax.dynamic_slice_in_dim(row, place * piece_len, piece_len, 0)
        theirs = lax.dynamic_slice_in_dim(row, (1 - place) * piece_len, piece_len, 0)
        other = lax.ppermute(theirs, "seq", pair)
        return jnp.where(place == 0, jnp.stack([mine, other]), jnp.stack([other, mine]))[None, None]

    source = row_of(inputs[0, 0]).astype(single)
    grad_low = row_of(cot)
    incoming = grad_low.astype(single)

    normed, norm1_pull = jax.vjp(
        norm_apply, source, norm1_gain.astype(single), norm1_bias.astype(single)
    )
    normed_low = normed.astype(bfloat)
    bias_query = qv_bias[0].astype(single)
    joined = jnp.concatenate([bias_query, jnp.zeros_like(bias_query), qv_bias[1].astype(single)])
    projected = jnp.dot(normed_low, qkv_weight, preferred_element_type=single) + joined
    proj_low = projected.astype(bfloat).reshape(1, length, 3, H, HD)
    query, keys, values = proj_low[:, :, 0], proj_low[:, :, 1], proj_low[:, :, 2]
    allowed = jnp.arange(length)[:, None] >= jnp.arange(length)[None, :]
    attended, highest, totals = attend_forward(query, keys, values, allowed)
    attended_low = attended.astype(bfloat).reshape(length, features)
    branch = jnp.dot(attended_low, out_weight, preferred_element_type=single) + out_bias.astype(
        single
    )
    middle = source + branch
    normed_two, norm2_pull = jax.vjp(
        norm_apply, middle, norm2_gain.astype(single), norm2_bias.astype(single)
    )
    normed_two_low = normed_two.astype(bfloat)
    hidden = jnp.dot(normed_two_low, up_weight, preferred_element_type=single) + up_bias.astype(
        single
    )
    active, gelu_pull = jax.vjp(functools.partial(jax.nn.gelu, approximate=True), hidden)
    active_low = active.astype(bfloat)
    branch_two = jnp.dot(active_low, down_weight, preferred_element_type=single) + down_bias.astype(
        single
    )
    result = middle + branch_two
    output = row_back((result * row_present).astype(bfloat))

    grad_active = jnp.einsum("td,fd->tf", grad_low, down_weight, preferred_element_type=single)
    grad_hidden = gelu_pull(grad_active)[0].astype(bfloat)
    grad_normed_two = jnp.einsum("tf,mf->tm", grad_hidden, up_weight, preferred_element_type=single)
    grad_mid_norm, grad_norm2_gain, grad_norm2_bias = norm2_pull(grad_normed_two)
    grad_middle = incoming + grad_mid_norm
    grad_branch = grad_middle.astype(bfloat)
    grad_attended = jnp.einsum("td,md->tm", grad_branch, out_weight, preferred_element_type=single)
    grad_heads = grad_attended.astype(bfloat).reshape(1, length, H, HD)
    grad_query, grad_keys, grad_values = attend_backward(
        query, keys, values, grad_heads, highest, totals, allowed
    )
    grad_projected = jnp.concatenate(
        [g.reshape(length, features) for g in (grad_query, grad_keys, grad_values)], axis=1
    ).astype(bfloat)
    grad_normed = jnp.einsum("tn,mn->tm", grad_projected, qkv_weight, preferred_element_type=single)
    grad_src_norm, grad_norm1_gain, grad_norm1_bias = norm1_pull(grad_normed)
    input_grad = row_back((grad_middle + grad_src_norm).astype(bfloat))

    def weight_grad(left, right):
        width = right.shape[1] // 2
        mine = lax.dynamic_slice_in_dim(right, core * width, width, 1)
        theirs = lax.dynamic_slice_in_dim(right, (1 - core) * width, width, 1)
        left_other = lax.ppermute(left, "src", pair)
        right_other = lax.ppermute(theirs, "src", pair)
        left_all = jnp.concatenate([left, left_other])
        right_all = jnp.concatenate([mine, right_other])
        total = jnp.einsum("tm,tn->mn", left_all, right_all, preferred_element_type=single)
        chunks = total.astype(bfloat).reshape(groups, left.shape[1] // groups, width)
        return relative(chunks, own)

    def column_sum(entries):
        return jnp.sum(entries.astype(single), axis=0)

    columns = column_sum(grad_projected)
    chunked = [
        v.reshape(groups, -1)
        for v in (
            grad_norm1_gain,
            grad_norm1_bias,
            columns[:features],
            columns[2 * features :],
            column_sum(grad_branch),
            grad_norm2_gain,
            grad_norm2_bias,
            column_sum(grad_low),
            column_sum(grad_hidden),
        )
    ]
    n_digits = (slots * piece_len).bit_length()
    digits = (local_count >> jnp.arange(n_digits)) & 1
    both_digits = jnp.where(jnp.arange(2)[:, None] == core, digits[None, :], 0).astype(single)
    chunked.append(jnp.broadcast_to(both_digits.reshape(1, -1), (groups, 2 * n_digits)))
    sizes = [v.shape[1] for v in chunked]
    vector = jnp.concatenate(chunked, axis=1)
    fill = -vector.shape[1] % 256
    vector = jnp.pad(vector, ((0, 0), (0, fill))).reshape(groups, 2, -1)
    vector = vector + lax.ppermute(vector, "src", pair)
    vector_sum = scatter_sum(relative(vector.astype(bfloat), own), (0, 1, 2, "seq")).reshape(-1)
    parts = []
    at = 0
    for size in sizes:
        parts.append(vector_sum[at : at + size])
        at += size
    counted = parts[-1].astype(jnp.int32).reshape(2, n_digits)
    source_counts = jnp.sum(counted << jnp.arange(n_digits)[None, :], axis=1)
    whole = jnp.sum(source_counts).astype(single)

    def finish(total):
        low = total.astype(bfloat)
        other = lax.ppermute(low, "src", pair)
        return jnp.where(
            core == 0, jnp.concatenate([low, other], 1), jnp.concatenate([other, low], 1)
        ).astype(single) / whole

    grad_down_weight = finish(scatter_sum(weight_grad(active_low, grad_low), (0, 1, 2, "seq")))
    grad_up_weight = finish(scatter_sum(weight_grad(normed_two_low, grad_hidden), (1, 2, 0, "seq")))
    grad_out_weight = finish(scatter_sum(weight_grad(attended_low, grad_branch), (0, 1, 2, "seq")))
    grad_qkv_weight = finish(
        scatter_sum(weight_grad(normed_low, grad_projected), ("seq", 0, 1, 2))
    )
    scaled = [p / whole for p in parts[:-1]]
    return (
        output,
        input_grad,
        source_counts,
        scaled[0],
        scaled[1],
        grad_qkv_weight,
        jnp.stack([scaled[2], scaled[3]]),
        grad_out_weight,
        scaled[4],
        scaled[5],
        scaled[6],
        grad_up_weight,
        scaled[8],
        grad_down_weight,
        scaled[7],
    )


def solution(mesh):
    placed = (
        P("src", "dp", None, "seq", None),
        P("src", "dp", None, "seq", None),
        P("src", "dp"),
        P("src", "dp", None, "seq"),
        P(),
        P(),
        P(),
        P(),
        P(),
        P(),
        P(),
        P(),
        P(),
        P(),
        P(),
        P(),
    )
    sizes = dict(mesh.shape)
    paired = sizes["src"] == 2 and sizes["seq"] == 2 and sizes["dp"] == 8
    return jax.shard_map(
        body_fast if paired else body_generic,
        mesh=mesh,
        in_specs=placed,
        out_specs=(
            P("src", "dp", None, "seq", None),
            P("src", "dp", None, "seq", None),
            P(),
            P("dp"),
            P("dp"),
            P("dp", None),
            P(None, "dp"),
            P("dp", None),
            P("dp"),
            P("dp"),
            P("dp"),
            P("dp", None),
            P("dp"),
            P("dp", None),
            P("dp"),
        ),
        check_vma=False,
    )
```

```python
import functools
import math

import jax
import jax.numpy as jnp
from jax import lax
from jax.experimental import pallas as pl
from jax.experimental.pallas import tpu as pltpu
from jax.sharding import PartitionSpec as P

H = 12
HD = 64


EPS = 1e-05
NEGATIVE = -1e30


def norm_apply(values, scaling, offset):
    centre = jnp.mean(values, axis=-1, keepdims=True)
    centered = values - centre
    spread = jnp.mean(centered * centered, axis=-1, keepdims=True)
    return centered * lax.rsqrt(spread + EPS) * scaling + offset


def causal_scores(query_part, keys_part, allowed):
    scores = jnp.einsum(
        "rqhd,rkhd->rhqk", query_part, keys_part, preferred_element_type=jnp.float32
    )
    scores = scores * HD ** (-0.5)
    return jnp.where(allowed, scores, NEGATIVE)


def attend_forward(query_part, keys_part, values_part, allowed):
    scores = causal_scores(query_part, keys_part, allowed)
    highest = jnp.max(scores, axis=-1, keepdims=True)
    powers = jnp.exp(scores - highest)
    totals = jnp.sum(powers, axis=-1, keepdims=True)
    probs_low = (powers / totals).astype(jnp.bfloat16)
    mixed = jnp.einsum(
        "rhqk,rkhd->rqhd", probs_low, values_part, preferred_element_type=jnp.float32
    )
    return (mixed, highest, totals)


def attend_backward(query_part, keys_part, values_part, grad_part, highest, totals, allowed):
    scores = causal_scores(query_part, keys_part, allowed)
    probs = jnp.exp(scores - highest) / totals
    probs_low = probs.astype(jnp.bfloat16)
    grad_probs = jnp.einsum(
        "rqhd,rkhd->rhqk", grad_part, values_part, preferred_element_type=jnp.float32
    )
    inner = jnp.sum(probs * grad_probs, axis=-1, keepdims=True)
    grad_scores = (probs * (grad_probs - inner)).astype(jnp.bfloat16)
    factor = HD ** (-0.5)
    grad_query = (
        jnp.einsum("rhqk,rkhd->rqhd", grad_scores, keys_part, preferred_element_type=jnp.float32)
        * factor
    )
    grad_keys = (
        jnp.einsum("rhqk,rqhd->rkhd", grad_scores, query_part, preferred_element_type=jnp.float32)
        * factor
    )
    grad_values = jnp.einsum(
        "rhqk,rqhd->rkhd", probs_low, grad_part, preferred_element_type=jnp.float32
    )
    return (grad_query, grad_keys, grad_values)


def body_generic(
    inputs,
    cotangent,
    row_counts,
    response_mask,
    norm1_gain,
    norm1_bias,
    qkv_weight,
    qv_bias,
    out_weight,
    out_bias,
    norm2_gain,
    norm2_bias,
    up_weight,
    up_bias,
    down_weight,
    down_bias,
):
    slots = inputs.shape[2]
    piece_len = inputs.shape[3]
    features = inputs.shape[4]
    tokens = slots * piece_len
    blocks_seq = lax.axis_size("seq")
    row_len = piece_len * blocks_seq
    group_heads = math.gcd(H, 4)
    bfloat = jnp.bfloat16
    single = jnp.float32
    present_int = (jnp.arange(slots) < row_counts[0, 0]).astype(jnp.int32)
    weight = (response_mask[0, 0] * present_int[:, None]).astype(single)
    local_count = jnp.sum(response_mask[0, 0] * present_int[:, None])
    picked = jnp.where(jnp.arange(lax.axis_size("src")) == lax.axis_index("src"), local_count, 0)
    source_counts = lax.psum(picked, ("src", "dp", "seq"))
    whole = jnp.sum(source_counts).astype(single)
    source = inputs.reshape(tokens, features).astype(single)
    normed, norm1_pull = jax.vjp(
        norm_apply, source, norm1_gain.astype(single), norm1_bias.astype(single)
    )
    normed_low = normed.astype(bfloat)
    bias_query = qv_bias[0].astype(single)
    joined = jnp.concatenate([bias_query, jnp.zeros_like(bias_query), qv_bias[1].astype(single)])
    projected = jnp.dot(normed_low, qkv_weight, preferred_element_type=single) + joined
    proj_low = projected.astype(bfloat)
    query = proj_low[:, :features].reshape(slots, piece_len, H, HD)
    keys_own = proj_low[:, features : 2 * features].reshape(slots, piece_len, features)
    values_own = proj_low[:, 2 * features :].reshape(slots, piece_len, features)
    keys_all, values_all = (
        lax.all_gather(keys_own, "seq", axis=1, tiled=True),
        lax.all_gather(values_own, "seq", axis=1, tiled=True),
    )
    query_pos = lax.axis_index("seq") * piece_len + jnp.arange(piece_len)
    allowed = query_pos[:, None] >= jnp.arange(row_len)[None, :]
    keys_heads = keys_all.reshape(slots, row_len, H, HD)
    values_heads = values_all.reshape(slots, row_len, H, HD)
    mixed_parts = []
    kept_stats = []
    for group in range(H // group_heads):
        first = group * group_heads
        last = first + group_heads
        mixed, highest, totals = attend_forward(
            query[:, :, first:last],
            keys_heads[:, :, first:last],
            values_heads[:, :, first:last],
            allowed,
        )
        mixed_parts.append(mixed)
        kept_stats.append((highest, totals))
    attended = jnp.concatenate(mixed_parts, axis=2).reshape(tokens, features)
    attended_low = attended.astype(bfloat)
    branch = jnp.dot(attended_low, out_weight, preferred_element_type=single) + out_bias.astype(
        single
    )
    middle = source + branch
    normed_two, norm2_pull = jax.vjp(
        norm_apply, middle, norm2_gain.astype(single), norm2_bias.astype(single)
    )
    normed_two_low = normed_two.astype(bfloat)
    hidden = jnp.dot(normed_two_low, up_weight, preferred_element_type=single) + up_bias.astype(
        single
    )
    active, gelu_pull = jax.vjp(functools.partial(jax.nn.gelu, approximate=True), hidden)
    active_low = active.astype(bfloat)
    branch_two = jnp.dot(active_low, down_weight, preferred_element_type=single) + down_bias.astype(
        single
    )
    result = middle + branch_two
    present_tok = jnp.repeat(present_int.astype(single), piece_len)
    output = (result * present_tok[:, None]).astype(bfloat).reshape(inputs.shape)
    incoming = cotangent.reshape(tokens, features).astype(single) * weight.reshape(tokens)[:, None]
    grad_branch_two = incoming.astype(bfloat)
    grad_down_weight = jnp.einsum(
        "tf,td->fd", active_low, grad_branch_two, preferred_element_type=single
    )
    grad_down_bias = jnp.sum(grad_branch_two.astype(single), axis=0)
    grad_active = jnp.einsum(
        "td,fd->tf", grad_branch_two, down_weight, preferred_element_type=single
    )
    grad_hidden = gelu_pull(grad_active)[0].astype(bfloat)
    grad_up_weight = jnp.einsum(
        "tm,tf->mf", normed_two_low, grad_hidden, preferred_element_type=single
    )
    grad_up_bias = jnp.sum(grad_hidden.astype(single), axis=0)
    grad_normed_two = jnp.einsum("tf,mf->tm", grad_hidden, up_weight, preferred_element_type=single)
    grad_mid_norm, grad_norm2_gain, grad_norm2_bias = norm2_pull(grad_normed_two)
    grad_middle = incoming + grad_mid_norm
    grad_branch = grad_middle.astype(bfloat)
    grad_out_weight = jnp.einsum(
        "tm,td->md", attended_low, grad_branch, preferred_element_type=single
    )
    grad_out_bias = jnp.sum(grad_branch.astype(single), axis=0)
    grad_attended = jnp.einsum("td,md->tm", grad_branch, out_weight, preferred_element_type=single)
    grad_heads = grad_attended.astype(bfloat).reshape(slots, piece_len, H, HD)
    query_grads = []
    key_grads = []
    value_grads = []
    for group in range(H // group_heads):
        first = group * group_heads
        last = first + group_heads
        highest, totals = kept_stats[group]
        grad_query, grad_keys, grad_values = attend_backward(
            query[:, :, first:last],
            keys_heads[:, :, first:last],
            values_heads[:, :, first:last],
            grad_heads[:, :, first:last],
            highest,
            totals,
            allowed,
        )
        query_grads.append(grad_query)
        key_grads.append(grad_keys)
        value_grads.append(grad_values)
    grad_query_all = jnp.concatenate(query_grads, axis=2).reshape(tokens, features)
    grad_keys_all = jnp.concatenate(key_grads, axis=2).reshape(slots, row_len, features)
    grad_values_all = jnp.concatenate(value_grads, axis=2).reshape(slots, row_len, features)
    grad_keys_own, grad_values_own = (
        lax.psum_scatter(
            grad_keys_all.astype(jnp.bfloat16), "seq", scatter_dimension=1, tiled=True
        ).astype(jnp.float32),
        lax.psum_scatter(
            grad_values_all.astype(jnp.bfloat16), "seq", scatter_dimension=1, tiled=True
        ).astype(jnp.float32),
    )
    grad_projected = jnp.concatenate(
        [
            grad_query_all,
            grad_keys_own.reshape(tokens, features),
            grad_values_own.reshape(tokens, features),
        ],
        axis=1,
    ).astype(bfloat)
    grad_qkv_weight = jnp.einsum(
        "tm,tn->mn", normed_low, grad_projected, preferred_element_type=single
    )
    column_sums = jnp.sum(grad_projected.astype(single), axis=0)
    grad_qv_bias = jnp.stack([column_sums[:features], column_sums[2 * features :]])
    grad_normed = jnp.einsum("tn,mn->tm", grad_projected, qkv_weight, preferred_element_type=single)
    grad_src_norm, grad_norm1_gain, grad_norm1_bias = norm1_pull(grad_normed)
    input_grad = (grad_middle + grad_src_norm).astype(bfloat).reshape(inputs.shape)
    grads = (
        grad_norm1_gain,
        grad_norm1_bias,
        grad_qkv_weight,
        grad_qv_bias,
        grad_out_weight,
        grad_out_bias,
        grad_norm2_gain,
        grad_norm2_bias,
        grad_up_weight,
        grad_up_bias,
        grad_down_weight,
        grad_down_bias,
    )
    summed = (
        lax.psum_scatter(
            grads[0].astype(jnp.bfloat16), "dp", scatter_dimension=0, tiled=True
        ).astype(jnp.float32),
        lax.psum_scatter(
            grads[1].astype(jnp.bfloat16), "dp", scatter_dimension=0, tiled=True
        ).astype(jnp.float32),
        lax.psum_scatter(
            grads[2].astype(jnp.bfloat16), "dp", scatter_dimension=0, tiled=True
        ).astype(jnp.float32),
        lax.psum_scatter(
            grads[3].astype(jnp.bfloat16), "dp", scatter_dimension=1, tiled=True
        ).astype(jnp.float32),
        lax.psum_scatter(
            grads[4].astype(jnp.bfloat16), "dp", scatter_dimension=0, tiled=True
        ).astype(jnp.float32),
        lax.psum_scatter(
            grads[5].astype(jnp.bfloat16), "dp", scatter_dimension=0, tiled=True
        ).astype(jnp.float32),
        lax.psum_scatter(
            grads[6].astype(jnp.bfloat16), "dp", scatter_dimension=0, tiled=True
        ).astype(jnp.float32),
        lax.psum_scatter(
            grads[7].astype(jnp.bfloat16), "dp", scatter_dimension=0, tiled=True
        ).astype(jnp.float32),
        lax.psum_scatter(
            grads[8].astype(jnp.bfloat16), "dp", scatter_dimension=0, tiled=True
        ).astype(jnp.float32),
        lax.psum_scatter(
            grads[9].astype(jnp.bfloat16), "dp", scatter_dimension=0, tiled=True
        ).astype(jnp.float32),
        lax.psum_scatter(
            grads[10].astype(jnp.bfloat16), "dp", scatter_dimension=0, tiled=True
        ).astype(jnp.float32),
        lax.psum_scatter(
            grads[11].astype(jnp.bfloat16), "dp", scatter_dimension=0, tiled=True
        ).astype(jnp.float32),
    )
    summed = (
        lax.psum(summed[0].astype(jnp.bfloat16), ("src", "seq")).astype(jnp.float32),
        lax.psum(summed[1].astype(jnp.bfloat16), ("src", "seq")).astype(jnp.float32),
        lax.psum(summed[2].astype(jnp.bfloat16), ("src", "seq")).astype(jnp.float32),
        lax.psum(summed[3].astype(jnp.bfloat16), ("src", "seq")).astype(jnp.float32),
        lax.psum(summed[4].astype(jnp.bfloat16), ("src", "seq")).astype(jnp.float32),
        lax.psum(summed[5].astype(jnp.bfloat16), ("src", "seq")).astype(jnp.float32),
        lax.psum(summed[6].astype(jnp.bfloat16), ("src", "seq")).astype(jnp.float32),
        lax.psum(summed[7].astype(jnp.bfloat16), ("src", "seq")).astype(jnp.float32),
        lax.psum(summed[8].astype(jnp.bfloat16), ("src", "seq")).astype(jnp.float32),
        lax.psum(summed[9].astype(jnp.bfloat16), ("src", "seq")).astype(jnp.float32),
        lax.psum(summed[10].astype(jnp.bfloat16), ("src", "seq")).astype(jnp.float32),
        lax.psum(summed[11].astype(jnp.bfloat16), ("src", "seq")).astype(jnp.float32),
    )
    final = [g / whole for g in summed]
    return (
        output,
        input_grad,
        source_counts,
        final[0],
        final[1],
        final[2],
        final[3],
        final[4],
        final[5],
        final[6],
        final[7],
        final[8],
        final[9],
        final[10],
        final[11],
    )


SINGLE = jnp.float32
LOW = jnp.bfloat16
GROUP = 4
GW = GROUP * HD
DIGITS = 16


def behind(kernel, skipped):
    def ordered(at_ref, *refs):
        kernel(at_ref, *refs[skipped:])

    return ordered


def tokens(after):
    return [pl.BlockSpec(memory_space=pl.ANY)] * len(after)


def dot_nt(left, right):
    return lax.dot_general(left, right, (((1,), (1,)), ((), ())), preferred_element_type=SINGLE)


def dot_tn(left, right):
    return lax.dot_general(left, right, (((0,), (0,)), ((), ())), preferred_element_type=SINGLE)


def dot_nn(left, right):
    return jnp.dot(left, right, preferred_element_type=SINGLE)


def normalize(values):
    centered = values - jnp.mean(values, axis=-1, keepdims=True)
    inverse = lax.rsqrt(jnp.mean(centered * centered, axis=-1, keepdims=True) + EPS)
    return centered * inverse, inverse


def norm_back(normal, inverse, grad, gain):
    scaled = grad * gain
    return inverse * (
        scaled
        - jnp.mean(scaled, axis=-1, keepdims=True)
        - normal * jnp.mean(scaled * normal, axis=-1, keepdims=True)
    )


def head_mask(head):
    lanes = lax.broadcasted_iota(jnp.int32, (1, GW), 1)
    return (lanes >= head * HD) & (lanes < (head + 1) * HD)


def join_row(place, mine_ref, other_ref, row_ref):
    piece = mine_ref.shape[0]
    row_ref[pl.ds(pl.multiple_of(place * piece, piece), piece), :] = mine_ref[...].astype(
        row_ref.dtype
    )
    row_ref[pl.ds(pl.multiple_of((1 - place) * piece, piece), piece), :] = other_ref[
        ...
    ].astype(row_ref.dtype)


def prepare_kernel(at_ref, rows_ref, cot_ref, mask_ref, c_send, c_mine, count_ref):
    core, place = at_ref[0], at_ref[2]
    piece = mask_ref.shape[1]
    diagonal = lax.broadcasted_iota(jnp.int32, (piece, piece), 0) == lax.broadcasted_iota(
        jnp.int32, (piece, piece), 1
    )

    def column(row):
        kept = mask_ref[pl.ds(row, 1), :].astype(SINGLE) * (row < rows_ref[0, 0]).astype(SINGLE)
        return jnp.sum(jnp.where(diagonal, kept, 0.0), axis=1, keepdims=True), kept

    weight_mine, kept_mine = column(place)
    weight_send, kept_send = column(1 - place)
    c_send[...] = (cot_ref[1 - place].astype(SINGLE) * weight_send).astype(LOW)
    c_mine[...] = (cot_ref[place].astype(SINGLE) * weight_mine).astype(LOW)
    count = jnp.sum(kept_mine + kept_send, axis=1, keepdims=True).astype(jnp.int32)
    lane = lax.broadcasted_iota(jnp.int32, count_ref.shape, 1) - core * DIGITS
    digit = lax.shift_right_logical(
        jnp.broadcast_to(count, count_ref.shape), jnp.clip(lane, 0, DIGITS - 1)
    )
    count_ref[...] = jnp.where((lane >= 0) & (lane < DIGITS), digit & 1, 0).astype(SINGLE)


def prepare(at, rows, cot, mask):
    piece, features = cot.shape[1:]
    part = jax.ShapeDtypeStruct((piece, features), LOW)
    smem = pl.BlockSpec(memory_space=pltpu.SMEM)
    vmem = pl.BlockSpec(memory_space=pltpu.VMEM)
    return pl.pallas_call(
        prepare_kernel,
        in_specs=[smem, smem, vmem, vmem],
        out_specs=[vmem] * 3,
        out_shape=[part, part, jax.ShapeDtypeStruct((1, 128), SINGLE)],
        cost_estimate=pl.CostEstimate(flops=1, bytes_accessed=1, transcendentals=0),
    )(at, rows, cot, mask)


def attend_kernel(
    at_ref, x_mine, x_other, gain1, bias1, wq, wk, wv, bq, bv, wo, bo, gain2, bias2,
    n1_out, q_out, k_out, v_out, probs_out, a_out, m_out, n2_out, row,
):
    group = pl.program_id(0)
    length = row.shape[0]

    @pl.when(group == 0)
    def _():
        join_row(at_ref[2], x_mine, x_other, row)
        normal, _ = normalize(row[...])
        n1_out[...] = (normal * gain1[...].astype(SINGLE) + bias1[...].astype(SINGLE)).astype(LOW)

    n1 = n1_out[...]
    query = (dot_nn(n1, wq[...]) + bq[...].astype(SINGLE)).astype(LOW)
    keys = dot_nn(n1, wk[...]).astype(LOW)
    values = (dot_nn(n1, wv[...]) + bv[...].astype(SINGLE)).astype(LOW)
    q_out[...] = query
    k_out[...] = keys
    v_out[...] = values
    allowed = lax.broadcasted_iota(jnp.int32, (length, length), 0) >= lax.broadcasted_iota(
        jnp.int32, (length, length), 1
    )
    scaled = query * HD**-0.5
    mixed = None
    for head in range(GROUP):
        mask = head_mask(head)
        scores = dot_nt(jnp.where(mask, scaled, 0), keys)
        scores = jnp.where(allowed, scores, NEGATIVE)
        powers = jnp.exp(scores - jnp.max(scores, axis=-1, keepdims=True))
        probs = (powers * (1.0 / jnp.sum(powers, axis=-1, keepdims=True))).astype(LOW)
        probs_out[head] = probs
        part = dot_nn(probs, values)
        mixed = part if head == 0 else jnp.where(mask, part, mixed)
    at = pl.ds(pl.multiple_of(group * GW, GW), GW)
    a_out[:, at] = mixed.astype(LOW)

    @pl.when(group == pl.num_programs(0) - 1)
    def _():
        middle = row[...] + dot_nn(a_out[...], wo[...]) + bo[...].astype(SINGLE)
        m_out[...] = middle
        normal, _ = normalize(middle)
        n2_out[...] = (normal * gain2[...].astype(SINGLE) + bias2[...].astype(SINGLE)).astype(LOW)


def attend(at, inputs, x_other, gain1, bias1, qkv_weight, qv_bias, out_weight, out_bias, gain2, bias2):
    piece, features = x_other.shape
    length = 2 * piece
    groups = features // GW
    vec = pl.BlockSpec((1, features), lambda g, at: (0, 0))

    def whole(*shape):
        return pl.BlockSpec(shape, lambda g, at: (0,) * len(shape))

    def columns(first):
        return pl.BlockSpec((features, GW), lambda g, at: (0, first * groups + g))

    act = pl.BlockSpec((length, GW), lambda g, at: (0, g))
    return pl.pallas_call(
        attend_kernel,
        grid_spec=pltpu.PrefetchScalarGridSpec(
            num_scalar_prefetch=1,
            grid=(groups,),
            in_specs=[
                pl.BlockSpec((None, piece, features), lambda g, at: (at[2], 0, 0)),
                whole(piece, features), vec, vec,
                columns(0), columns(1), columns(2),
                pl.BlockSpec((None, 1, GW), lambda g, at: (0, 0, g)),
                pl.BlockSpec((None, 1, GW), lambda g, at: (1, 0, g)),
                whole(features, features), vec, vec, vec,
            ],
            out_specs=[
                whole(length, features), act, act, act,
                pl.BlockSpec((GROUP, length, length), lambda g, at: (g, 0, 0)),
                whole(length, features), whole(length, features), whole(length, features),
            ],
            scratch_shapes=[pltpu.VMEM((length, features), SINGLE)],
        ),
        out_shape=[
            jax.ShapeDtypeStruct((length, features), LOW),
            jax.ShapeDtypeStruct((length, features), LOW),
            jax.ShapeDtypeStruct((length, features), LOW),
            jax.ShapeDtypeStruct((length, features), LOW),
            jax.ShapeDtypeStruct((groups * GROUP, length, length), LOW),
            jax.ShapeDtypeStruct((length, features), LOW),
            jax.ShapeDtypeStruct((length, features), SINGLE),
            jax.ShapeDtypeStruct((length, features), LOW),
        ],
        compiler_params=pltpu.CompilerParams(vmem_limit_bytes=40 << 20),
        cost_estimate=pl.CostEstimate(flops=1, bytes_accessed=1, transcendentals=0),
    )(at, inputs, x_other, gain1, bias1, qkv_weight, qkv_weight, qkv_weight, qv_bias, qv_bias,
      out_weight, out_bias, gain2, bias2)


def gelu_and_slope(u):
    c = math.sqrt(2 / math.pi)
    square = u * u
    bent = jnp.tanh(u * (c + (c * 0.044715) * square))
    half = 0.5 + 0.5 * bent
    slope = half + u * (0.5 - 0.5 * bent * bent) * (c + (3 * c * 0.044715) * square)
    return u * half, slope


def feed_kernel(
    at_ref, rows_ref, n2_ref, m_ref, c_mine, c_other, up, up_bias, down, down_bias, gain2, count,
    g_out, du_theirs, du_mine, y_mine, y_send, dm_out, db1_out, db1_theirs, db2_out, db2_theirs, vec_out,
    y_sum, dn_sum,
):
    step = pl.program_id(0)
    steps = pl.num_programs(0)
    core, place = at_ref[0], at_ref[2]
    features = n2_ref.shape[1]
    width = up.shape[1]
    half = features // 2
    theirs = pl.ds(pl.multiple_of((1 - core) * half, half), half)

    @pl.when(step == 0)
    def _():
        join_row(place, c_mine, c_other, db2_out)
        db2_theirs[...] = db2_out[:, theirs]
        vec_out[...] = jnp.zeros_like(vec_out)
        vec_out[7:8, :] = jnp.sum(db2_out[...].astype(SINGLE), axis=0, keepdims=True)
        vec_out[12:13, 0:128] = count[...]

    n2 = n2_ref[...]
    hidden = dot_nn(n2, up[...]) + up_bias[...].astype(SINGLE)
    active, slope = gelu_and_slope(hidden)
    active = active.astype(LOW)
    g_out[...] = active
    grad = (dot_nt(db2_out[...], down[...]) * slope).astype(LOW)
    tile = lax.rem(step + (steps // 2) * (1 - core), steps)
    sums = jnp.sum(grad.astype(SINGLE), axis=0, keepdims=True)
    for part in range(width // features):
        vec_out[pl.ds(8 + tile * (width // features) + part, 1), :] = sums[
            :, part * features : (part + 1) * features
        ]

    @pl.when(step < steps // 2)
    def _():
        du_theirs[...] = grad

    @pl.when(step >= steps // 2)
    def _():
        du_mine[...] = grad

    y = dot_nn(active, down[...])
    dn = dot_nt(grad, up[...])

    @pl.when(step == 0)
    def _():
        y_sum[...] = y
        dn_sum[...] = dn

    @pl.when(step > 0)
    def _():
        y_sum[...] += y
        dn_sum[...] += dn

    @pl.when(step == steps - 1)
    def _():
        middle = m_ref[...]
        piece = y_mine.shape[0]
        present = (place < rows_ref[0, 0]).astype(SINGLE)
        y_sum[...] = (middle + y_sum[...] + down_bias[...].astype(SINGLE)) * present
        y_mine[...] = y_sum[pl.ds(pl.multiple_of(place * piece, piece), piece), :].astype(LOW)
        y_send[...] = y_sum[pl.ds(pl.multiple_of((1 - place) * piece, piece), piece), :].astype(LOW)
        normal, inverse = normalize(middle)
        grad_n = dn_sum[...]
        vec_out[5:6, :] = jnp.sum(grad_n * normal, axis=0, keepdims=True)
        vec_out[6:7, :] = jnp.sum(grad_n, axis=0, keepdims=True)
        back = norm_back(normal, inverse, grad_n, gain2[...].astype(SINGLE))
        dm = db2_out[...].astype(SINGLE) + back
        dm_out[...] = dm
        low = dm.astype(LOW)
        db1_out[...] = low
        db1_theirs[...] = db1_out[:, theirs]
        vec_out[4:5, :] = jnp.sum(low.astype(SINGLE), axis=0, keepdims=True)


def feed(at, rows, n2, middle, c_mine, c_other, up, up_bias, down, down_bias, gain2, count):
    length, features = n2.shape
    piece = length // 2
    hidden = up.shape[1]
    steps = hidden // features
    half = steps // 2
    width = features

    def whole(*shape):
        return pl.BlockSpec(shape, lambda f, at: (0,) * len(shape))

    def tile(f, at):
        return lax.rem(f + half * (1 - at[0]), steps)

    act = jax.ShapeDtypeStruct((length, features), LOW)
    part = jax.ShapeDtypeStruct((piece, features), LOW)
    vec = whole(1, features)
    return pl.pallas_call(
        feed_kernel,
        grid_spec=pltpu.PrefetchScalarGridSpec(
            num_scalar_prefetch=1,
            grid=(steps,),
            in_specs=[
                pl.BlockSpec(memory_space=pltpu.SMEM),
                whole(length, features), whole(length, features),
                whole(piece, features), whole(piece, features),
                pl.BlockSpec((features, width), lambda f, at: (0, tile(f, at))),
                pl.BlockSpec((1, width), lambda f, at: (0, tile(f, at))),
                pl.BlockSpec((width, features), lambda f, at: (tile(f, at), 0)),
                vec, vec, whole(1, 128),
            ],
            out_specs=[
                pl.BlockSpec((length, width), lambda f, at: (0, tile(f, at))),
                pl.BlockSpec((length, width), lambda f, at: (0, jnp.minimum(f, half - 1))),
                pl.BlockSpec((length, width), lambda f, at: (0, jnp.maximum(f - half, 0))),
                whole(piece, features), whole(piece, features),
                whole(length, features), whole(length, features), whole(length, features // 2),
                whole(length, features), whole(length, features // 2),
                whole(16, features),
            ],
            scratch_shapes=[pltpu.VMEM((length, features), SINGLE)] * 2,
        ),
        out_shape=[
            jax.ShapeDtypeStruct((length, hidden), LOW),
            jax.ShapeDtypeStruct((length, hidden // 2), LOW),
            jax.ShapeDtypeStruct((length, hidden // 2), LOW),
            part, part,
            jax.ShapeDtypeStruct((length, features), SINGLE),
            act, jax.ShapeDtypeStruct((length, features // 2), LOW),
            act, jax.ShapeDtypeStruct((length, features // 2), LOW),
            jax.ShapeDtypeStruct((16, features), SINGLE),
        ],
        compiler_params=pltpu.CompilerParams(vmem_limit_bytes=40 << 20),
        cost_estimate=pl.CostEstimate(flops=1, bytes_accessed=1, transcendentals=0),
    )(at, rows, n2, middle, c_mine, c_other, up, up_bias, down, down_bias, gain2, count)


def back_kernel(
    at_ref, x_mine, x_other, gain1, query_ref, keys_ref, values_ref, probs_ref, db1, dm, wo,
    wq, wk, wv, vec_in, dp_theirs, dp_mine, x_grad_mine, x_grad_send, vec_out,
    row, dp, dn_sum,
):
    group = pl.program_id(0)
    groups = pl.num_programs(0)
    core, place = at_ref[0], at_ref[2]
    features = db1.shape[1]
    grad_mixed = dot_nt(db1[...], wo[...]).astype(LOW)
    query = query_ref[...] * HD**-0.5
    keys = keys_ref[...] * HD**-0.5
    values = values_ref[...]
    dq = dk = dv = None
    for head in range(GROUP):
        mask = head_mask(head)
        grad_head = jnp.where(mask, grad_mixed, 0)
        probs_low = probs_ref[head]
        probs = probs_low.astype(SINGLE)
        grad_probs = dot_nt(grad_head, values)
        inner = jnp.sum(probs * grad_probs, axis=-1, keepdims=True)
        grad_scores = (probs * (grad_probs - inner)).astype(LOW)
        part = dot_nn(grad_scores, keys)
        dq = part if head == 0 else jnp.where(mask, part, dq)
        part = dot_tn(grad_scores, query)
        dk = part if head == 0 else jnp.where(mask, part, dk)
        part = dot_tn(probs_low, grad_mixed)
        dv = part if head == 0 else jnp.where(mask, part, dv)
    dq, dk, dv = dq.astype(LOW), dk.astype(LOW), dv.astype(LOW)
    for which, value in enumerate((dq, dk, dv)):
        dp[:, pl.ds(pl.multiple_of(which * features + group * GW, GW), GW)] = value
    at = pl.ds(pl.multiple_of(group * GW, GW), GW)

    @pl.when(group == 0)
    def _():
        vec_out[...] = vec_in[...]

    vec_out[2:3, at] = jnp.sum(dq.astype(SINGLE), axis=0, keepdims=True)
    vec_out[3:4, at] = jnp.sum(dv.astype(SINGLE), axis=0, keepdims=True)
    dn = dot_nt(dq, wq[...]) + dot_nt(dk, wk[...]) + dot_nt(dv, wv[...])

    @pl.when(group == 0)
    def _():
        dn_sum[...] = dn

    @pl.when(group > 0)
    def _():
        dn_sum[...] += dn

    @pl.when(group == groups - 1)
    def _():
        half = dp_mine.shape[1]
        dp_theirs[...] = dp[:, pl.ds(pl.multiple_of((1 - core) * half, half), half)]
        dp_mine[...] = dp[:, pl.ds(pl.multiple_of(core * half, half), half)]
        join_row(place, x_mine, x_other, row)
        normal, inverse = normalize(row[...])
        grad_n = dn_sum[...]
        vec_out[0:1, :] = jnp.sum(grad_n * normal, axis=0, keepdims=True)
        vec_out[1:2, :] = jnp.sum(grad_n, axis=0, keepdims=True)
        back = norm_back(normal, inverse, grad_n, gain1[...].astype(SINGLE))
        row[...] = dm[...] + back
        piece = x_mine.shape[0]
        x_grad_mine[...] = row[pl.ds(pl.multiple_of(place * piece, piece), piece), :].astype(LOW)
        x_grad_send[...] = row[pl.ds(pl.multiple_of((1 - place) * piece, piece), piece), :].astype(LOW)


def back(at, inputs, x_other, gain1, query, keys, values, probs, db1, dm, out_weight, qkv_weight, vec, after):
    piece, features = x_other.shape
    length = 2 * piece
    groups = features // GW

    def whole(*shape):
        return pl.BlockSpec(shape, lambda g, at: (0,) * len(shape))

    def columns(first):
        return pl.BlockSpec((features, GW), lambda g, at: (0, first * groups + g))

    act = pl.BlockSpec((length, GW), lambda g, at: (0, g))
    half = jax.ShapeDtypeStruct((length, 3 * features // 2), LOW)
    part = jax.ShapeDtypeStruct((piece, features), LOW)
    return pl.pallas_call(
        behind(back_kernel, len(after)),
        grid_spec=pltpu.PrefetchScalarGridSpec(
            num_scalar_prefetch=1,
            grid=(groups,),
            in_specs=[
                *tokens(after),
                pl.BlockSpec((None, piece, features), lambda g, at: (at[2], 0, 0)),
                whole(piece, features), whole(1, features),
                act, act, act,
                pl.BlockSpec((GROUP, length, length), lambda g, at: (g, 0, 0)),
                whole(length, features), whole(length, features),
                pl.BlockSpec((GW, features), lambda g, at: (g, 0)),
                columns(0), columns(1), columns(2), whole(16, features),
            ],
            out_specs=[whole(*half.shape), whole(*half.shape), whole(*part.shape), whole(*part.shape), whole(16, features)],
            scratch_shapes=[
                pltpu.VMEM((length, features), SINGLE),
                pltpu.VMEM((length, 3 * features), LOW),
                pltpu.VMEM((length, features), SINGLE),
            ],
        ),
        out_shape=[half, half, part, part, jax.ShapeDtypeStruct((16, features), SINGLE)],
        compiler_params=pltpu.CompilerParams(vmem_limit_bytes=40 << 20),
        cost_estimate=pl.CostEstimate(flops=1, bytes_accessed=1, transcendentals=0),
    )(at, *after, inputs, x_other, gain1, query, keys, values, probs, db1, dm, out_weight,
      qkv_weight, qkv_weight, qkv_weight, vec)


def lanes_kernel(at_ref, left, left_other, right, right_other, out, *whole, halved):
    total = (dot_tn(left[...], right[...]) + dot_tn(left_other[...], right_other[...])).astype(LOW)
    if halved:
        half = total.shape[0] // 2
        whole[0][...] = total
        for side in (0, 1):
            first = pl.multiple_of((at_ref[2] ^ side) * half, half)
            out[0, side * half : (side + 1) * half, :] = whole[0][pl.ds(first, half), :]
    else:
        out[0] = total


def grad_lanes(at, left, left_other, right, right_other, chunk_ids, count, after=(), halved=False):
    length, tall = left.shape
    rows = tall // count
    width = right_other.shape[1]
    pick = len(chunk_ids)

    def chunk(j, at):
        number = jnp.int32(chunk_ids[0])
        for spot, value in enumerate(chunk_ids[1:], 1):
            number = jnp.where(j == spot, value, number)
        return (0, number ^ at[1])

    return pl.pallas_call(
        behind(functools.partial(lanes_kernel, halved=halved), len(after)),
        grid_spec=pltpu.PrefetchScalarGridSpec(
            num_scalar_prefetch=1,
            grid=(pick,),
            in_specs=[
                *tokens(after),
                pl.BlockSpec((length, rows), chunk),
                pl.BlockSpec((length, rows), chunk),
                pl.BlockSpec((length, width), lambda j, at: (0, at[0])),
                pl.BlockSpec((length, width), lambda j, at: (0, 0)),
            ],
            out_specs=pl.BlockSpec((1, rows, width), lambda j, at: (j, 0, 0)),
            scratch_shapes=[pltpu.VMEM((rows, width), LOW)] * halved,
        ),
        out_shape=jax.ShapeDtypeStruct((pick, rows, width), LOW),
        compiler_params=pltpu.CompilerParams(vmem_limit_bytes=32 << 20),
        cost_estimate=pl.CostEstimate(flops=1, bytes_accessed=1, transcendentals=0),
    )(at, *after, left, left_other, right, right_other)


def rows_kernel(at_ref, left, left_other, right, right_other, *rest, count, sent, kept, with_vec, halved):
    if with_vec:
        vec, vec_other, send, keep, whole, spread = rest
    else:
        send, keep, whole = rest
    whole[...] = (
        dot_tn(left[...], right[...]) + dot_tn(left_other[...], right_other[...])
    ).astype(LOW)
    rows = whole.shape[0] // count
    if with_vec:
        total = vec[...] + vec_other[...]
        wide = 4 * total.shape[1] // count
        spread[...] = jnp.zeros_like(spread)
        for chunk in range(count):
            spread[chunk, 0:8, :rows] = total[0:8, chunk * rows : (chunk + 1) * rows]
            line = 8 + chunk * wide // total.shape[1]
            begin = chunk * wide % total.shape[1]
            for part in range(wide // rows):
                spread[chunk, 8 + part : 9 + part, :rows] = total[
                    line : line + 1, begin + part * rows : begin + (part + 1) * rows
                ]
            spread[chunk, 12:13, : 2 * DIGITS] = total[12:13, : 2 * DIGITS]
    for out, numbers in ((send, sent), (keep, kept)):
        if with_vec:
            out[:, rows:, :] = jnp.zeros_like(out[:, rows:, :])
        for spot, number in enumerate(numbers):
            chunk = at_ref[1] ^ number
            if halved:
                half = rows // 2
                for side in (0, 1):
                    first = chunk * rows + (at_ref[2] ^ side) * half
                    out[spot, side * half : (side + 1) * half, :] = whole[
                        pl.ds(pl.multiple_of(first, half), half), :
                    ]
            else:
                out[spot, :rows, :] = whole[pl.ds(pl.multiple_of(chunk * rows, rows), rows), :]
            if with_vec:
                out[spot, rows:, :128] = spread[chunk].astype(LOW)


def grad_rows(at, left, left_other, right, right_other, sent, kept, tile, pick_core, vecs=(), after=(), halved=False):
    length, tall = left.shape
    count = len(sent) + len(kept)
    rows = tall // count
    width = right_other.shape[1]
    steps = width // tile
    more = 16 if vecs else 0
    return pl.pallas_call(
        behind(
            functools.partial(
                rows_kernel, count=count, sent=sent, kept=kept, with_vec=bool(vecs), halved=halved
            ),
            len(after),
        ),
        grid_spec=pltpu.PrefetchScalarGridSpec(
            num_scalar_prefetch=1,
            grid=(steps,),
            in_specs=[
                *tokens(after),
                pl.BlockSpec((length, tall), lambda j, at: (0, 0)),
                pl.BlockSpec((length, tall), lambda j, at: (0, 0)),
                pl.BlockSpec((length, tile), lambda j, at: (0, (at[0] * steps if pick_core else 0) + j)),
                pl.BlockSpec((length, tile), lambda j, at: (0, j)),
                *[pl.BlockSpec(v.shape, lambda j, at: (0, 0)) for v in vecs],
            ],
            out_specs=[
                pl.BlockSpec((len(sent), rows + more, tile), lambda j, at: (0, 0, j)),
                pl.BlockSpec((len(kept), rows + more, tile), lambda j, at: (0, 0, j)),
            ],
            scratch_shapes=[pltpu.VMEM((tall, tile), LOW)]
            + [pltpu.VMEM((count, 16, 128), SINGLE)] * bool(vecs),
        ),
        out_shape=[
            jax.ShapeDtypeStruct((len(sent), rows + more, width), LOW),
            jax.ShapeDtypeStruct((len(kept), rows + more, width), LOW),
        ],
        compiler_params=pltpu.CompilerParams(vmem_limit_bytes=32 << 20),
        cost_estimate=pl.CostEstimate(flops=1, bytes_accessed=1, transcendentals=0),
    )(at, *after, left, left_other, right, right_other, *vecs)


def counts_of(vec):
    line = vec[12:13, :].astype(SINGLE)
    lane = lax.broadcasted_iota(jnp.int32, line.shape, 1)
    worth = lax.shift_left(jnp.ones_like(lane), lax.rem(lane, DIGITS)).astype(SINGLE)
    return [
        jnp.sum(
            jnp.where((lane >= half * DIGITS) & (lane < (half + 1) * DIGITS), line * worth, 0.0),
            axis=1,
            keepdims=True,
        )
        for half in (0, 1)
    ]


def finish_kernel(at_ref, vec, mine, other, out):
    core = at_ref[0]
    first, second = counts_of(vec[...])
    whole = first + second
    rows = out.shape[0]
    width = mine.shape[1]
    out[:, pl.ds(pl.multiple_of(core * width, 128), width)] = (
        mine[:rows, :].astype(SINGLE) / whole
    )
    out[:, pl.ds(pl.multiple_of((1 - core) * width, 128), width)] = (
        other[:rows, :].astype(SINGLE) / whole
    )


def finish(at, vec, mine, other, rows):
    width = mine.shape[1]
    vmem = pl.BlockSpec(memory_space=pltpu.VMEM)
    return pl.pallas_call(
        finish_kernel,
        in_specs=[pl.BlockSpec(memory_space=pltpu.SMEM), vmem, vmem, vmem],
        out_specs=vmem,
        out_shape=jax.ShapeDtypeStruct((rows, 2 * width), SINGLE),
        cost_estimate=pl.CostEstimate(flops=1, bytes_accessed=1, transcendentals=0),
    )(at, vec, mine, other)


def finish_halves_kernel(at_ref, vec, *refs):
    parts, out = refs[:4], refs[4]
    core, place = at_ref[0], at_ref[2]
    first, second = counts_of(vec[...])
    whole = first + second
    half, width = parts[0].shape
    for number, part in enumerate(parts):
        row = pl.multiple_of((place ^ (number & 1)) * half, half)
        column = pl.multiple_of((core ^ (number >> 1)) * width, 128)
        out[pl.ds(row, half), pl.ds(column, width)] = part[...].astype(SINGLE) / whole


def finish_halves(at, vec, parts):
    half, width = parts[0].shape
    vmem = pl.BlockSpec(memory_space=pltpu.VMEM)
    return pl.pallas_call(
        finish_halves_kernel,
        in_specs=[pl.BlockSpec(memory_space=pltpu.SMEM)] + [vmem] * 5,
        out_specs=vmem,
        out_shape=jax.ShapeDtypeStruct((2 * half, 2 * width), SINGLE),
        cost_estimate=pl.CostEstimate(flops=1, bytes_accessed=1, transcendentals=0),
    )(at, vec, *parts)


def close_kernel(vec, counts, plain, qv, up):
    first, second = counts_of(vec[...])
    counts[:, 0:1] = first.astype(jnp.int32)
    counts[:, 1:2] = second.astype(jnp.int32)
    rows = plain.shape[1]
    scaled = vec[...].astype(SINGLE) / (first + second)
    plain[...] = scaled[0:8, :rows]
    qv[...] = scaled[2:4, :rows]
    for part in range(up.shape[1] // rows):
        up[:, part * rows : (part + 1) * rows] = scaled[8 + part : 9 + part, :rows]


def close(vec, rows, wide):
    vmem = pl.BlockSpec(memory_space=pltpu.VMEM)
    return pl.pallas_call(
        close_kernel,
        in_specs=[vmem],
        out_specs=[vmem] * 4,
        out_shape=[
            jax.ShapeDtypeStruct((1, 2), jnp.int32),
            jax.ShapeDtypeStruct((8, rows), SINGLE),
            jax.ShapeDtypeStruct((2, rows), SINGLE),
            jax.ShapeDtypeStruct((1, wide), SINGLE),
        ],
        cost_estimate=pl.CostEstimate(flops=1, bytes_accessed=1, transcendentals=0),
    )(vec)


STAGES = ((1, "seq", 0, 2, "gather"), (0, "seq", 1, 2, "gather"), (0, "seq", 1, 2, "gather"), (1, 0, 2, "seq"))
STEPS = "uduoduqoqudqodqo"


def swap_pairs(size, bit):
    return [(i, i ^ bit) for i in range(size)]


def added(one, two):
    return (one.astype(SINGLE) + two.astype(SINGLE)).astype(LOW)


def split_numbers(count, stage):
    sent = [j for j in range(count) if j >> stage & 1]
    return sent, [j for j in range(count) if not j >> stage & 1]


class Order:
    def __init__(self):
        self.last = None

    def tie(self, value):
        if self.last is not None:
            value, _ = lax.optimization_barrier((value, self.last))
        return value

    def mark(self, value):
        self.last = value


class Sum:
    def __init__(self, order, groups, stages, send, keep):
        self.order, self.groups, self.stages = order, groups, list(stages)
        self.given = tuple(stages)
        self.left = [b for b in range(groups.bit_length() - 2, -1, -1) if b != stages[0]]
        self.keep = keep
        self.done = []
        self.go(send)

    def go(self, send):
        stage = self.stages[0]
        if stage in ("seq", "gather"):
            self.flying = lax.ppermute(send, "seq", swap_pairs(2, 1))
        else:
            self.flying = lax.ppermute(send, "dp", swap_pairs(self.groups, 1 << stage))

    def split(self, value, stage):
        if stage == "gather" or (stage == "seq" and len(self.stages) == 1):
            return value, value
        if stage == "seq":
            half = value.shape[-2] // 2
            return value[..., :half, :], value[..., half:, :]
        spot = self.left.index(stage)
        cut = value.reshape((2,) * len(self.left) + value.shape[1:])
        shape = (-1,) + value.shape[1:]
        return tuple(
            lax.index_in_dim(cut, side, spot, keepdims=False).reshape(shape) for side in (0, 1)
        )

    def step(self):
        other = self.order.tie(self.flying)
        self.stages.pop(0)
        if not self.stages:
            self.total = added(self.keep, other)
            if self.total.ndim == 3:
                self.total = self.total[0]
            self.order.mark(self.total)
            return
        following = self.stages[0]
        if following == "gather":
            self.total = added(self.keep, other)[0]
            self.order.mark(self.total)
            self.go(self.total)
            return
        one, two = self.split(self.keep, following), self.split(other, following)
        send = added(one[1], two[1])
        same = following == "seq" and len(self.stages) == 1
        self.keep = send if same else added(one[0], two[0])
        if following != "seq":
            self.left.remove(following)
        self.order.mark(send)
        self.go(send)


def body_fast(
    inputs,
    cotangent,
    row_counts,
    response_mask,
    norm1_gain,
    norm1_bias,
    qkv_weight,
    qv_bias,
    out_weight,
    out_bias,
    norm2_gain,
    norm2_bias,
    up_weight,
    up_bias,
    down_weight,
    down_bias,
):
    groups = lax.axis_size("dp")
    pair = swap_pairs(2, 1)
    core, own, place = (lax.axis_index(a) for a in ("src", "dp", "seq"))
    at = jnp.stack([core, own, place]).astype(jnp.int32)
    gain1, bias1, gain2, bias2, out_bias, down_bias, up_bias = (
        v[None]
        for v in (norm1_gain, norm1_bias, norm2_gain, norm2_bias, out_bias, down_bias, up_bias)
    )

    x_both = inputs[0, 0]
    x_other = lax.ppermute(
        lax.dynamic_index_in_dim(x_both, 1 - place, 0, keepdims=False), "seq", pair
    )
    c_send, c_mine, count = prepare(at, row_counts, cotangent[0, 0], response_mask[0, 0])
    c_other = lax.ppermute(c_send, "seq", pair)

    order = Order()

    n1, query, keys, values, probs, mixed, middle, n2 = attend(
        at, x_both, x_other, gain1, bias1, qkv_weight, qv_bias[:, None], out_weight, out_bias, gain2, bias2
    )
    active, du_theirs, du_mine, y_mine, y_send, dm, db1, db1_theirs, db2, db2_theirs, vec = feed(
        at, row_counts, n2, middle, c_mine, c_other, up_weight, up_bias, down_weight, down_bias, gain2, count
    )

    def from_core(value):
        return lax.ppermute(value, "src", pair)

    def numbers(stages):
        return split_numbers(groups, stages[0])

    up_stages, down_stages, qkv_stages, out_stages = STAGES
    up_parts = grad_rows(
        at, n2, from_core(n2), du_mine, from_core(du_theirs), *numbers(up_stages), 512, False,
        halved="gather" in up_stages,
    )
    order.mark(up_parts[0])
    up_sum = Sum(order, groups, up_stages, *up_parts)
    active_other, db2_other = from_core(active), from_core(db2_theirs)
    down_parts = []
    for ids in numbers(down_stages):
        down_parts.append(
            grad_lanes(
                order.tie(at), active, active_other, db2, db2_other, ids, groups,
                halved="gather" in down_stages,
            )
        )
        order.mark(down_parts[-1])
    down_sum = Sum(order, groups, down_stages, *down_parts)
    dp_theirs, dp_mine, x_grad_mine, x_grad_send, vec = back(
        order.tie(at), x_both, x_other, gain1, query, keys, values, probs, db1, dm, out_weight, qkv_weight, vec, ()
    )
    order.mark(vec)
    out_parts = grad_rows(
        order.tie(at), mixed, from_core(mixed), db1, from_core(db1_theirs), *numbers(out_stages), 384, True,
        (vec, from_core(vec)), halved="gather" in out_stages,
    )
    order.mark(out_parts[0])
    out_sum = Sum(order, groups, out_stages, *out_parts)
    qkv_parts = grad_rows(
        order.tie(at), n1, from_core(n1), dp_mine, from_core(dp_theirs), *numbers(qkv_stages), 384, False,
        halved="gather" in qkv_stages,
    )
    order.mark(qkv_parts[0])
    qkv_sum = Sum(order, groups, qkv_stages, *qkv_parts)
    sums = {"u": up_sum, "d": down_sum, "o": out_sum, "q": qkv_sum}
    for name in STEPS:
        sums[name].step()

    rows = out_weight.shape[0] // groups
    vec = out_sum.total[rows:, :128]

    def joined(done, rows):
        if "gather" in done.given:
            parts = [done.total, done.flying]
            return finish_halves(at, vec, parts + [from_core(p) for p in parts])
        return finish(at, vec, done.total, from_core(done.total), rows)

    def rows_home(mine, send):
        other = lax.ppermute(send, "seq", pair)
        both = jnp.where(place == 0, jnp.stack([mine, other]), jnp.stack([other, mine]))
        return both[None, None]

    counts, plain, qv, up_small = close(vec, rows, up_bias.shape[1] // groups)
    return (
        rows_home(y_mine, y_send),
        rows_home(x_grad_mine, x_grad_send),
        counts[0],
        plain[0],
        plain[1],
        joined(qkv_sum, rows),
        qv,
        joined(out_sum, rows),
        plain[4],
        plain[5],
        plain[6],
        joined(up_sum, rows),
        up_small[0],
        joined(down_sum, 4 * rows),
        plain[7],
    )


def solution(mesh):
    placed = (
        P("src", "dp", None, "seq", None),
        P("src", "dp", None, "seq", None),
        P("src", "dp"),
        P("src", "dp", None, "seq"),
        P(),
        P(),
        P(),
        P(),
        P(),
        P(),
        P(),
        P(),
        P(),
        P(),
        P(),
        P(),
    )
    sizes = dict(mesh.shape)
    paired = sizes["src"] == 2 and sizes["seq"] == 2 and sizes["dp"] == 8
    return jax.shard_map(
        body_fast if paired else body_generic,
        mesh=mesh,
        in_specs=placed,
        out_specs=(
            P("src", "dp", None, "seq", None),
            P("src", "dp", None, "seq", None),
            P(),
            P("dp"),
            P("dp"),
            P("dp", None),
            P(None, "dp"),
            P("dp", None),
            P("dp"),
            P("dp"),
            P("dp"),
            P("dp", None),
            P("dp"),
            P("dp", None),
            P("dp"),
        ),
        check_vma=False,
    )
```

```python
import functools
import math

import jax
import jax.numpy as jnp
from jax import lax
from jax.experimental import pallas as pl
from jax.experimental.pallas import tpu as pltpu
from jax.sharding import PartitionSpec as P

H = 12
HD = 64


EPS = 1e-05
NEGATIVE = -1e30


def norm_apply(values, scaling, offset):
    centre = jnp.mean(values, axis=-1, keepdims=True)
    centered = values - centre
    spread = jnp.mean(centered * centered, axis=-1, keepdims=True)
    return centered * lax.rsqrt(spread + EPS) * scaling + offset


def causal_scores(query_part, keys_part, allowed):
    scores = jnp.einsum(
        "rqhd,rkhd->rhqk", query_part, keys_part, preferred_element_type=jnp.float32
    )
    scores = scores * HD ** (-0.5)
    return jnp.where(allowed, scores, NEGATIVE)


def attend_forward(query_part, keys_part, values_part, allowed):
    scores = causal_scores(query_part, keys_part, allowed)
    highest = jnp.max(scores, axis=-1, keepdims=True)
    powers = jnp.exp(scores - highest)
    totals = jnp.sum(powers, axis=-1, keepdims=True)
    probs_low = (powers / totals).astype(jnp.bfloat16)
    mixed = jnp.einsum(
        "rhqk,rkhd->rqhd", probs_low, values_part, preferred_element_type=jnp.float32
    )
    return (mixed, highest, totals)


def attend_backward(query_part, keys_part, values_part, grad_part, highest, totals, allowed):
    scores = causal_scores(query_part, keys_part, allowed)
    probs = jnp.exp(scores - highest) / totals
    probs_low = probs.astype(jnp.bfloat16)
    grad_probs = jnp.einsum(
        "rqhd,rkhd->rhqk", grad_part, values_part, preferred_element_type=jnp.float32
    )
    inner = jnp.sum(probs * grad_probs, axis=-1, keepdims=True)
    grad_scores = (probs * (grad_probs - inner)).astype(jnp.bfloat16)
    factor = HD ** (-0.5)
    grad_query = (
        jnp.einsum("rhqk,rkhd->rqhd", grad_scores, keys_part, preferred_element_type=jnp.float32)
        * factor
    )
    grad_keys = (
        jnp.einsum("rhqk,rqhd->rkhd", grad_scores, query_part, preferred_element_type=jnp.float32)
        * factor
    )
    grad_values = jnp.einsum(
        "rhqk,rqhd->rkhd", probs_low, grad_part, preferred_element_type=jnp.float32
    )
    return (grad_query, grad_keys, grad_values)


def body_generic(
    inputs,
    cotangent,
    row_counts,
    response_mask,
    norm1_gain,
    norm1_bias,
    qkv_weight,
    qv_bias,
    out_weight,
    out_bias,
    norm2_gain,
    norm2_bias,
    up_weight,
    up_bias,
    down_weight,
    down_bias,
):
    slots = inputs.shape[2]
    piece_len = inputs.shape[3]
    features = inputs.shape[4]
    tokens = slots * piece_len
    blocks_seq = lax.axis_size("seq")
    row_len = piece_len * blocks_seq
    group_heads = math.gcd(H, 4)
    bfloat = jnp.bfloat16
    single = jnp.float32
    present_int = (jnp.arange(slots) < row_counts[0, 0]).astype(jnp.int32)
    weight = (response_mask[0, 0] * present_int[:, None]).astype(single)
    local_count = jnp.sum(response_mask[0, 0] * present_int[:, None])
    picked = jnp.where(jnp.arange(lax.axis_size("src")) == lax.axis_index("src"), local_count, 0)
    source_counts = lax.psum(picked, ("src", "dp", "seq"))
    whole = jnp.sum(source_counts).astype(single)
    source = inputs.reshape(tokens, features).astype(single)
    normed, norm1_pull = jax.vjp(
        norm_apply, source, norm1_gain.astype(single), norm1_bias.astype(single)
    )
    normed_low = normed.astype(bfloat)
    bias_query = qv_bias[0].astype(single)
    joined = jnp.concatenate([bias_query, jnp.zeros_like(bias_query), qv_bias[1].astype(single)])
    projected = jnp.dot(normed_low, qkv_weight, preferred_element_type=single) + joined
    proj_low = projected.astype(bfloat)
    query = proj_low[:, :features].reshape(slots, piece_len, H, HD)
    keys_own = proj_low[:, features : 2 * features].reshape(slots, piece_len, features)
    values_own = proj_low[:, 2 * features :].reshape(slots, piece_len, features)
    keys_all, values_all = (
        lax.all_gather(keys_own, "seq", axis=1, tiled=True),
        lax.all_gather(values_own, "seq", axis=1, tiled=True),
    )
    query_pos = lax.axis_index("seq") * piece_len + jnp.arange(piece_len)
    allowed = query_pos[:, None] >= jnp.arange(row_len)[None, :]
    keys_heads = keys_all.reshape(slots, row_len, H, HD)
    values_heads = values_all.reshape(slots, row_len, H, HD)
    mixed_parts = []
    kept_stats = []
    for group in range(H // group_heads):
        first = group * group_heads
        last = first + group_heads
        mixed, highest, totals = attend_forward(
            query[:, :, first:last],
            keys_heads[:, :, first:last],
            values_heads[:, :, first:last],
            allowed,
        )
        mixed_parts.append(mixed)
        kept_stats.append((highest, totals))
    attended = jnp.concatenate(mixed_parts, axis=2).reshape(tokens, features)
    attended_low = attended.astype(bfloat)
    branch = jnp.dot(attended_low, out_weight, preferred_element_type=single) + out_bias.astype(
        single
    )
    middle = source + branch
    normed_two, norm2_pull = jax.vjp(
        norm_apply, middle, norm2_gain.astype(single), norm2_bias.astype(single)
    )
    normed_two_low = normed_two.astype(bfloat)
    hidden = jnp.dot(normed_two_low, up_weight, preferred_element_type=single) + up_bias.astype(
        single
    )
    active, gelu_pull = jax.vjp(functools.partial(jax.nn.gelu, approximate=True), hidden)
    active_low = active.astype(bfloat)
    branch_two = jnp.dot(active_low, down_weight, preferred_element_type=single) + down_bias.astype(
        single
    )
    result = middle + branch_two
    present_tok = jnp.repeat(present_int.astype(single), piece_len)
    output = (result * present_tok[:, None]).astype(bfloat).reshape(inputs.shape)
    incoming = cotangent.reshape(tokens, features).astype(single) * weight.reshape(tokens)[:, None]
    grad_branch_two = incoming.astype(bfloat)
    grad_down_weight = jnp.einsum(
        "tf,td->fd", active_low, grad_branch_two, preferred_element_type=single
    )
    grad_down_bias = jnp.sum(grad_branch_two.astype(single), axis=0)
    grad_active = jnp.einsum(
        "td,fd->tf", grad_branch_two, down_weight, preferred_element_type=single
    )
    grad_hidden = gelu_pull(grad_active)[0].astype(bfloat)
    grad_up_weight = jnp.einsum(
        "tm,tf->mf", normed_two_low, grad_hidden, preferred_element_type=single
    )
    grad_up_bias = jnp.sum(grad_hidden.astype(single), axis=0)
    grad_normed_two = jnp.einsum("tf,mf->tm", grad_hidden, up_weight, preferred_element_type=single)
    grad_mid_norm, grad_norm2_gain, grad_norm2_bias = norm2_pull(grad_normed_two)
    grad_middle = incoming + grad_mid_norm
    grad_branch = grad_middle.astype(bfloat)
    grad_out_weight = jnp.einsum(
        "tm,td->md", attended_low, grad_branch, preferred_element_type=single
    )
    grad_out_bias = jnp.sum(grad_branch.astype(single), axis=0)
    grad_attended = jnp.einsum("td,md->tm", grad_branch, out_weight, preferred_element_type=single)
    grad_heads = grad_attended.astype(bfloat).reshape(slots, piece_len, H, HD)
    query_grads = []
    key_grads = []
    value_grads = []
    for group in range(H // group_heads):
        first = group * group_heads
        last = first + group_heads
        highest, totals = kept_stats[group]
        grad_query, grad_keys, grad_values = attend_backward(
            query[:, :, first:last],
            keys_heads[:, :, first:last],
            values_heads[:, :, first:last],
            grad_heads[:, :, first:last],
            highest,
            totals,
            allowed,
        )
        query_grads.append(grad_query)
        key_grads.append(grad_keys)
        value_grads.append(grad_values)
    grad_query_all = jnp.concatenate(query_grads, axis=2).reshape(tokens, features)
    grad_keys_all = jnp.concatenate(key_grads, axis=2).reshape(slots, row_len, features)
    grad_values_all = jnp.concatenate(value_grads, axis=2).reshape(slots, row_len, features)
    grad_keys_own, grad_values_own = (
        lax.psum_scatter(
            grad_keys_all.astype(jnp.bfloat16), "seq", scatter_dimension=1, tiled=True
        ).astype(jnp.float32),
        lax.psum_scatter(
            grad_values_all.astype(jnp.bfloat16), "seq", scatter_dimension=1, tiled=True
        ).astype(jnp.float32),
    )
    grad_projected = jnp.concatenate(
        [
            grad_query_all,
            grad_keys_own.reshape(tokens, features),
            grad_values_own.reshape(tokens, features),
        ],
        axis=1,
    ).astype(bfloat)
    grad_qkv_weight = jnp.einsum(
        "tm,tn->mn", normed_low, grad_projected, preferred_element_type=single
    )
    column_sums = jnp.sum(grad_projected.astype(single), axis=0)
    grad_qv_bias = jnp.stack([column_sums[:features], column_sums[2 * features :]])
    grad_normed = jnp.einsum("tn,mn->tm", grad_projected, qkv_weight, preferred_element_type=single)
    grad_src_norm, grad_norm1_gain, grad_norm1_bias = norm1_pull(grad_normed)
    input_grad = (grad_middle + grad_src_norm).astype(bfloat).reshape(inputs.shape)
    grads = (
        grad_norm1_gain,
        grad_norm1_bias,
        grad_qkv_weight,
        grad_qv_bias,
        grad_out_weight,
        grad_out_bias,
        grad_norm2_gain,
        grad_norm2_bias,
        grad_up_weight,
        grad_up_bias,
        grad_down_weight,
        grad_down_bias,
    )
    summed = (
        lax.psum_scatter(
            grads[0].astype(jnp.bfloat16), "dp", scatter_dimension=0, tiled=True
        ).astype(jnp.float32),
        lax.psum_scatter(
            grads[1].astype(jnp.bfloat16), "dp", scatter_dimension=0, tiled=True
        ).astype(jnp.float32),
        lax.psum_scatter(
            grads[2].astype(jnp.bfloat16), "dp", scatter_dimension=0, tiled=True
        ).astype(jnp.float32),
        lax.psum_scatter(
            grads[3].astype(jnp.bfloat16), "dp", scatter_dimension=1, tiled=True
        ).astype(jnp.float32),
        lax.psum_scatter(
            grads[4].astype(jnp.bfloat16), "dp", scatter_dimension=0, tiled=True
        ).astype(jnp.float32),
        lax.psum_scatter(
            grads[5].astype(jnp.bfloat16), "dp", scatter_dimension=0, tiled=True
        ).astype(jnp.float32),
        lax.psum_scatter(
            grads[6].astype(jnp.bfloat16), "dp", scatter_dimension=0, tiled=True
        ).astype(jnp.float32),
        lax.psum_scatter(
            grads[7].astype(jnp.bfloat16), "dp", scatter_dimension=0, tiled=True
        ).astype(jnp.float32),
        lax.psum_scatter(
            grads[8].astype(jnp.bfloat16), "dp", scatter_dimension=0, tiled=True
        ).astype(jnp.float32),
        lax.psum_scatter(
            grads[9].astype(jnp.bfloat16), "dp", scatter_dimension=0, tiled=True
        ).astype(jnp.float32),
        lax.psum_scatter(
            grads[10].astype(jnp.bfloat16), "dp", scatter_dimension=0, tiled=True
        ).astype(jnp.float32),
        lax.psum_scatter(
            grads[11].astype(jnp.bfloat16), "dp", scatter_dimension=0, tiled=True
        ).astype(jnp.float32),
    )
    summed = (
        lax.psum(summed[0].astype(jnp.bfloat16), ("src", "seq")).astype(jnp.float32),
        lax.psum(summed[1].astype(jnp.bfloat16), ("src", "seq")).astype(jnp.float32),
        lax.psum(summed[2].astype(jnp.bfloat16), ("src", "seq")).astype(jnp.float32),
        lax.psum(summed[3].astype(jnp.bfloat16), ("src", "seq")).astype(jnp.float32),
        lax.psum(summed[4].astype(jnp.bfloat16), ("src", "seq")).astype(jnp.float32),
        lax.psum(summed[5].astype(jnp.bfloat16), ("src", "seq")).astype(jnp.float32),
        lax.psum(summed[6].astype(jnp.bfloat16), ("src", "seq")).astype(jnp.float32),
        lax.psum(summed[7].astype(jnp.bfloat16), ("src", "seq")).astype(jnp.float32),
        lax.psum(summed[8].astype(jnp.bfloat16), ("src", "seq")).astype(jnp.float32),
        lax.psum(summed[9].astype(jnp.bfloat16), ("src", "seq")).astype(jnp.float32),
        lax.psum(summed[10].astype(jnp.bfloat16), ("src", "seq")).astype(jnp.float32),
        lax.psum(summed[11].astype(jnp.bfloat16), ("src", "seq")).astype(jnp.float32),
    )
    final = [g / whole for g in summed]
    return (
        output,
        input_grad,
        source_counts,
        final[0],
        final[1],
        final[2],
        final[3],
        final[4],
        final[5],
        final[6],
        final[7],
        final[8],
        final[9],
        final[10],
        final[11],
    )


WAYS = {
    "u": ("x12y", "12xy"),
    "d": ("yx12", "1yx2"),
    "o": ("yx12", "y12x"),
    "q": ("yx12", "xy12"),
}
EVENTS = "UDCIuQOdoqdouqYduoqudoqodouqioyuqd"
BITS = {"y": 1, "1": 2, "2": 4}


COSTS = {"prepare": 2, "load": 4, "attend": 8, "feed_one": 5, "feed_two": 5, "back": 0, "input": 0, "lanes": 4, "rows": 4, "result": 0}
AXES = ("src", "dp", "seq")
SINGLE = jnp.float32
LOW = jnp.bfloat16
GROUP = 4
GW = GROUP * HD
DIGITS = 16


def dot_nt(left, right):
    return lax.dot_general(left, right, (((1,), (1,)), ((), ())), preferred_element_type=SINGLE)


def dot_tn(left, right):
    return lax.dot_general(left, right, (((0,), (0,)), ((), ())), preferred_element_type=SINGLE)


def dot_nn(left, right):
    return jnp.dot(left, right, preferred_element_type=SINGLE)


def normalize(values):
    centered = values - jnp.mean(values, axis=-1, keepdims=True)
    inverse = lax.rsqrt(jnp.mean(centered * centered, axis=-1, keepdims=True) + EPS)
    return centered * inverse, inverse


def norm_back(normal, inverse, grad, gain):
    scaled = grad * gain
    return inverse * (
        scaled
        - jnp.mean(scaled, axis=-1, keepdims=True)
        - normal * jnp.mean(scaled * normal, axis=-1, keepdims=True)
    )


def head_mask(head):
    lanes = lax.broadcasted_iota(jnp.int32, (1, GW), 1)
    return (lanes >= head * HD) & (lanes < (head + 1) * HD)


def rows_at(first, count):
    return pl.ds(pl.multiple_of(first, count), count)


def where_am_i():
    return tuple(lax.axis_index(axis) for axis in AXES)


def call(name, kernel, operands, outs, scratch=(), loaded=()):
    vmem = pl.BlockSpec(memory_space=pltpu.VMEM)
    return pl.pallas_call(
        kernel,
        in_specs=[pl.BlockSpec(memory_space=pl.ANY)] * len(loaded) + [vmem] * len(operands),
        out_specs=[vmem] * (len(loaded) + len(outs)),
        out_shape=[jax.ShapeDtypeStruct(v.shape, v.dtype) for v in loaded]
        + [jax.ShapeDtypeStruct(*o) for o in outs],
        scratch_shapes=[pltpu.VMEM(*s) for s in scratch]
        + [pltpu.SemaphoreType.DMA((len(loaded),))] * bool(loaded),
        compiler_params=pltpu.CompilerParams(vmem_limit_bytes=16 << 20),
        cost_estimate=pl.CostEstimate(
            flops=int(COSTS[name] * 10**9) + 1, bytes_accessed=1, transcendentals=0
        ),
    )(*in_hbm(loaded), *operands)


def prepare_kernel(*refs):
    rows_ref, ins, refs = refs[0], refs[1:14], refs[14:]
    x_mine, c_send, c_mine, count_ref, small, wqkv, wo = refs[:7]
    held, sems = refs[7:18], refs[18]
    core, _, place = where_am_i()
    copies = [
        pltpu.make_async_copy(source, target, sems.at[i])
        for i, (source, target) in enumerate(zip(ins, held + (wqkv, wo)))
    ]
    for copy in copies:
        copy.start()
    for copy in copies[:11]:
        copy.wait()
    (
        mask_ref, x_ref, cot_ref, gain1, bias1, qv_bias, out_bias, gain2, bias2, down_bias, up_bias,
    ) = held
    piece = mask_ref.shape[1]
    diagonal = lax.broadcasted_iota(jnp.int32, (piece, piece), 0) == lax.broadcasted_iota(
        jnp.int32, (piece, piece), 1
    )
    rows = rows_ref[0, 0]

    def column(row):
        kept = mask_ref[pl.ds(row, 1), :].astype(SINGLE) * (row < rows).astype(SINGLE)
        return jnp.sum(jnp.where(diagonal, kept, 0.0), axis=1, keepdims=True), kept

    weight_send, kept_send = column(1 - place)
    c_send[...] = (cot_ref[1 - place].astype(SINGLE) * weight_send).astype(LOW)
    weight_mine, kept_mine = column(place)
    c_mine[...] = (cot_ref[place].astype(SINGLE) * weight_mine).astype(LOW)
    x_mine[...] = x_ref[place]
    count = jnp.sum(kept_mine + kept_send, axis=1, keepdims=True).astype(jnp.int32)
    lane = lax.broadcasted_iota(jnp.int32, count_ref.shape, 1) - core * DIGITS
    digit = lax.shift_right_logical(
        jnp.broadcast_to(count, count_ref.shape), jnp.clip(lane, 0, DIGITS - 1)
    )
    count_ref[...] = jnp.where((lane >= 0) & (lane < DIGITS), digit & 1, 0).astype(SINGLE)
    features = small.shape[1]
    small[12:16, :] = jnp.broadcast_to((place < rows).astype(SINGLE), (4, features))
    small[2:4, :] = qv_bias[...].astype(SINGLE)
    for line, value in ((0, gain1), (1, bias1), (4, out_bias), (5, gain2), (6, bias2), (7, down_bias)):
        small[line : line + 1, :] = value[...].astype(SINGLE)[None, :]
    ups = up_bias[...].astype(SINGLE)[None, :]
    for part in range(ups.shape[1] // features):
        small[8 + part : 9 + part, :] = ups[:, part * features : (part + 1) * features]
    for copy in copies[11:]:
        copy.wait()


def in_hbm(values):
    return [pltpu.with_memory_space_constraint(value, pltpu.HBM) for value in values]


def prepare(rows, mask, x, cot, vectors, weights):
    piece, features = cot.shape[1:]
    part = jax.ShapeDtypeStruct((piece, features), LOW)
    vmem = pl.BlockSpec(memory_space=pltpu.VMEM)
    held = (mask, x, cot, *vectors)
    return pl.pallas_call(
        prepare_kernel,
        in_specs=[pl.BlockSpec(memory_space=pltpu.SMEM)] + [pl.BlockSpec(memory_space=pl.ANY)] * 13,
        out_specs=[vmem] * 7,
        out_shape=[
            part,
            part,
            part,
            jax.ShapeDtypeStruct((1, 128), SINGLE),
            jax.ShapeDtypeStruct((16, features), SINGLE),
        ]
        + [jax.ShapeDtypeStruct(w.shape, w.dtype) for w in weights],
        scratch_shapes=[pltpu.VMEM(v.shape, v.dtype) for v in held]
        + [pltpu.SemaphoreType.DMA((13,))],
        compiler_params=pltpu.CompilerParams(vmem_limit_bytes=8 << 20),
        cost_estimate=pl.CostEstimate(flops=2 * 10**9, bytes_accessed=1, transcendentals=0),
    )(rows, *in_hbm(held), *in_hbm(weights))


def join_row(place, mine_ref, other_ref, row_ref):
    piece = mine_ref.shape[0]
    row_ref[rows_at(place * piece, piece), :] = mine_ref[...].astype(row_ref.dtype)
    row_ref[rows_at((1 - place) * piece, piece), :] = other_ref[...].astype(row_ref.dtype)


def attend_kernel(
    up_ref, down_ref, x_mine, x_other, small, wqkv, wo,
    up, down, n1, qkv, probs, mixed_low, middle, n2, sems,
):
    _, _, place = where_am_i()
    copies = [
        pltpu.make_async_copy(up_ref, up, sems.at[0]),
        pltpu.make_async_copy(down_ref, down, sems.at[1]),
    ]
    for copy in copies:
        copy.start()
    length, features = n1.shape
    groups = features // GW
    join_row(place, x_mine, x_other, middle)
    normal, _ = normalize(middle[...])
    n1[...] = (normal * small[0:1, :] + small[1:2, :]).astype(LOW)
    for which in range(3):
        value = dot_nn(n1[...], wqkv[:, which * features : (which + 1) * features])
        if which != 1:
            line = 2 + which // 2
            value = value + small[line : line + 1, :]
        value = value.astype(LOW)
        for group in range(groups):
            qkv[which * groups + group] = value[:, group * GW : (group + 1) * GW]
    allowed = lax.broadcasted_iota(jnp.int32, (length, length), 0) >= lax.broadcasted_iota(
        jnp.int32, (length, length), 1
    )

    def one_group(group, carry):
        query, keys, values = (qkv[which * groups + group] for which in range(3))
        scaled = query * HD**-0.5
        mixed = None
        for head in range(GROUP):
            mask = head_mask(head)
            scores = dot_nt(jnp.where(mask, scaled, 0), keys)
            scores = jnp.where(allowed, scores, NEGATIVE)
            powers = jnp.exp(scores - jnp.max(scores, axis=-1, keepdims=True))
            low = (powers * (1.0 / jnp.sum(powers, axis=-1, keepdims=True))).astype(LOW)
            probs[group * GROUP + head] = low
            part = dot_nn(low, values)
            mixed = part if head == 0 else jnp.where(mask, part, mixed)
        mixed_low[:, rows_at(group * GW, GW)] = mixed.astype(LOW)
        return carry

    lax.fori_loop(0, groups, one_group, 0)
    middle[...] += dot_nn(mixed_low[...], wo[...]) + small[4:5, :]
    normal, _ = normalize(middle[...])
    n2[...] = (normal * small[5:6, :] + small[6:7, :]).astype(LOW)
    for copy in copies:
        copy.wait()


def attend(x_mine, x_other, small, qkv_weight, out_weight, up_weight, down_weight):
    piece, features = x_other.shape
    length = 2 * piece
    groups = features // GW
    act = ((length, features), LOW)
    return call(
        "attend",
        attend_kernel,
        (x_mine, x_other, small, qkv_weight, out_weight),
        [
            act,
            ((3 * groups, length, GW), LOW),
            ((groups * GROUP, length, length), LOW),
            act,
            ((length, features), SINGLE),
            act,
        ],
        loaded=(up_weight, down_weight),
    )


def gelu_and_slope(u):
    c = math.sqrt(2 / math.pi)
    square = u * u
    bent = jnp.tanh(u * (c + (c * 0.044715) * square))
    half = 0.5 + 0.5 * bent
    slope = half + u * (0.5 - 0.5 * bent * bent) * (c + (3 * c * 0.044715) * square)
    return u * half, slope


def feed_tiles(side, n2, db2, small, up, down, g, du, vec, total):
    tiles, _, features = g.shape

    def one_tile(tile, carry):
        number = side * tiles + tile
        cut = rows_at(number * features, features)
        line = pl.ds(8 + number, 1)
        hidden = dot_nn(n2[...], up[:, cut]) + small[line, :]
        active, slope = gelu_and_slope(hidden)
        g[tile] = active.astype(LOW)
        grad = (dot_nt(db2[...], down[cut, :]) * slope).astype(LOW)
        du[tile] = grad
        vec[line, :] = jnp.sum(grad.astype(SINGLE), axis=0, keepdims=True)
        total[...] += dot_nt(grad, up[:, cut])
        return carry

    lax.fori_loop(0, tiles, one_tile, 0)


def feed_one_kernel(
    n2, c_mine, c_other, small, count, up, down, g, du, db2, theirs, dn, vec,
):
    core, _, place = where_am_i()
    half = theirs.shape[1]
    join_row(place, c_mine, c_other, db2)
    theirs[...] = db2[:, rows_at((1 - core) * half, half)]
    vec[...] = jnp.zeros_like(vec)
    vec[7:8, :] = jnp.sum(db2[...].astype(SINGLE), axis=0, keepdims=True)
    vec[12:13, 0:128] = count[...]
    dn[...] = jnp.zeros_like(dn)
    feed_tiles(1 - core, n2, db2, small, up, down, g, du, vec, dn)


def feed_one(n2, c_mine, c_other, small, count, up, down):
    length, features = n2.shape
    tiles = up.shape[1] // 2 // features
    hid = ((tiles, length, features), LOW)
    return call(
        "feed_one",
        feed_one_kernel,
        (n2, c_mine, c_other, small, count, up, down),
        [
            hid, hid, ((length, features), LOW), ((length, features // 2), LOW),
            ((length, features), SINGLE), ((16, features), SINGLE),
        ],
    )


def feed_two_kernel(
    n2, db2, small, up, down, middle, dn, vec_in, g, du, dm, db1, theirs, vec,
):
    core, _, _ = where_am_i()
    half = theirs.shape[1]
    vec[...] = vec_in[...]
    dm[...] = dn[...]
    feed_tiles(core, n2, db2, small, up, down, g, du, vec, dm)
    grad_n = dm[...]
    normal, inverse = normalize(middle[...])
    vec[5:6, :] = jnp.sum(grad_n * normal, axis=0, keepdims=True)
    vec[6:7, :] = jnp.sum(grad_n, axis=0, keepdims=True)
    grad = db2[...].astype(SINGLE) + norm_back(normal, inverse, grad_n, small[5:6, :])
    dm[...] = grad
    low = grad.astype(LOW)
    db1[...] = low
    theirs[...] = db1[:, rows_at((1 - core) * half, half)]
    vec[4:5, :] = jnp.sum(low.astype(SINGLE), axis=0, keepdims=True)


def feed_two(n2, db2, small, up, down, middle, dn, vec_in):
    length, features = n2.shape
    tiles = up.shape[1] // 2 // features
    hid = ((tiles, length, features), LOW)
    return call(
        "feed_two",
        feed_two_kernel,
        (n2, db2, small, up, down, middle, dn, vec_in),
        [
            hid, hid, ((length, features), SINGLE), ((length, features), LOW),
            ((length, features // 2), LOW), ((16, features), SINGLE),
        ],
    )


def result_kernel(g_mine, g_theirs, middle, small, down, y_mine, y_send, total):
    core, _, place = where_am_i()
    tiles, _, features = g_mine.shape
    piece = y_mine.shape[0]
    total[...] = middle[...] + small[7:8, :]

    def one_tile(tile, carry):
        for side, active in ((core, g_mine), (1 - core, g_theirs)):
            cut = rows_at((side * tiles + tile) * features, features)
            total[...] += dot_nn(active[tile], down[cut, :])
        return carry

    lax.fori_loop(0, tiles, one_tile, 0)
    present = small[12:13, :]
    y_mine[...] = (total[rows_at(place * piece, piece), :] * present).astype(LOW)
    y_send[...] = (total[rows_at((1 - place) * piece, piece), :] * present).astype(LOW)


def result(g_mine, g_theirs, middle, small, down):
    length, features = middle.shape
    part = ((length // 2, features), LOW)
    return call(
        "result",
        result_kernel,
        (g_mine, g_theirs, middle, small, down),
        [part, part],
        [((length, features), SINGLE)],
    )


def back_kernel(qkv, probs, db1, wo, vec_in, theirs, mine, vec, dp):
    core, _, _ = where_am_i()
    features = db1.shape[1]
    groups = features // GW
    vec[...] = vec_in[...]

    def one_group(group, carry):
        cut = rows_at(group * GW, GW)
        grad_mixed = dot_nt(db1[...], wo[cut, :]).astype(LOW)
        query, keys, values = (qkv[which * groups + group] for which in range(3))
        query = query * HD**-0.5
        keys = keys * HD**-0.5
        dq = dk = dv = None
        for head in range(GROUP):
            mask = head_mask(head)
            grad_head = jnp.where(mask, grad_mixed, 0)
            probs_low = probs[group * GROUP + head]
            weights = probs_low.astype(SINGLE)
            grad_probs = dot_nt(grad_head, values)
            inner = jnp.sum(weights * grad_probs, axis=-1, keepdims=True)
            grad_scores = (weights * (grad_probs - inner)).astype(LOW)
            part = dot_nn(grad_scores, keys)
            dq = part if head == 0 else jnp.where(mask, part, dq)
            part = dot_tn(grad_scores, query)
            dk = part if head == 0 else jnp.where(mask, part, dk)
            part = dot_tn(probs_low, grad_mixed)
            dv = part if head == 0 else jnp.where(mask, part, dv)
        for which, value in enumerate((dq, dk, dv)):
            low = value.astype(LOW)
            dp[:, rows_at(which * features + group * GW, GW)] = low
            if which != 1:
                line = 2 + which // 2
                vec[line : line + 1, cut] = jnp.sum(low.astype(SINGLE), axis=0, keepdims=True)
        return carry

    lax.fori_loop(0, groups, one_group, 0)
    half = mine.shape[1]
    theirs[...] = dp[:, rows_at((1 - core) * half, half)]
    mine[...] = dp[:, rows_at(core * half, half)]


def back(qkv, probs, db1, out_weight, vec_in):
    length, features = db1.shape
    half = ((length, 3 * features // 2), LOW)
    return call(
        "back",
        back_kernel,
        (qkv, probs, db1, out_weight, vec_in),
        [half, half, ((16, features), SINGLE)],
        [((length, 3 * features), LOW)],
    )


def input_kernel(
    x_mine, x_other, small, dp_mine, dp_theirs, wqkv, dm, vec_in, mine, send, vec, row,
):
    core, _, place = where_am_i()
    half = dp_mine.shape[1]
    piece = mine.shape[0]
    grad_n = dot_nt(dp_mine[...], wqkv[:, rows_at(core * half, half)])
    grad_n = grad_n + dot_nt(dp_theirs[...], wqkv[:, rows_at((1 - core) * half, half)])
    join_row(place, x_mine, x_other, row)
    normal, inverse = normalize(row[...])
    vec[...] = vec_in[...]
    vec[0:1, :] = jnp.sum(grad_n * normal, axis=0, keepdims=True)
    vec[1:2, :] = jnp.sum(grad_n, axis=0, keepdims=True)
    row[...] = dm[...] + norm_back(normal, inverse, grad_n, small[0:1, :])
    mine[...] = row[rows_at(place * piece, piece), :].astype(LOW)
    send[...] = row[rows_at((1 - place) * piece, piece), :].astype(LOW)


def input_gradient(x_mine, x_other, small, dp_mine, dp_theirs, qkv_weight, dm, vec_in):
    piece, features = x_other.shape
    part = ((piece, features), LOW)
    return call(
        "input",
        input_kernel,
        (x_mine, x_other, small, dp_mine, dp_theirs, qkv_weight, dm, vec_in),
        [part, part, ((16, features), SINGLE)],
        [((2 * piece, features), SINGLE)],
    )


UNITS = 16


def unit_of(name, number):
    core, own, place = where_am_i()
    units = []
    for order in WAYS[name]:
        unit = 0
        for stage, axis in enumerate(order):
            if number >> (3 - stage) & 1:
                unit |= 1 if axis == "x" else BITS[axis] << 1
        units.append(unit)
    return jnp.where(core == 0, units[0], units[1]) ^ (own * 2 + place)


def lanes_kernel(
    g_mine, g_theirs, other_mine, other_theirs, right, right_other, send, keep, turned, whole, *, name
):
    core, _, _ = where_am_i()
    chunks, tall, wide = whole.shape
    tiles, length, features = g_mine.shape
    per_tile = features // wide
    half = tall // 2
    turned[:, :length] = right[:, rows_at(core * tall, tall)].T
    turned[:, length:] = right_other[...].T
    for side, one, two in ((core, g_mine, other_theirs), (1 - core, g_theirs, other_mine)):

        def one_tile(tile, carry, side=side, one=one, two=two):
            total = dot_nn(turned[:, :length], one[tile]) + dot_nn(turned[:, length:], two[tile])
            total = total.astype(LOW)
            for chunk in range(per_tile):
                whole[(side * tiles + tile) * per_tile + chunk] = total[:, chunk * wide : (chunk + 1) * wide]
            return carry

        lax.fori_loop(0, tiles, one_tile, 0)
    for number in range(UNITS):
        unit = unit_of(name, number)
        out = send if number >= UNITS // 2 else keep
        out[number % (UNITS // 2)] = whole[lax.div(unit, 2), rows_at(lax.rem(unit, 2) * half, half), :]


def grad_lanes(name, mine, theirs, other_mine, other_theirs, right, right_other):
    tiles, length, features = mine.shape
    tall = right_other.shape[1]
    chunks = UNITS // 2
    wide = 2 * tiles * features // chunks
    unit = ((UNITS // 2, tall // 2, wide), LOW)
    return call(
        "lanes",
        functools.partial(lanes_kernel, name=name),
        (mine, theirs, other_mine, other_theirs, right, right_other),
        [unit, unit],
        [((tall, 2 * length), LOW), ((chunks, tall, wide), LOW)],
    )


def rows_kernel(left, left_other, right, right_other, *rest, name, pick_core):
    if len(rest) > 4:
        vec, vec_other, send, keep, turned, whole, spread = rest
    else:
        send, keep, turned, whole = rest
        vec = None
    core, _, _ = where_am_i()
    length = left.shape[0]
    split = len(right_other.shape) == 2
    tiles, tile = (1, right_other.shape[1]) if split else (right_other.shape[0], right_other.shape[2])
    turned[:, :length] = left[...].T
    turned[:, length:] = left_other[...].T
    rows = turned.shape[0] // UNITS
    units = [unit_of(name, number) for number in range(UNITS)]
    if vec is not None:
        total = vec[...] + vec_other[...]
        features = total.shape[1]
        part = 2 * rows
        spread[...] = jnp.zeros_like(spread)
        for chunk in range(UNITS // 2):
            spread[2 * chunk, 0:8, :part] = total[0:8, chunk * part : (chunk + 1) * part]
            for piece in range(4):
                line, begin = divmod((4 * chunk + piece) * part, features)
                spread[2 * chunk + 1, piece : piece + 1, :part] = total[
                    8 + line : 9 + line, begin : begin + part
                ]
            spread[2 * chunk + 1, 4:5, : 2 * DIGITS] = total[12:13, : 2 * DIGITS]
        for out in (send, keep):
            out[:, rows:, :] = jnp.zeros_like(out[:, rows:, :])

    def one_tile(step, carry):
        if split:
            here = right[:, rows_at(core * tile, tile)] if pick_core else right[...]
            there = right_other[...]
        else:
            here, there = right[step], right_other[step]
        whole[...] = (dot_nn(turned[:, :length], here) + dot_nn(turned[:, length:], there)).astype(LOW)
        columns = rows_at(step * tile, tile)
        for number, unit in enumerate(units):
            out = send if number >= UNITS // 2 else keep
            out[number % (UNITS // 2), :rows, columns] = whole[rows_at(unit * rows, rows), :]
        return carry

    if tiles == 1:
        one_tile(0, 0)
    else:
        lax.fori_loop(0, tiles, one_tile, 0)
    if vec is not None:
        for number, unit in enumerate(units):
            out = send if number >= UNITS // 2 else keep
            out[number % (UNITS // 2), rows:, :128] = spread[unit].astype(LOW)


def grad_rows(name, left, left_other, right, right_other, pick_core=False, vecs=()):
    length, tall = left.shape
    rows = tall // UNITS
    tile = right_other.shape[-1]
    width = math.prod(right_other.shape) // length
    unit = ((UNITS // 2, rows + (16 if vecs else 0), width), LOW)
    return call(
        "rows",
        functools.partial(rows_kernel, name=name, pick_core=pick_core),
        (left, left_other, right, right_other, *vecs),
        [unit, unit],
        [((tall, 2 * length), LOW), ((tall, tile), LOW)] + [((UNITS, 16, 128), SINGLE)] * bool(vecs),
    )


def close_kernel(mine, other, *outs):
    vec = outs[-1]
    counts, whole, up, qv = outs[:4]
    plain = outs[4:-1]
    _, _, place = where_am_i()
    rows = mine.shape[0] - 16
    vec[rows_at(place * 8, 8), :] = mine[rows:, :128].astype(SINGLE)[:8]
    vec[rows_at((1 - place) * 8, 8), :] = other[rows:, :128].astype(SINGLE)[:8]
    line = vec[12:13, :]
    lane = lax.broadcasted_iota(jnp.int32, line.shape, 1)
    worth = lax.shift_left(jnp.ones_like(lane), lax.rem(lane, DIGITS)).astype(SINGLE)
    first, second = (
        jnp.sum(jnp.where(lane // DIGITS == half, line * worth, 0.0), axis=1, keepdims=True)
        for half in (0, 1)
    )
    total = first + second
    spot = lax.broadcasted_iota(jnp.int32, (1, 128), 1)
    both = jnp.where(spot == 0, first, second).astype(jnp.int32)
    counts[...] = both[0, :2]
    whole[...] = jnp.broadcast_to(total, whole.shape)
    width = qv.shape[1]
    scaled = vec[...] / total
    qv[...] = scaled[2:4, :width]
    for number, out in zip((0, 1, 4, 5, 6, 7), plain):
        out[...] = scaled[number, :width]
    up[...] = jnp.concatenate([scaled[8 + part : 9 + part, :width] for part in range(4)], axis=1)[0]


def close(mine, other, width):
    return call(
        "result",
        close_kernel,
        (mine, other),
        [((2,), jnp.int32), ((8, 128), SINGLE), ((4 * width,), SINGLE), ((2, width), SINGLE)]
        + [((width,), SINGLE)] * 6,
        [((16, 128), SINGLE)],
    )


def finish_kernel(whole, *refs, rows, turned):
    parts, out = refs[:4], refs[4]
    core, _, place = where_am_i()
    total = whole[0:1, 0:1]
    for number, part in enumerate(parts):
        side, half = core ^ (number >> 1), place ^ (number & 1)
        if turned:
            refs[5][rows_at((side * 2 + half) * rows, rows), :] = part[...].astype(SINGLE)
        else:
            width = part.shape[1]
            out[rows_at(half * rows, rows), rows_at(side * width, width)] = (
                part[:rows, :].astype(SINGLE) / total
            )
    if turned:
        out[...] = refs[5][...].T / total


def finish(whole, parts, rows, turned=False):
    width = parts[0].shape[1]
    shape = (width, 4 * rows) if turned else (2 * rows, 2 * width)
    return call(
        "result",
        functools.partial(finish_kernel, rows=rows, turned=turned),
        (whole, *parts),
        [(shape, SINGLE)],
        [((4 * rows, width), SINGLE)] * turned,
    )[0]


def swap_pairs(size, bit):
    return [(i, i ^ bit) for i in range(size)]


def partners(name, stage, groups):
    pairs = []
    for core in range(2):
        axis = WAYS[name][core][stage]
        for own in range(groups):
            for place in range(2):
                to = (own, place ^ 1) if axis == "x" else (own ^ BITS[axis], place)
                pairs.append(((core * groups + own) * 2 + place, (core * groups + to[0]) * 2 + to[1]))
    return pairs


def added(one, two):
    return (one.astype(SINGLE) + two.astype(SINGLE)).astype(LOW)


class Order:
    def __init__(self):
        self.last = None

    def tie(self, value):
        if self.last is not None:
            value, _ = lax.optimization_barrier((value, self.last))
        return value

    def mark(self, value):
        self.last = value


class Sum:
    def __init__(self, order, name, groups, send, keep):
        self.order, self.name, self.groups = order, name, groups
        self.keep = keep
        self.stage = 0
        self.go(send)

    def go(self, send):
        self.flying = lax.ppermute(send, AXES, partners(self.name, self.stage, self.groups))

    def step(self):
        other = self.order.tie(self.flying)
        keep = self.keep
        self.stage += 1
        pair = swap_pairs(2, 1)
        if self.stage == 5:
            self.order.mark(other)
            self.parts = [self.total, other, self.across, lax.ppermute(other, "src", pair)]
            return
        if self.stage == 4:
            self.total = added(keep[0], other[0])
            self.order.mark(self.total)
            self.flying = lax.ppermute(self.total, "seq", pair)
            self.across = lax.ppermute(self.total, "src", pair)
            return
        half = keep.shape[0] // 2
        send = added(keep[half:], other[half:])
        self.keep = added(keep[:half], other[:half])
        self.order.mark(send)
        self.go(send)


def body_fast(
    inputs,
    cotangent,
    row_counts,
    response_mask,
    norm1_gain,
    norm1_bias,
    qkv_weight,
    qv_bias,
    out_weight,
    out_bias,
    norm2_gain,
    norm2_bias,
    up_weight,
    up_bias,
    down_weight,
    down_bias,
):
    groups = lax.axis_size("dp")
    pair = swap_pairs(2, 1)
    core, own, place = (lax.axis_index(a) for a in ("src", "dp", "seq"))
    x_both = inputs[0, 0]
    x_other = lax.ppermute(
        lax.dynamic_index_in_dim(x_both, 1 - place, 0, keepdims=False), "seq", pair
    )
    x_mine, c_send, c_mine, count, small, qkv_weight, out_weight = prepare(
        row_counts,
        response_mask[0, 0],
        x_both,
        cotangent[0, 0],
        (norm1_gain, norm1_bias, qv_bias, out_bias, norm2_gain, norm2_bias, down_bias, up_bias),
        (qkv_weight, out_weight),
    )
    c_other = lax.ppermute(c_send, "seq", pair)
    order = Order()

    def from_core(value):
        return lax.ppermute(value, "src", pair)

    up_weight, down_weight, n1, qkv, probs, mixed, middle, n2 = attend(
        x_mine, x_other, small, qkv_weight, out_weight, up_weight, down_weight
    )
    g_theirs, du_theirs, db2, db2_theirs, dn, vec = feed_one(
        n2, c_mine, c_other, small, count, up_weight, down_weight
    )
    order.mark(vec)
    n2_other = order.tie(from_core(n2))
    order.mark(n2_other)
    g_mine, du_mine, dm, db1, db1_theirs, vec = feed_two(
        order.tie(n2), db2, small, up_weight, down_weight, middle, dn, vec
    )
    order.mark(vec)
    du_other = from_core(du_theirs)
    other_theirs, other_mine = from_core(g_theirs), from_core(g_mine)
    db2_other = from_core(db2_theirs)
    n1_other, mixed_other, db1_other = from_core(n1), from_core(mixed), from_core(db1_theirs)

    sums = {}
    done = {}
    rows = out_weight.shape[0] // groups

    def rows_home(mine, send):
        other = order.tie(lax.ppermute(send, "seq", pair))
        both = jnp.where(place == 0, jnp.stack([mine, other]), jnp.stack([other, mine]))
        order.mark(both)
        return both[None, None]

    def finished(name):
        parts = sums[name].parts
        parts[3] = order.tie(parts[3])
        turned = name == "d"
        shard = finish(done["whole"], parts, 2 * rows if turned else rows // 2, turned)
        order.mark(shard)
        return shard

    for event in EVENTS:
        if event == "y":
            done["output"] = rows_home(y_mine, y_send)
            continue
        if event == "i":
            done["input_grad"] = rows_home(x_grad_mine, x_grad_send)
            continue
        if event.islower():
            if event in sums and sums[event].stage < 5:
                sums[event].step()
                if event == "o" and sums[event].stage == 5:
                    counts, done["whole"], up_small, qv, *plain = close(*sums["o"].parts[:2], rows)
                    order.mark(done["whole"])
            else:
                done[event] = finished(event)
            continue
        name = event.lower()
        if event == "U":
            parts = grad_rows(name, order.tie(n2), n2_other, du_mine, du_other)
        elif event == "D":
            parts = grad_lanes(
                name, order.tie(g_mine), g_theirs, other_mine, other_theirs, db2, db2_other
            )
        elif event == "C":
            n1_other, mixed_other, db1_other = order.tie((n1_other, mixed_other, db1_other))
            here, n1_other, mixed_other, db1_other = lax.optimization_barrier(
                (qkv, n1_other, mixed_other, db1_other)
            )
            dp_theirs, dp_mine, vec = back(here, probs, db1, out_weight, vec)
            dp_other = from_core(dp_theirs)
            order.mark(vec)
            continue
        elif event == "I":
            x_grad_mine, x_grad_send, vec = input_gradient(
                order.tie(x_mine), x_other, small, dp_mine, dp_theirs, qkv_weight, dm, vec
            )
            vec_other = from_core(vec)
            order.mark(vec)
            continue
        elif event == "Y":
            y_mine, y_send = result(order.tie(g_mine), g_theirs, middle, small, down_weight)
            order.mark(y_send)
            continue
        elif event == "O":
            parts = grad_rows(
                name, order.tie(mixed), mixed_other, db1, db1_other, True, (vec, vec_other)
            )
        else:
            parts = grad_rows(name, order.tie(n1), n1_other, dp_mine, dp_other)
        order.mark(parts[0])
        sums[name] = Sum(order, name, groups, *parts)

    return (
        done["output"],
        done["input_grad"],
        counts,
        plain[0],
        plain[1],
        done["q"],
        qv,
        done["o"],
        plain[2],
        plain[3],
        plain[4],
        done["u"],
        up_small,
        done["d"],
        plain[5],
    )


def solution(mesh):
    placed = (
        P("src", "dp", None, "seq", None),
        P("src", "dp", None, "seq", None),
        P("src", "dp"),
        P("src", "dp", None, "seq"),
        P(),
        P(),
        P(),
        P(),
        P(),
        P(),
        P(),
        P(),
        P(),
        P(),
        P(),
        P(),
    )
    sizes = dict(mesh.shape)
    paired = sizes["src"] == 2 and sizes["seq"] == 2 and sizes["dp"] == 8
    return jax.shard_map(
        body_fast if paired else body_generic,
        mesh=mesh,
        in_specs=placed,
        out_specs=(
            P("src", "dp", None, "seq", None),
            P("src", "dp", None, "seq", None),
            P(),
            P("dp"),
            P("dp"),
            P("dp", None),
            P(None, "dp"),
            P("dp", None),
            P("dp"),
            P("dp"),
            P("dp"),
            P("dp", None),
            P("dp"),
            P("dp", None),
            P("dp"),
        ),
        check_vma=False,
    )
```

```python
import functools
import math

import jax
import jax.numpy as jnp
from jax import lax
from jax.experimental import pallas as pl
from jax.experimental.pallas import tpu as pltpu
from jax.sharding import PartitionSpec as P

H = 12
HD = 64


EPS = 1e-05
NEGATIVE = -1e30


def norm_apply(values, scaling, offset):
    centre = jnp.mean(values, axis=-1, keepdims=True)
    centered = values - centre
    spread = jnp.mean(centered * centered, axis=-1, keepdims=True)
    return centered * lax.rsqrt(spread + EPS) * scaling + offset


def causal_scores(query_part, keys_part, allowed):
    scores = jnp.einsum(
        "rqhd,rkhd->rhqk", query_part, keys_part, preferred_element_type=jnp.float32
    )
    scores = scores * HD ** (-0.5)
    return jnp.where(allowed, scores, NEGATIVE)


def attend_forward(query_part, keys_part, values_part, allowed):
    scores = causal_scores(query_part, keys_part, allowed)
    highest = jnp.max(scores, axis=-1, keepdims=True)
    powers = jnp.exp(scores - highest)
    totals = jnp.sum(powers, axis=-1, keepdims=True)
    probs_low = (powers / totals).astype(jnp.bfloat16)
    mixed = jnp.einsum(
        "rhqk,rkhd->rqhd", probs_low, values_part, preferred_element_type=jnp.float32
    )
    return (mixed, highest, totals)


def attend_backward(query_part, keys_part, values_part, grad_part, highest, totals, allowed):
    scores = causal_scores(query_part, keys_part, allowed)
    probs = jnp.exp(scores - highest) / totals
    probs_low = probs.astype(jnp.bfloat16)
    grad_probs = jnp.einsum(
        "rqhd,rkhd->rhqk", grad_part, values_part, preferred_element_type=jnp.float32
    )
    inner = jnp.sum(probs * grad_probs, axis=-1, keepdims=True)
    grad_scores = (probs * (grad_probs - inner)).astype(jnp.bfloat16)
    factor = HD ** (-0.5)
    grad_query = (
        jnp.einsum("rhqk,rkhd->rqhd", grad_scores, keys_part, preferred_element_type=jnp.float32)
        * factor
    )
    grad_keys = (
        jnp.einsum("rhqk,rqhd->rkhd", grad_scores, query_part, preferred_element_type=jnp.float32)
        * factor
    )
    grad_values = jnp.einsum(
        "rhqk,rqhd->rkhd", probs_low, grad_part, preferred_element_type=jnp.float32
    )
    return (grad_query, grad_keys, grad_values)


def body_generic(
    inputs,
    cotangent,
    row_counts,
    response_mask,
    norm1_gain,
    norm1_bias,
    qkv_weight,
    qv_bias,
    out_weight,
    out_bias,
    norm2_gain,
    norm2_bias,
    up_weight,
    up_bias,
    down_weight,
    down_bias,
):
    slots = inputs.shape[2]
    piece_len = inputs.shape[3]
    features = inputs.shape[4]
    tokens = slots * piece_len
    blocks_seq = lax.axis_size("seq")
    row_len = piece_len * blocks_seq
    group_heads = math.gcd(H, 4)
    bfloat = jnp.bfloat16
    single = jnp.float32
    present_int = (jnp.arange(slots) < row_counts[0, 0]).astype(jnp.int32)
    weight = (response_mask[0, 0] * present_int[:, None]).astype(single)
    local_count = jnp.sum(response_mask[0, 0] * present_int[:, None])
    picked = jnp.where(jnp.arange(lax.axis_size("src")) == lax.axis_index("src"), local_count, 0)
    source_counts = lax.psum(picked, ("src", "dp", "seq"))
    whole = jnp.sum(source_counts).astype(single)
    source = inputs.reshape(tokens, features).astype(single)
    normed, norm1_pull = jax.vjp(
        norm_apply, source, norm1_gain.astype(single), norm1_bias.astype(single)
    )
    normed_low = normed.astype(bfloat)
    bias_query = qv_bias[0].astype(single)
    joined = jnp.concatenate([bias_query, jnp.zeros_like(bias_query), qv_bias[1].astype(single)])
    projected = jnp.dot(normed_low, qkv_weight, preferred_element_type=single) + joined
    proj_low = projected.astype(bfloat)
    query = proj_low[:, :features].reshape(slots, piece_len, H, HD)
    keys_own = proj_low[:, features : 2 * features].reshape(slots, piece_len, features)
    values_own = proj_low[:, 2 * features :].reshape(slots, piece_len, features)
    keys_all, values_all = (
        lax.all_gather(keys_own, "seq", axis=1, tiled=True),
        lax.all_gather(values_own, "seq", axis=1, tiled=True),
    )
    query_pos = lax.axis_index("seq") * piece_len + jnp.arange(piece_len)
    allowed = query_pos[:, None] >= jnp.arange(row_len)[None, :]
    keys_heads = keys_all.reshape(slots, row_len, H, HD)
    values_heads = values_all.reshape(slots, row_len, H, HD)
    mixed_parts = []
    kept_stats = []
    for group in range(H // group_heads):
        first = group * group_heads
        last = first + group_heads
        mixed, highest, totals = attend_forward(
            query[:, :, first:last],
            keys_heads[:, :, first:last],
            values_heads[:, :, first:last],
            allowed,
        )
        mixed_parts.append(mixed)
        kept_stats.append((highest, totals))
    attended = jnp.concatenate(mixed_parts, axis=2).reshape(tokens, features)
    attended_low = attended.astype(bfloat)
    branch = jnp.dot(attended_low, out_weight, preferred_element_type=single) + out_bias.astype(
        single
    )
    middle = source + branch
    normed_two, norm2_pull = jax.vjp(
        norm_apply, middle, norm2_gain.astype(single), norm2_bias.astype(single)
    )
    normed_two_low = normed_two.astype(bfloat)
    hidden = jnp.dot(normed_two_low, up_weight, preferred_element_type=single) + up_bias.astype(
        single
    )
    active, gelu_pull = jax.vjp(functools.partial(jax.nn.gelu, approximate=True), hidden)
    active_low = active.astype(bfloat)
    branch_two = jnp.dot(active_low, down_weight, preferred_element_type=single) + down_bias.astype(
        single
    )
    result = middle + branch_two
    present_tok = jnp.repeat(present_int.astype(single), piece_len)
    output = (result * present_tok[:, None]).astype(bfloat).reshape(inputs.shape)
    incoming = cotangent.reshape(tokens, features).astype(single) * weight.reshape(tokens)[:, None]
    grad_branch_two = incoming.astype(bfloat)
    grad_down_weight = jnp.einsum(
        "tf,td->fd", active_low, grad_branch_two, preferred_element_type=single
    )
    grad_down_bias = jnp.sum(grad_branch_two.astype(single), axis=0)
    grad_active = jnp.einsum(
        "td,fd->tf", grad_branch_two, down_weight, preferred_element_type=single
    )
    grad_hidden = gelu_pull(grad_active)[0].astype(bfloat)
    grad_up_weight = jnp.einsum(
        "tm,tf->mf", normed_two_low, grad_hidden, preferred_element_type=single
    )
    grad_up_bias = jnp.sum(grad_hidden.astype(single), axis=0)
    grad_normed_two = jnp.einsum("tf,mf->tm", grad_hidden, up_weight, preferred_element_type=single)
    grad_mid_norm, grad_norm2_gain, grad_norm2_bias = norm2_pull(grad_normed_two)
    grad_middle = incoming + grad_mid_norm
    grad_branch = grad_middle.astype(bfloat)
    grad_out_weight = jnp.einsum(
        "tm,td->md", attended_low, grad_branch, preferred_element_type=single
    )
    grad_out_bias = jnp.sum(grad_branch.astype(single), axis=0)
    grad_attended = jnp.einsum("td,md->tm", grad_branch, out_weight, preferred_element_type=single)
    grad_heads = grad_attended.astype(bfloat).reshape(slots, piece_len, H, HD)
    query_grads = []
    key_grads = []
    value_grads = []
    for group in range(H // group_heads):
        first = group * group_heads
        last = first + group_heads
        highest, totals = kept_stats[group]
        grad_query, grad_keys, grad_values = attend_backward(
            query[:, :, first:last],
            keys_heads[:, :, first:last],
            values_heads[:, :, first:last],
            grad_heads[:, :, first:last],
            highest,
            totals,
            allowed,
        )
        query_grads.append(grad_query)
        key_grads.append(grad_keys)
        value_grads.append(grad_values)
    grad_query_all = jnp.concatenate(query_grads, axis=2).reshape(tokens, features)
    grad_keys_all = jnp.concatenate(key_grads, axis=2).reshape(slots, row_len, features)
    grad_values_all = jnp.concatenate(value_grads, axis=2).reshape(slots, row_len, features)
    grad_keys_own, grad_values_own = (
        lax.psum_scatter(
            grad_keys_all.astype(jnp.bfloat16), "seq", scatter_dimension=1, tiled=True
        ).astype(jnp.float32),
        lax.psum_scatter(
            grad_values_all.astype(jnp.bfloat16), "seq", scatter_dimension=1, tiled=True
        ).astype(jnp.float32),
    )
    grad_projected = jnp.concatenate(
        [
            grad_query_all,
            grad_keys_own.reshape(tokens, features),
            grad_values_own.reshape(tokens, features),
        ],
        axis=1,
    ).astype(bfloat)
    grad_qkv_weight = jnp.einsum(
        "tm,tn->mn", normed_low, grad_projected, preferred_element_type=single
    )
    column_sums = jnp.sum(grad_projected.astype(single), axis=0)
    grad_qv_bias = jnp.stack([column_sums[:features], column_sums[2 * features :]])
    grad_normed = jnp.einsum("tn,mn->tm", grad_projected, qkv_weight, preferred_element_type=single)
    grad_src_norm, grad_norm1_gain, grad_norm1_bias = norm1_pull(grad_normed)
    input_grad = (grad_middle + grad_src_norm).astype(bfloat).reshape(inputs.shape)
    grads = (
        grad_norm1_gain,
        grad_norm1_bias,
        grad_qkv_weight,
        grad_qv_bias,
        grad_out_weight,
        grad_out_bias,
        grad_norm2_gain,
        grad_norm2_bias,
        grad_up_weight,
        grad_up_bias,
        grad_down_weight,
        grad_down_bias,
    )
    summed = (
        lax.psum_scatter(
            grads[0].astype(jnp.bfloat16), "dp", scatter_dimension=0, tiled=True
        ).astype(jnp.float32),
        lax.psum_scatter(
            grads[1].astype(jnp.bfloat16), "dp", scatter_dimension=0, tiled=True
        ).astype(jnp.float32),
        lax.psum_scatter(
            grads[2].astype(jnp.bfloat16), "dp", scatter_dimension=0, tiled=True
        ).astype(jnp.float32),
        lax.psum_scatter(
            grads[3].astype(jnp.bfloat16), "dp", scatter_dimension=1, tiled=True
        ).astype(jnp.float32),
        lax.psum_scatter(
            grads[4].astype(jnp.bfloat16), "dp", scatter_dimension=0, tiled=True
        ).astype(jnp.float32),
        lax.psum_scatter(
            grads[5].astype(jnp.bfloat16), "dp", scatter_dimension=0, tiled=True
        ).astype(jnp.float32),
        lax.psum_scatter(
            grads[6].astype(jnp.bfloat16), "dp", scatter_dimension=0, tiled=True
        ).astype(jnp.float32),
        lax.psum_scatter(
            grads[7].astype(jnp.bfloat16), "dp", scatter_dimension=0, tiled=True
        ).astype(jnp.float32),
        lax.psum_scatter(
            grads[8].astype(jnp.bfloat16), "dp", scatter_dimension=0, tiled=True
        ).astype(jnp.float32),
        lax.psum_scatter(
            grads[9].astype(jnp.bfloat16), "dp", scatter_dimension=0, tiled=True
        ).astype(jnp.float32),
        lax.psum_scatter(
            grads[10].astype(jnp.bfloat16), "dp", scatter_dimension=0, tiled=True
        ).astype(jnp.float32),
        lax.psum_scatter(
            grads[11].astype(jnp.bfloat16), "dp", scatter_dimension=0, tiled=True
        ).astype(jnp.float32),
    )
    summed = (
        lax.psum(summed[0].astype(jnp.bfloat16), ("src", "seq")).astype(jnp.float32),
        lax.psum(summed[1].astype(jnp.bfloat16), ("src", "seq")).astype(jnp.float32),
        lax.psum(summed[2].astype(jnp.bfloat16), ("src", "seq")).astype(jnp.float32),
        lax.psum(summed[3].astype(jnp.bfloat16), ("src", "seq")).astype(jnp.float32),
        lax.psum(summed[4].astype(jnp.bfloat16), ("src", "seq")).astype(jnp.float32),
        lax.psum(summed[5].astype(jnp.bfloat16), ("src", "seq")).astype(jnp.float32),
        lax.psum(summed[6].astype(jnp.bfloat16), ("src", "seq")).astype(jnp.float32),
        lax.psum(summed[7].astype(jnp.bfloat16), ("src", "seq")).astype(jnp.float32),
        lax.psum(summed[8].astype(jnp.bfloat16), ("src", "seq")).astype(jnp.float32),
        lax.psum(summed[9].astype(jnp.bfloat16), ("src", "seq")).astype(jnp.float32),
        lax.psum(summed[10].astype(jnp.bfloat16), ("src", "seq")).astype(jnp.float32),
        lax.psum(summed[11].astype(jnp.bfloat16), ("src", "seq")).astype(jnp.float32),
    )
    final = [g / whole for g in summed]
    return (
        output,
        input_grad,
        source_counts,
        final[0],
        final[1],
        final[2],
        final[3],
        final[4],
        final[5],
        final[6],
        final[7],
        final[8],
        final[9],
        final[10],
        final[11],
    )


WAYS = {
    "u": ("x12y", "yx12"),
    "d": ("y1x2", "12yx"),
    "o": ("xy12", "1xy2"),
    "q": ("yx12", "xy12"),
}
EVENTS = "UDCIOQudoqudoqYudoqiudoqyudoq+"
BITS = {"y": 1, "1": 2, "2": 4}


COSTS = {"prepare": 2, "load": 4, "attend": 8, "feed_one": 5, "feed_two": 5, "back": 0, "input": 0, "lanes": 0, "rows_u": 4, "rows_q": 0, "rows_o": 0, "result": 0}
AXES = ("src", "dp", "seq")
SINGLE = jnp.float32
LOW = jnp.bfloat16
GROUP = 4
GW = GROUP * HD
DIGITS = 16


def dot_nt(left, right):
    return lax.dot_general(left, right, (((1,), (1,)), ((), ())), preferred_element_type=SINGLE)


def dot_tn(left, right):
    return lax.dot_general(left, right, (((0,), (0,)), ((), ())), preferred_element_type=SINGLE)


def dot_nn(left, right):
    return jnp.dot(left, right, preferred_element_type=SINGLE)


def normalize(values):
    centered = values - jnp.mean(values, axis=-1, keepdims=True)
    inverse = lax.rsqrt(jnp.mean(centered * centered, axis=-1, keepdims=True) + EPS)
    return centered * inverse, inverse


def norm_back(normal, inverse, grad, gain):
    scaled = grad * gain
    return inverse * (
        scaled
        - jnp.mean(scaled, axis=-1, keepdims=True)
        - normal * jnp.mean(scaled * normal, axis=-1, keepdims=True)
    )


def spread_heads(value, out, scale=1.0):
    length = value.shape[0]
    lanes = lax.broadcasted_iota(jnp.int32, (1, GW), 1)
    for head in range(GROUP):
        keep = jnp.where((lanes >= head * HD) & (lanes < (head + 1) * HD), scale, 0.0).astype(LOW)
        out[head * length : (head + 1) * length, :] = value * keep


def side_by_side(stacked, out):
    length = out.shape[0]
    for head in range(GROUP):
        out[:, head * length : (head + 1) * length] = stacked[head * length : (head + 1) * length, :]


def rows_at(first, count):
    return pl.ds(pl.multiple_of(first, count), count)


def where_am_i():
    return tuple(lax.axis_index(axis) for axis in AXES)


def call(name, kernel, operands, outs, scratch=(), loaded=()):
    vmem = pl.BlockSpec(memory_space=pltpu.VMEM)
    return pl.pallas_call(
        kernel,
        in_specs=[pl.BlockSpec(memory_space=pl.ANY)] * len(loaded) + [vmem] * len(operands),
        out_specs=[vmem] * (len(loaded) + len(outs)),
        out_shape=[jax.ShapeDtypeStruct(v.shape, v.dtype) for v in loaded]
        + [jax.ShapeDtypeStruct(*o) for o in outs],
        scratch_shapes=[pltpu.VMEM(*s) for s in scratch]
        + [pltpu.SemaphoreType.DMA((len(loaded),))] * bool(loaded),
        compiler_params=pltpu.CompilerParams(vmem_limit_bytes=16 << 20),
        cost_estimate=pl.CostEstimate(
            flops=int(COSTS[name] * 10**9) + 1, bytes_accessed=1, transcendentals=0
        ),
    )(*in_hbm(loaded), *operands)


def prepare_kernel(*refs):
    rows_ref, ins, refs = refs[0], refs[1:14], refs[14:]
    x_mine, c_send, c_mine, count_ref, small, wqkv, wo = refs[:7]
    held, sems = refs[7:18], refs[18]
    core, _, place = where_am_i()
    copies = [
        pltpu.make_async_copy(source, target, sems.at[i])
        for i, (source, target) in enumerate(zip(ins, held + (wqkv, wo)))
    ]
    for copy in copies:
        copy.start()
    for copy in copies[:11]:
        copy.wait()
    (
        mask_ref, x_ref, cot_ref, gain1, bias1, qv_bias, out_bias, gain2, bias2, down_bias, up_bias,
    ) = held
    piece = mask_ref.shape[1]
    diagonal = lax.broadcasted_iota(jnp.int32, (piece, piece), 0) == lax.broadcasted_iota(
        jnp.int32, (piece, piece), 1
    )
    rows = rows_ref[0, 0]

    def column(row):
        kept = mask_ref[pl.ds(row, 1), :].astype(SINGLE) * (row < rows).astype(SINGLE)
        return jnp.sum(jnp.where(diagonal, kept, 0.0), axis=1, keepdims=True), kept

    weight_send, kept_send = column(1 - place)
    c_send[...] = (cot_ref[1 - place].astype(SINGLE) * weight_send).astype(LOW)
    weight_mine, kept_mine = column(place)
    c_mine[...] = (cot_ref[place].astype(SINGLE) * weight_mine).astype(LOW)
    x_mine[...] = x_ref[place]
    count = jnp.sum(kept_mine + kept_send, axis=1, keepdims=True).astype(jnp.int32)
    lane = lax.broadcasted_iota(jnp.int32, count_ref.shape, 1) - core * DIGITS
    digit = lax.shift_right_logical(
        jnp.broadcast_to(count, count_ref.shape), jnp.clip(lane, 0, DIGITS - 1)
    )
    count_ref[...] = jnp.where((lane >= 0) & (lane < DIGITS), digit & 1, 0).astype(SINGLE)
    features = small.shape[1]
    small[12:16, :] = jnp.broadcast_to((place < rows).astype(SINGLE), (4, features))
    small[2:4, :] = qv_bias[...].astype(SINGLE)
    for line, value in ((0, gain1), (1, bias1), (4, out_bias), (5, gain2), (6, bias2), (7, down_bias)):
        small[line : line + 1, :] = value[...].astype(SINGLE)[None, :]
    ups = up_bias[...].astype(SINGLE)[None, :]
    for part in range(ups.shape[1] // features):
        small[8 + part : 9 + part, :] = ups[:, part * features : (part + 1) * features]
    for copy in copies[11:]:
        copy.wait()


def in_hbm(values):
    return [pltpu.with_memory_space_constraint(value, pltpu.HBM) for value in values]


def prepare(rows, mask, x, cot, vectors, weights):
    piece, features = cot.shape[1:]
    part = jax.ShapeDtypeStruct((piece, features), LOW)
    vmem = pl.BlockSpec(memory_space=pltpu.VMEM)
    held = (mask, x, cot, *vectors)
    return pl.pallas_call(
        prepare_kernel,
        in_specs=[pl.BlockSpec(memory_space=pltpu.SMEM)] + [pl.BlockSpec(memory_space=pl.ANY)] * 13,
        out_specs=[vmem] * 7,
        out_shape=[
            part,
            part,
            part,
            jax.ShapeDtypeStruct((1, 128), SINGLE),
            jax.ShapeDtypeStruct((16, features), SINGLE),
        ]
        + [jax.ShapeDtypeStruct(w.shape, w.dtype) for w in weights],
        scratch_shapes=[pltpu.VMEM(v.shape, v.dtype) for v in held]
        + [pltpu.SemaphoreType.DMA((13,))],
        compiler_params=pltpu.CompilerParams(vmem_limit_bytes=8 << 20),
        cost_estimate=pl.CostEstimate(flops=2 * 10**9, bytes_accessed=1, transcendentals=0),
    )(rows, *in_hbm(held), *in_hbm(weights))


def join_row(place, mine_ref, other_ref, row_ref):
    piece = mine_ref.shape[0]
    row_ref[rows_at(place * piece, piece), :] = mine_ref[...].astype(row_ref.dtype)
    row_ref[rows_at((1 - place) * piece, piece), :] = other_ref[...].astype(row_ref.dtype)


def attend_kernel(
    up_ref, down_ref, x_mine, x_other, small, wqkv, wo,
    up, down, n1, qkv, probs, mixed_low, middle, n2, heads_q, sems,
):
    _, _, place = where_am_i()
    copies = [
        pltpu.make_async_copy(up_ref, up, sems.at[0]),
        pltpu.make_async_copy(down_ref, down, sems.at[1]),
    ]
    for copy in copies:
        copy.start()
    length, features = n1.shape
    groups = features // GW
    join_row(place, x_mine, x_other, middle)
    normal, _ = normalize(middle[...])
    n1[...] = (normal * small[0:1, :] + small[1:2, :]).astype(LOW)
    for which in range(3):
        value = dot_nn(n1[...], wqkv[:, which * features : (which + 1) * features])
        if which != 1:
            line = 2 + which // 2
            value = value + small[line : line + 1, :]
        value = value.astype(LOW)
        for group in range(groups):
            qkv[which * groups + group] = value[:, group * GW : (group + 1) * GW]
    allowed = lax.broadcasted_iota(jnp.int32, (length, length), 0) >= lax.broadcasted_iota(
        jnp.int32, (length, length), 1
    )
    lanes = lax.broadcasted_iota(jnp.int32, (1, GW), 1)

    def one_group(group, carry):
        query, keys, values = (qkv[which * groups + group] for which in range(3))
        spread_heads(query, heads_q, HD**-0.5)
        parts = []
        for head in range(GROUP):
            cut = slice(head * length, (head + 1) * length)
            scores = jnp.where(allowed, dot_nt(heads_q[cut, :], keys), NEGATIVE)
            powers = jnp.exp(scores - jnp.max(scores, axis=-1, keepdims=True))
            low = (powers * (1.0 / jnp.sum(powers, axis=-1, keepdims=True))).astype(LOW)
            probs[group, cut, :] = low
            parts.append(low)
        mixed = dot_nn(parts[0], values)
        for head in range(1, GROUP):
            mixed = jnp.where(lanes >= head * HD, dot_nn(parts[head], values), mixed)
        mixed_low[:, rows_at(group * GW, GW)] = mixed.astype(LOW)
        return carry

    lax.fori_loop(0, groups, one_group, 0)
    middle[...] += dot_nn(mixed_low[...], wo[...]) + small[4:5, :]
    normal, _ = normalize(middle[...])
    n2[...] = (normal * small[5:6, :] + small[6:7, :]).astype(LOW)
    for copy in copies:
        copy.wait()


def attend(x_mine, x_other, small, qkv_weight, out_weight, up_weight, down_weight):
    piece, features = x_other.shape
    length = 2 * piece
    groups = features // GW
    act = ((length, features), LOW)
    return call(
        "attend",
        attend_kernel,
        (x_mine, x_other, small, qkv_weight, out_weight),
        [
            act,
            ((3 * groups, length, GW), LOW),
            ((groups, GROUP * length, length), LOW),
            act,
            ((length, features), SINGLE),
            act,
        ],
        [((GROUP * length, GW), LOW)],
        loaded=(up_weight, down_weight),
    )


def gelu_and_slope(u):
    c = math.sqrt(2 / math.pi)
    square = u * u
    bent = jnp.tanh(u * (c + (c * 0.044715) * square))
    half = 0.5 + 0.5 * bent
    slope = half + u * (0.5 - 0.5 * bent * bent) * (c + (3 * c * 0.044715) * square)
    return u * half, slope


def feed_tiles(side, n2, db2, small, up, down, g, du, vec, total):
    tiles, _, features = g.shape

    def one_tile(tile, carry):
        number = side * tiles + tile
        cut = rows_at(number * features, features)
        line = pl.ds(8 + number, 1)
        hidden = dot_nn(n2[...], up[:, cut]) + small[line, :]
        active, slope = gelu_and_slope(hidden)
        g[tile] = active.astype(LOW)
        grad = (dot_nt(db2[...], down[cut, :]) * slope).astype(LOW)
        du[tile] = grad
        vec[line, :] = jnp.sum(grad.astype(SINGLE), axis=0, keepdims=True)
        total[...] += dot_nt(grad, up[:, cut])
        return carry

    lax.fori_loop(0, tiles, one_tile, 0)


def feed_one_kernel(
    n2, c_mine, c_other, small, count, up, down, g, du, db2, theirs, dn, vec,
):
    core, _, place = where_am_i()
    half = theirs.shape[1]
    join_row(place, c_mine, c_other, db2)
    theirs[...] = db2[:, rows_at((1 - core) * half, half)]
    vec[...] = jnp.zeros_like(vec)
    vec[7:8, :] = jnp.sum(db2[...].astype(SINGLE), axis=0, keepdims=True)
    vec[12:13, 0:128] = count[...]
    dn[...] = jnp.zeros_like(dn)
    feed_tiles(1 - core, n2, db2, small, up, down, g, du, vec, dn)


def feed_one(n2, c_mine, c_other, small, count, up, down):
    length, features = n2.shape
    tiles = up.shape[1] // 2 // features
    hid = ((tiles, length, features), LOW)
    return call(
        "feed_one",
        feed_one_kernel,
        (n2, c_mine, c_other, small, count, up, down),
        [
            hid, hid, ((length, features), LOW), ((length, features // 2), LOW),
            ((length, features), SINGLE), ((16, features), SINGLE),
        ],
    )


def feed_two_kernel(
    n2, db2, small, up, down, middle, dn, vec_in, g, du, dm, db1, theirs, vec,
):
    core, _, _ = where_am_i()
    half = theirs.shape[1]
    vec[...] = vec_in[...]
    dm[...] = dn[...]
    feed_tiles(core, n2, db2, small, up, down, g, du, vec, dm)
    grad_n = dm[...]
    normal, inverse = normalize(middle[...])
    vec[5:6, :] = jnp.sum(grad_n * normal, axis=0, keepdims=True)
    vec[6:7, :] = jnp.sum(grad_n, axis=0, keepdims=True)
    grad = db2[...].astype(SINGLE) + norm_back(normal, inverse, grad_n, small[5:6, :])
    dm[...] = grad
    low = grad.astype(LOW)
    db1[...] = low
    theirs[...] = db1[:, rows_at((1 - core) * half, half)]
    vec[4:5, :] = jnp.sum(low.astype(SINGLE), axis=0, keepdims=True)


def feed_two(n2, db2, small, up, down, middle, dn, vec_in):
    length, features = n2.shape
    tiles = up.shape[1] // 2 // features
    hid = ((tiles, length, features), LOW)
    return call(
        "feed_two",
        feed_two_kernel,
        (n2, db2, small, up, down, middle, dn, vec_in),
        [
            hid, hid, ((length, features), SINGLE), ((length, features), LOW),
            ((length, features // 2), LOW), ((16, features), SINGLE),
        ],
    )


def result_kernel(g_mine, g_theirs, middle, small, down, y_mine, y_send, total):
    core, _, place = where_am_i()
    tiles, _, features = g_mine.shape
    piece = y_mine.shape[0]
    total[...] = middle[...] + small[7:8, :]

    def one_tile(tile, carry):
        for side, active in ((core, g_mine), (1 - core, g_theirs)):
            cut = rows_at((side * tiles + tile) * features, features)
            total[...] += dot_nn(active[tile], down[cut, :])
        return carry

    lax.fori_loop(0, tiles, one_tile, 0)
    present = small[12:13, :]
    y_mine[...] = (total[rows_at(place * piece, piece), :] * present).astype(LOW)
    y_send[...] = (total[rows_at((1 - place) * piece, piece), :] * present).astype(LOW)


def result(g_mine, g_theirs, middle, small, down):
    length, features = middle.shape
    part = ((length // 2, features), LOW)
    return call(
        "result",
        result_kernel,
        (g_mine, g_theirs, middle, small, down),
        [part, part],
        [((length, features), SINGLE)],
    )


def back_kernel(
    qkv, probs, db1, wo, vec_in, theirs, mine, vec, dp, heads_q, heads_k, heads_g, side,
):
    core, _, _ = where_am_i()
    features = db1.shape[1]
    groups = features // GW
    vec[...] = vec_in[...]

    def one_group(group, carry):
        cut = rows_at(group * GW, GW)
        grad_mixed = dot_nt(db1[...], wo[cut, :]).astype(LOW)
        query, keys, values = (qkv[which * groups + group] for which in range(3))
        spread_heads(grad_mixed, heads_g)
        spread_heads(query, heads_q, HD**-0.5)
        spread_heads(keys, heads_k, HD**-0.5)
        weights = probs[group].astype(SINGLE)
        grad_probs = dot_nt(heads_g[...], values)
        inner = jnp.sum(weights * grad_probs, axis=-1, keepdims=True)
        grad_scores = (weights * (grad_probs - inner)).astype(LOW)
        side_by_side(grad_scores, side)
        dv = dot_tn(probs[group], heads_g[...])
        dk = dot_tn(grad_scores, heads_q[...])
        dq = dot_nn(side[...], heads_k[...])
        for which, value in enumerate((dq, dk, dv)):
            low = value.astype(LOW)
            dp[:, rows_at(which * features + group * GW, GW)] = low
            if which != 1:
                line = 2 + which // 2
                vec[line : line + 1, cut] = jnp.sum(low.astype(SINGLE), axis=0, keepdims=True)
        return carry

    lax.fori_loop(0, groups, one_group, 0)
    half = mine.shape[1]
    theirs[...] = dp[:, rows_at((1 - core) * half, half)]
    mine[...] = dp[:, rows_at(core * half, half)]


def back(qkv, probs, db1, out_weight, vec_in):
    length, features = db1.shape
    half = ((length, 3 * features // 2), LOW)
    return call(
        "back",
        back_kernel,
        (qkv, probs, db1, out_weight, vec_in),
        [half, half, ((16, features), SINGLE)],
        [((length, 3 * features), LOW)]
        + [((GROUP * length, GW), LOW)] * 3
        + [((length, GROUP * length), LOW)],
    )


def input_kernel(
    x_mine, x_other, small, dp_mine, dp_theirs, wqkv, dm, vec_in, mine, send, vec, row,
):
    core, _, place = where_am_i()
    half = dp_mine.shape[1]
    piece = mine.shape[0]
    grad_n = dot_nt(dp_mine[...], wqkv[:, rows_at(core * half, half)])
    grad_n = grad_n + dot_nt(dp_theirs[...], wqkv[:, rows_at((1 - core) * half, half)])
    join_row(place, x_mine, x_other, row)
    normal, inverse = normalize(row[...])
    vec[...] = vec_in[...]
    vec[0:1, :] = jnp.sum(grad_n * normal, axis=0, keepdims=True)
    vec[1:2, :] = jnp.sum(grad_n, axis=0, keepdims=True)
    row[...] = dm[...] + norm_back(normal, inverse, grad_n, small[0:1, :])
    mine[...] = row[rows_at(place * piece, piece), :].astype(LOW)
    send[...] = row[rows_at((1 - place) * piece, piece), :].astype(LOW)


def input_gradient(x_mine, x_other, small, dp_mine, dp_theirs, qkv_weight, dm, vec_in):
    piece, features = x_other.shape
    part = ((piece, features), LOW)
    return call(
        "input",
        input_kernel,
        (x_mine, x_other, small, dp_mine, dp_theirs, qkv_weight, dm, vec_in),
        [part, part, ((16, features), SINGLE)],
        [((2 * piece, features), SINGLE)],
    )


UNITS = 16


def unit_of(name, number):
    core, own, place = where_am_i()
    units = []
    for order in WAYS[name]:
        unit = 0
        for stage, axis in enumerate(order):
            if number >> (3 - stage) & 1:
                unit |= 1 if axis == "x" else BITS[axis] << 1
        units.append(unit)
    return jnp.where(core == 0, units[0], units[1]) ^ (own * 2 + place)


def lanes_kernel(
    g_mine, g_theirs, other_mine, other_theirs, right, right_other, send, keep, turned, whole, *, name
):
    core, _, _ = where_am_i()
    chunks, tall, wide = whole.shape
    tiles, length, features = g_mine.shape
    per_tile = features // wide
    half = tall // 2
    turned[:, :length] = right[:, rows_at(core * tall, tall)].T
    turned[:, length:] = right_other[...].T
    for side, one, two in ((core, g_mine, other_theirs), (1 - core, g_theirs, other_mine)):

        def one_tile(tile, carry, side=side, one=one, two=two):
            total = dot_nn(turned[:, :length], one[tile]) + dot_nn(turned[:, length:], two[tile])
            total = total.astype(LOW)
            for chunk in range(per_tile):
                whole[(side * tiles + tile) * per_tile + chunk] = total[:, chunk * wide : (chunk + 1) * wide]
            return carry

        lax.fori_loop(0, tiles, one_tile, 0)
    for number in range(UNITS):
        unit = unit_of(name, number)
        out = send if number >= UNITS // 2 else keep
        out[number % (UNITS // 2)] = whole[lax.div(unit, 2), rows_at(lax.rem(unit, 2) * half, half), :]


def grad_lanes(name, mine, theirs, other_mine, other_theirs, right, right_other):
    tiles, length, features = mine.shape
    tall = right_other.shape[1]
    chunks = UNITS // 2
    wide = 2 * tiles * features // chunks
    unit = ((UNITS // 2, tall // 2, wide), LOW)
    return call(
        "lanes",
        functools.partial(lanes_kernel, name=name),
        (mine, theirs, other_mine, other_theirs, right, right_other),
        [unit, unit],
        [((tall, 2 * length), LOW), ((chunks, tall, wide), LOW)],
    )


def rows_kernel(left, left_other, right, right_other, *rest, name, pick_core):
    if len(rest) > 4:
        vec, vec_other, send, keep, turned, whole, spread = rest
    else:
        send, keep, turned, whole = rest
        vec = None
    core, _, _ = where_am_i()
    length = left.shape[0]
    split = len(right_other.shape) == 2
    tiles, tile = (1, right_other.shape[1]) if split else (right_other.shape[0], right_other.shape[2])
    turned[:, :length] = left[...].T
    turned[:, length:] = left_other[...].T
    rows = turned.shape[0] // UNITS
    units = [unit_of(name, number) for number in range(UNITS)]
    if vec is not None:
        total = vec[...] + vec_other[...]
        features = total.shape[1]
        part = 2 * rows
        spread[...] = jnp.zeros_like(spread)
        for chunk in range(UNITS // 2):
            spread[2 * chunk, 0:8, :part] = total[0:8, chunk * part : (chunk + 1) * part]
            for piece in range(4):
                line, begin = divmod((4 * chunk + piece) * part, features)
                spread[2 * chunk + 1, piece : piece + 1, :part] = total[
                    8 + line : 9 + line, begin : begin + part
                ]
            spread[2 * chunk + 1, 4:5, : 2 * DIGITS] = total[12:13, : 2 * DIGITS]
        for out in (send, keep):
            out[:, rows:, :] = jnp.zeros_like(out[:, rows:, :])

    def one_tile(step, carry):
        if split:
            here = right[:, rows_at(core * tile, tile)] if pick_core else right[...]
            there = right_other[...]
        else:
            here, there = right[step], right_other[step]
        whole[...] = (dot_nn(turned[:, :length], here) + dot_nn(turned[:, length:], there)).astype(LOW)
        columns = rows_at(step * tile, tile)
        for number, unit in enumerate(units):
            out = send if number >= UNITS // 2 else keep
            out[number % (UNITS // 2), :rows, columns] = whole[rows_at(unit * rows, rows), :]
        return carry

    if tiles == 1:
        one_tile(0, 0)
    else:
        lax.fori_loop(0, tiles, one_tile, 0)
    if vec is not None:
        for number, unit in enumerate(units):
            out = send if number >= UNITS // 2 else keep
            out[number % (UNITS // 2), rows:, :128] = spread[unit].astype(LOW)


def grad_rows(name, left, left_other, right, right_other, pick_core=False, vecs=()):
    length, tall = left.shape
    rows = tall // UNITS
    tile = right_other.shape[-1]
    width = math.prod(right_other.shape) // length
    unit = ((UNITS // 2, rows + (16 if vecs else 0), width), LOW)
    return call(
        "rows_" + name,
        functools.partial(rows_kernel, name=name, pick_core=pick_core),
        (left, left_other, right, right_other, *vecs),
        [unit, unit],
        [((tall, 2 * length), LOW), ((tall, tile), LOW)] + [((UNITS, 16, 128), SINGLE)] * bool(vecs),
    )


def close_kernel(mine, other, *outs):
    vec = outs[-1]
    counts, whole, up, qv = outs[:4]
    plain = outs[4:-1]
    _, _, place = where_am_i()
    rows = mine.shape[0] - 16
    vec[rows_at(place * 8, 8), :] = mine[rows:, :128].astype(SINGLE)[:8]
    vec[rows_at((1 - place) * 8, 8), :] = other[rows:, :128].astype(SINGLE)[:8]
    line = vec[12:13, :]
    lane = lax.broadcasted_iota(jnp.int32, line.shape, 1)
    worth = lax.shift_left(jnp.ones_like(lane), lax.rem(lane, DIGITS)).astype(SINGLE)
    first, second = (
        jnp.sum(jnp.where(lane // DIGITS == half, line * worth, 0.0), axis=1, keepdims=True)
        for half in (0, 1)
    )
    total = first + second
    spot = lax.broadcasted_iota(jnp.int32, (1, 128), 1)
    both = jnp.where(spot == 0, first, second).astype(jnp.int32)
    counts[...] = both[0, :2]
    whole[...] = jnp.broadcast_to(total, whole.shape)
    width = qv.shape[1]
    scaled = vec[...] / total
    qv[...] = scaled[2:4, :width]
    for number, out in zip((0, 1, 4, 5, 6, 7), plain):
        out[...] = scaled[number, :width]
    up[...] = jnp.concatenate([scaled[8 + part : 9 + part, :width] for part in range(4)], axis=1)[0]


def close(mine, other, width):
    return call(
        "result",
        close_kernel,
        (mine, other),
        [((2,), jnp.int32), ((8, 128), SINGLE), ((4 * width,), SINGLE), ((2, width), SINGLE)]
        + [((width,), SINGLE)] * 6,
        [((16, 128), SINGLE)],
    )


def finish_kernel(whole, *refs, rows, turned):
    parts, out = refs[:4], refs[4]
    core, _, place = where_am_i()
    total = whole[0:1, 0:1]
    for number, part in enumerate(parts):
        side, half = core ^ (number >> 1), place ^ (number & 1)
        if turned:
            refs[5][rows_at((side * 2 + half) * rows, rows), :] = part[...].astype(SINGLE)
        else:
            width = part.shape[1]
            out[rows_at(half * rows, rows), rows_at(side * width, width)] = (
                part[:rows, :].astype(SINGLE) / total
            )
    if turned:
        out[...] = refs[5][...].T / total


def finish(whole, parts, rows, turned=False):
    width = parts[0].shape[1]
    shape = (width, 4 * rows) if turned else (2 * rows, 2 * width)
    return call(
        "result",
        functools.partial(finish_kernel, rows=rows, turned=turned),
        (whole, *parts),
        [(shape, SINGLE)],
        [((4 * rows, width), SINGLE)] * turned,
    )[0]


def home_kernel(mine, other, out):
    _, _, place = where_am_i()
    out[place] = mine[...]
    out[1 - place] = other[...]


def home(mine, other):
    return call("result", home_kernel, (mine, other), [((2,) + mine.shape, LOW)])[0]


def swap_pairs(size, bit):
    return [(i, i ^ bit) for i in range(size)]


def partners(name, stage, groups):
    pairs = []
    for core in range(2):
        axis = WAYS[name][core][stage]
        for own in range(groups):
            for place in range(2):
                to = (own, place ^ 1) if axis == "x" else (own ^ BITS[axis], place)
                pairs.append(((core * groups + own) * 2 + place, (core * groups + to[0]) * 2 + to[1]))
    return pairs


def added(one, two):
    return (one.astype(SINGLE) + two.astype(SINGLE)).astype(LOW)


class Order:
    def __init__(self):
        self.last = None

    def tie(self, value):
        if self.last is not None:
            value, _ = lax.optimization_barrier((value, self.last))
        return value

    def mark(self, value):
        self.last = value


class Sum:
    def __init__(self, order, name, groups, send, keep):
        self.order, self.name, self.groups = order, name, groups
        self.keep = keep
        self.stage = 0
        self.whole_last = all(way[3] == "x" for way in WAYS[name])
        self.parts = None
        self.go(send)

    def go(self, send):
        self.flying = lax.ppermute(send, AXES, partners(self.name, self.stage, self.groups))

    def step(self):
        if self.parts is not None:
            return
        other = self.order.tie(self.flying)
        keep = self.keep
        self.stage += 1
        if self.stage == 5:
            self.order.mark(other)
            self.parts = [self.total, other]
        elif self.stage == 4 and self.whole_last:
            self.parts = [added(keep[0], other[1]), added(keep[1], other[0])]
            self.order.mark(self.parts[0])
        elif self.stage == 4:
            self.total = added(keep[0], other[0])
            self.order.mark(self.total)
            self.flying = lax.ppermute(self.total, "seq", swap_pairs(2, 1))
        elif self.stage == 3 and self.whole_last:
            self.keep = added(keep, other)
            self.order.mark(self.keep)
            self.go(self.keep)
        else:
            half = keep.shape[0] // 2
            send = added(keep[half:], other[half:])
            self.keep = added(keep[:half], other[:half])
            self.order.mark(send)
            self.go(send)


def body_fast(
    inputs,
    cotangent,
    row_counts,
    response_mask,
    norm1_gain,
    norm1_bias,
    qkv_weight,
    qv_bias,
    out_weight,
    out_bias,
    norm2_gain,
    norm2_bias,
    up_weight,
    up_bias,
    down_weight,
    down_bias,
):
    groups = lax.axis_size("dp")
    pair = swap_pairs(2, 1)
    core, own, place = (lax.axis_index(a) for a in ("src", "dp", "seq"))
    x_both = inputs[0, 0]
    x_other = lax.ppermute(
        lax.dynamic_index_in_dim(x_both, 1 - place, 0, keepdims=False), "seq", pair
    )
    x_mine, c_send, c_mine, count, small, qkv_weight, out_weight = prepare(
        row_counts,
        response_mask[0, 0],
        x_both,
        cotangent[0, 0],
        (norm1_gain, norm1_bias, qv_bias, out_bias, norm2_gain, norm2_bias, down_bias, up_bias),
        (qkv_weight, out_weight),
    )
    c_other = lax.ppermute(c_send, "seq", pair)
    order = Order()

    def from_core(value):
        return lax.ppermute(value, "src", pair)

    up_weight, down_weight, n1, qkv, probs, mixed, middle, n2 = attend(
        x_mine, x_other, small, qkv_weight, out_weight, up_weight, down_weight
    )
    g_theirs, du_theirs, db2, db2_theirs, dn, vec = feed_one(
        n2, c_mine, c_other, small, count, up_weight, down_weight
    )
    order.mark(vec)
    n2_other, n1_other, mixed_other = order.tie(
        (from_core(n2), from_core(n1), from_core(mixed))
    )
    here, n2_other, n1_other, mixed_other = lax.optimization_barrier(
        (n2, n2_other, n1_other, mixed_other)
    )
    g_mine, du_mine, dm, db1, db1_theirs, vec = feed_two(
        here, db2, small, up_weight, down_weight, middle, dn, vec
    )
    order.mark(vec)
    du_other, db2_other, other_theirs = order.tie(
        (from_core(du_theirs), from_core(db2_theirs), from_core(g_theirs))
    )
    here, du_other, db2_other, other_theirs = lax.optimization_barrier(
        (n2, du_other, db2_other, other_theirs)
    )
    other_mine, db1_other = from_core(g_mine), from_core(db1_theirs)

    sums = {}
    done = {}
    rows = out_weight.shape[0] // groups

    def rows_home(mine, send):
        other = order.tie(lax.ppermute(send, "seq", pair))
        both = home(mine, other)
        order.mark(both)
        return both[None, None]

    def finish_all():
        names = [n for n in sums if sums[n].parts is not None and n not in done]
        mine = order.tie([sums[n].parts for n in names])
        theirs = [[from_core(p) for p in parts] for parts in mine]
        for name, here, there in zip(names, mine, theirs):
            there = order.tie(there)
            turned = name == "d"
            done[name] = finish(
                done["whole"], here + there, 2 * rows if turned else rows // 2, turned
            )
            order.mark(done[name])

    for event in EVENTS:
        if event == "y":
            done["output"] = rows_home(y_mine, y_send)
            continue
        if event == "i":
            done["input_grad"] = rows_home(x_grad_mine, x_grad_send)
            continue
        if event == "+":
            finish_all()
            continue
        if event.islower():
            sums[event].step()
            if event == "o" and sums["o"].parts is not None and "whole" not in done:
                counts, done["whole"], up_small, qv, *plain = close(*sums["o"].parts, rows)
                order.mark(done["whole"])
            continue
        name = event.lower()
        if event == "U":
            parts = grad_rows(name, order.tie(here), n2_other, du_mine, du_other)
        elif event == "D":
            other_mine = order.tie(other_mine)
            here, other_mine = lax.optimization_barrier((g_mine, other_mine))
            parts = grad_lanes(name, here, g_theirs, other_mine, other_theirs, db2, db2_other)
        elif event == "C":
            here = order.tie(qkv)
            dp_theirs, dp_mine, vec = back(here, probs, db1, out_weight, vec)
            dp_other = from_core(dp_theirs)
            order.mark(vec)
            continue
        elif event == "I":
            x_grad_mine, x_grad_send, vec = input_gradient(
                order.tie(x_mine), x_other, small, dp_mine, dp_theirs, qkv_weight, dm, vec
            )
            vec_other = from_core(vec)
            order.mark(vec)
            continue
        elif event == "Y":
            y_mine, y_send = result(order.tie(g_mine), g_theirs, middle, small, down_weight)
            order.mark(y_send)
            continue
        elif event == "O":
            parts = grad_rows(
                name, order.tie(mixed), mixed_other, db1, db1_other, True, (vec, vec_other)
            )
        else:
            dp_other, db1_other = order.tie((dp_other, db1_other))
            here, dp_other, db1_other = lax.optimization_barrier((n1, dp_other, db1_other))
            parts = grad_rows(name, here, n1_other, dp_mine, dp_other)
        order.mark(parts[0])
        sums[name] = Sum(order, name, groups, *parts)

    return (
        done["output"],
        done["input_grad"],
        counts,
        plain[0],
        plain[1],
        done["q"],
        qv,
        done["o"],
        plain[2],
        plain[3],
        plain[4],
        done["u"],
        up_small,
        done["d"],
        plain[5],
    )


def solution(mesh):
    placed = (
        P("src", "dp", None, "seq", None),
        P("src", "dp", None, "seq", None),
        P("src", "dp"),
        P("src", "dp", None, "seq"),
        P(),
        P(),
        P(),
        P(),
        P(),
        P(),
        P(),
        P(),
        P(),
        P(),
        P(),
        P(),
    )
    sizes = dict(mesh.shape)
    paired = sizes["src"] == 2 and sizes["seq"] == 2 and sizes["dp"] == 8
    return jax.shard_map(
        body_fast if paired else body_generic,
        mesh=mesh,
        in_specs=placed,
        out_specs=(
            P("src", "dp", None, "seq", None),
            P("src", "dp", None, "seq", None),
            P(),
            P("dp"),
            P("dp"),
            P("dp", None),
            P(None, "dp"),
            P("dp", None),
            P("dp"),
            P("dp"),
            P("dp"),
            P("dp", None),
            P("dp"),
            P("dp", None),
            P("dp"),
        ),
        check_vma=False,
    )
```

```python
import functools
import math

import jax
import jax.numpy as jnp
from jax import lax
from jax.experimental import pallas as pl
from jax.experimental.pallas import tpu as pltpu
from jax.sharding import PartitionSpec as P

H = 12
HD = 64


EPS = 1e-05
NEGATIVE = -1e30


def norm_apply(values, scaling, offset):
    centre = jnp.mean(values, axis=-1, keepdims=True)
    centered = values - centre
    spread = jnp.mean(centered * centered, axis=-1, keepdims=True)
    return centered * lax.rsqrt(spread + EPS) * scaling + offset


def causal_scores(query_part, keys_part, allowed):
    scores = jnp.einsum(
        "rqhd,rkhd->rhqk", query_part, keys_part, preferred_element_type=jnp.float32
    )
    scores = scores * HD ** (-0.5)
    return jnp.where(allowed, scores, NEGATIVE)


def attend_forward(query_part, keys_part, values_part, allowed):
    scores = causal_scores(query_part, keys_part, allowed)
    highest = jnp.max(scores, axis=-1, keepdims=True)
    powers = jnp.exp(scores - highest)
    totals = jnp.sum(powers, axis=-1, keepdims=True)
    probs_low = (powers / totals).astype(jnp.bfloat16)
    mixed = jnp.einsum(
        "rhqk,rkhd->rqhd", probs_low, values_part, preferred_element_type=jnp.float32
    )
    return (mixed, highest, totals)


def attend_backward(query_part, keys_part, values_part, grad_part, highest, totals, allowed):
    scores = causal_scores(query_part, keys_part, allowed)
    probs = jnp.exp(scores - highest) / totals
    probs_low = probs.astype(jnp.bfloat16)
    grad_probs = jnp.einsum(
        "rqhd,rkhd->rhqk", grad_part, values_part, preferred_element_type=jnp.float32
    )
    inner = jnp.sum(probs * grad_probs, axis=-1, keepdims=True)
    grad_scores = (probs * (grad_probs - inner)).astype(jnp.bfloat16)
    factor = HD ** (-0.5)
    grad_query = (
        jnp.einsum("rhqk,rkhd->rqhd", grad_scores, keys_part, preferred_element_type=jnp.float32)
        * factor
    )
    grad_keys = (
        jnp.einsum("rhqk,rqhd->rkhd", grad_scores, query_part, preferred_element_type=jnp.float32)
        * factor
    )
    grad_values = jnp.einsum(
        "rhqk,rqhd->rkhd", probs_low, grad_part, preferred_element_type=jnp.float32
    )
    return (grad_query, grad_keys, grad_values)


def body_generic(
    inputs,
    cotangent,
    row_counts,
    response_mask,
    norm1_gain,
    norm1_bias,
    qkv_weight,
    qv_bias,
    out_weight,
    out_bias,
    norm2_gain,
    norm2_bias,
    up_weight,
    up_bias,
    down_weight,
    down_bias,
):
    slots = inputs.shape[2]
    piece_len = inputs.shape[3]
    features = inputs.shape[4]
    tokens = slots * piece_len
    blocks_seq = lax.axis_size("seq")
    row_len = piece_len * blocks_seq
    group_heads = math.gcd(H, 4)
    bfloat = jnp.bfloat16
    single = jnp.float32
    present_int = (jnp.arange(slots) < row_counts[0, 0]).astype(jnp.int32)
    weight = (response_mask[0, 0] * present_int[:, None]).astype(single)
    local_count = jnp.sum(response_mask[0, 0] * present_int[:, None])
    picked = jnp.where(jnp.arange(lax.axis_size("src")) == lax.axis_index("src"), local_count, 0)
    source_counts = lax.psum(picked, ("src", "dp", "seq"))
    whole = jnp.sum(source_counts).astype(single)
    source = inputs.reshape(tokens, features).astype(single)
    normed, norm1_pull = jax.vjp(
        norm_apply, source, norm1_gain.astype(single), norm1_bias.astype(single)
    )
    normed_low = normed.astype(bfloat)
    bias_query = qv_bias[0].astype(single)
    joined = jnp.concatenate([bias_query, jnp.zeros_like(bias_query), qv_bias[1].astype(single)])
    projected = jnp.dot(normed_low, qkv_weight, preferred_element_type=single) + joined
    proj_low = projected.astype(bfloat)
    query = proj_low[:, :features].reshape(slots, piece_len, H, HD)
    keys_own = proj_low[:, features : 2 * features].reshape(slots, piece_len, features)
    values_own = proj_low[:, 2 * features :].reshape(slots, piece_len, features)
    keys_all, values_all = (
        lax.all_gather(keys_own, "seq", axis=1, tiled=True),
        lax.all_gather(values_own, "seq", axis=1, tiled=True),
    )
    query_pos = lax.axis_index("seq") * piece_len + jnp.arange(piece_len)
    allowed = query_pos[:, None] >= jnp.arange(row_len)[None, :]
    keys_heads = keys_all.reshape(slots, row_len, H, HD)
    values_heads = values_all.reshape(slots, row_len, H, HD)
    mixed_parts = []
    kept_stats = []
    for group in range(H // group_heads):
        first = group * group_heads
        last = first + group_heads
        mixed, highest, totals = attend_forward(
            query[:, :, first:last],
            keys_heads[:, :, first:last],
            values_heads[:, :, first:last],
            allowed,
        )
        mixed_parts.append(mixed)
        kept_stats.append((highest, totals))
    attended = jnp.concatenate(mixed_parts, axis=2).reshape(tokens, features)
    attended_low = attended.astype(bfloat)
    branch = jnp.dot(attended_low, out_weight, preferred_element_type=single) + out_bias.astype(
        single
    )
    middle = source + branch
    normed_two, norm2_pull = jax.vjp(
        norm_apply, middle, norm2_gain.astype(single), norm2_bias.astype(single)
    )
    normed_two_low = normed_two.astype(bfloat)
    hidden = jnp.dot(normed_two_low, up_weight, preferred_element_type=single) + up_bias.astype(
        single
    )
    active, gelu_pull = jax.vjp(functools.partial(jax.nn.gelu, approximate=True), hidden)
    active_low = active.astype(bfloat)
    branch_two = jnp.dot(active_low, down_weight, preferred_element_type=single) + down_bias.astype(
        single
    )
    result = middle + branch_two
    present_tok = jnp.repeat(present_int.astype(single), piece_len)
    output = (result * present_tok[:, None]).astype(bfloat).reshape(inputs.shape)
    incoming = cotangent.reshape(tokens, features).astype(single) * weight.reshape(tokens)[:, None]
    grad_branch_two = incoming.astype(bfloat)
    grad_down_weight = jnp.einsum(
        "tf,td->fd", active_low, grad_branch_two, preferred_element_type=single
    )
    grad_down_bias = jnp.sum(grad_branch_two.astype(single), axis=0)
    grad_active = jnp.einsum(
        "td,fd->tf", grad_branch_two, down_weight, preferred_element_type=single
    )
    grad_hidden = gelu_pull(grad_active)[0].astype(bfloat)
    grad_up_weight = jnp.einsum(
        "tm,tf->mf", normed_two_low, grad_hidden, preferred_element_type=single
    )
    grad_up_bias = jnp.sum(grad_hidden.astype(single), axis=0)
    grad_normed_two = jnp.einsum("tf,mf->tm", grad_hidden, up_weight, preferred_element_type=single)
    grad_mid_norm, grad_norm2_gain, grad_norm2_bias = norm2_pull(grad_normed_two)
    grad_middle = incoming + grad_mid_norm
    grad_branch = grad_middle.astype(bfloat)
    grad_out_weight = jnp.einsum(
        "tm,td->md", attended_low, grad_branch, preferred_element_type=single
    )
    grad_out_bias = jnp.sum(grad_branch.astype(single), axis=0)
    grad_attended = jnp.einsum("td,md->tm", grad_branch, out_weight, preferred_element_type=single)
    grad_heads = grad_attended.astype(bfloat).reshape(slots, piece_len, H, HD)
    query_grads = []
    key_grads = []
    value_grads = []
    for group in range(H // group_heads):
        first = group * group_heads
        last = first + group_heads
        highest, totals = kept_stats[group]
        grad_query, grad_keys, grad_values = attend_backward(
            query[:, :, first:last],
            keys_heads[:, :, first:last],
            values_heads[:, :, first:last],
            grad_heads[:, :, first:last],
            highest,
            totals,
            allowed,
        )
        query_grads.append(grad_query)
        key_grads.append(grad_keys)
        value_grads.append(grad_values)
    grad_query_all = jnp.concatenate(query_grads, axis=2).reshape(tokens, features)
    grad_keys_all = jnp.concatenate(key_grads, axis=2).reshape(slots, row_len, features)
    grad_values_all = jnp.concatenate(value_grads, axis=2).reshape(slots, row_len, features)
    grad_keys_own, grad_values_own = (
        lax.psum_scatter(
            grad_keys_all.astype(jnp.bfloat16), "seq", scatter_dimension=1, tiled=True
        ).astype(jnp.float32),
        lax.psum_scatter(
            grad_values_all.astype(jnp.bfloat16), "seq", scatter_dimension=1, tiled=True
        ).astype(jnp.float32),
    )
    grad_projected = jnp.concatenate(
        [
            grad_query_all,
            grad_keys_own.reshape(tokens, features),
            grad_values_own.reshape(tokens, features),
        ],
        axis=1,
    ).astype(bfloat)
    grad_qkv_weight = jnp.einsum(
        "tm,tn->mn", normed_low, grad_projected, preferred_element_type=single
    )
    column_sums = jnp.sum(grad_projected.astype(single), axis=0)
    grad_qv_bias = jnp.stack([column_sums[:features], column_sums[2 * features :]])
    grad_normed = jnp.einsum("tn,mn->tm", grad_projected, qkv_weight, preferred_element_type=single)
    grad_src_norm, grad_norm1_gain, grad_norm1_bias = norm1_pull(grad_normed)
    input_grad = (grad_middle + grad_src_norm).astype(bfloat).reshape(inputs.shape)
    grads = (
        grad_norm1_gain,
        grad_norm1_bias,
        grad_qkv_weight,
        grad_qv_bias,
        grad_out_weight,
        grad_out_bias,
        grad_norm2_gain,
        grad_norm2_bias,
        grad_up_weight,
        grad_up_bias,
        grad_down_weight,
        grad_down_bias,
    )
    summed = (
        lax.psum_scatter(
            grads[0].astype(jnp.bfloat16), "dp", scatter_dimension=0, tiled=True
        ).astype(jnp.float32),
        lax.psum_scatter(
            grads[1].astype(jnp.bfloat16), "dp", scatter_dimension=0, tiled=True
        ).astype(jnp.float32),
        lax.psum_scatter(
            grads[2].astype(jnp.bfloat16), "dp", scatter_dimension=0, tiled=True
        ).astype(jnp.float32),
        lax.psum_scatter(
            grads[3].astype(jnp.bfloat16), "dp", scatter_dimension=1, tiled=True
        ).astype(jnp.float32),
        lax.psum_scatter(
            grads[4].astype(jnp.bfloat16), "dp", scatter_dimension=0, tiled=True
        ).astype(jnp.float32),
        lax.psum_scatter(
            grads[5].astype(jnp.bfloat16), "dp", scatter_dimension=0, tiled=True
        ).astype(jnp.float32),
        lax.psum_scatter(
            grads[6].astype(jnp.bfloat16), "dp", scatter_dimension=0, tiled=True
        ).astype(jnp.float32),
        lax.psum_scatter(
            grads[7].astype(jnp.bfloat16), "dp", scatter_dimension=0, tiled=True
        ).astype(jnp.float32),
        lax.psum_scatter(
            grads[8].astype(jnp.bfloat16), "dp", scatter_dimension=0, tiled=True
        ).astype(jnp.float32),
        lax.psum_scatter(
            grads[9].astype(jnp.bfloat16), "dp", scatter_dimension=0, tiled=True
        ).astype(jnp.float32),
        lax.psum_scatter(
            grads[10].astype(jnp.bfloat16), "dp", scatter_dimension=0, tiled=True
        ).astype(jnp.float32),
        lax.psum_scatter(
            grads[11].astype(jnp.bfloat16), "dp", scatter_dimension=0, tiled=True
        ).astype(jnp.float32),
    )
    summed = (
        lax.psum(summed[0].astype(jnp.bfloat16), ("src", "seq")).astype(jnp.float32),
        lax.psum(summed[1].astype(jnp.bfloat16), ("src", "seq")).astype(jnp.float32),
        lax.psum(summed[2].astype(jnp.bfloat16), ("src", "seq")).astype(jnp.float32),
        lax.psum(summed[3].astype(jnp.bfloat16), ("src", "seq")).astype(jnp.float32),
        lax.psum(summed[4].astype(jnp.bfloat16), ("src", "seq")).astype(jnp.float32),
        lax.psum(summed[5].astype(jnp.bfloat16), ("src", "seq")).astype(jnp.float32),
        lax.psum(summed[6].astype(jnp.bfloat16), ("src", "seq")).astype(jnp.float32),
        lax.psum(summed[7].astype(jnp.bfloat16), ("src", "seq")).astype(jnp.float32),
        lax.psum(summed[8].astype(jnp.bfloat16), ("src", "seq")).astype(jnp.float32),
        lax.psum(summed[9].astype(jnp.bfloat16), ("src", "seq")).astype(jnp.float32),
        lax.psum(summed[10].astype(jnp.bfloat16), ("src", "seq")).astype(jnp.float32),
        lax.psum(summed[11].astype(jnp.bfloat16), ("src", "seq")).astype(jnp.float32),
    )
    final = [g / whole for g in summed]
    return (
        output,
        input_grad,
        source_counts,
        final[0],
        final[1],
        final[2],
        final[3],
        final[4],
        final[5],
        final[6],
        final[7],
        final[8],
        final[9],
        final[10],
        final[11],
    )


WAYS = {
    "u": ("xy12", "12yx"),
    "d": ("yx12", "1yx2"),
    "o": ("x12y", "yx12"),
    "q": ("x1y2", "yx12"),
}
EVENTS = "UDCIOQYudoqudoqhudqoduoqiduoq"
BITS = {"y": 1, "1": 2, "2": 4}


COSTS = {"prepare": 2, "load": 4, "attend": 8, "feed_one": 5, "feed_two": 5, "back": 0, "input": 0, "lanes": 0, "rows_u": 4, "rows_q": 0, "rows_o": 0, "result": 0}
AXES = ("src", "dp", "seq")
SINGLE = jnp.float32
LOW = jnp.bfloat16
GROUP = 4
GW = GROUP * HD
DIGITS = 16


def dot_nt(left, right):
    return lax.dot_general(left, right, (((1,), (1,)), ((), ())), preferred_element_type=SINGLE)


def dot_tn(left, right):
    return lax.dot_general(left, right, (((0,), (0,)), ((), ())), preferred_element_type=SINGLE)


def dot_nn(left, right):
    return jnp.dot(left, right, preferred_element_type=SINGLE)


def normalize(values):
    centered = values - jnp.mean(values, axis=-1, keepdims=True)
    inverse = lax.rsqrt(jnp.mean(centered * centered, axis=-1, keepdims=True) + EPS)
    return centered * inverse, inverse


def norm_back(normal, inverse, grad, gain):
    scaled = grad * gain
    return inverse * (
        scaled
        - jnp.mean(scaled, axis=-1, keepdims=True)
        - normal * jnp.mean(scaled * normal, axis=-1, keepdims=True)
    )


def spread_heads(value, out, scale=1.0):
    length = value.shape[0]
    lanes = lax.broadcasted_iota(jnp.int32, (1, GW), 1)
    for head in range(GROUP):
        keep = jnp.where((lanes >= head * HD) & (lanes < (head + 1) * HD), scale, 0.0).astype(LOW)
        out[head * length : (head + 1) * length, :] = value * keep


def side_by_side(stacked, out):
    length = out.shape[0]
    for head in range(GROUP):
        out[:, head * length : (head + 1) * length] = stacked[head * length : (head + 1) * length, :]


def rows_at(first, count):
    return pl.ds(pl.multiple_of(first, count), count)


def where_am_i():
    return tuple(lax.axis_index(axis) for axis in AXES)


def call(name, kernel, operands, outs, scratch=(), loaded=()):
    vmem = pl.BlockSpec(memory_space=pltpu.VMEM)
    return pl.pallas_call(
        kernel,
        in_specs=[pl.BlockSpec(memory_space=pl.ANY)] * len(loaded) + [vmem] * len(operands),
        out_specs=[vmem] * (len(loaded) + len(outs)),
        out_shape=[jax.ShapeDtypeStruct(v.shape, v.dtype) for v in loaded]
        + [jax.ShapeDtypeStruct(*o) for o in outs],
        scratch_shapes=[pltpu.VMEM(*s) for s in scratch]
        + [pltpu.SemaphoreType.DMA((len(loaded),))] * bool(loaded),
        compiler_params=pltpu.CompilerParams(vmem_limit_bytes=16 << 20),
        cost_estimate=pl.CostEstimate(
            flops=int(COSTS[name] * 10**9) + 1, bytes_accessed=1, transcendentals=0
        ),
    )(*in_hbm(loaded), *operands)


def prepare_kernel(*refs):
    rows_ref, ins, refs = refs[0], refs[1:14], refs[14:]
    x_mine, c_send, c_mine, count_ref, small, wqkv, wo = refs[:7]
    held, sems = refs[7:18], refs[18]
    core, _, place = where_am_i()
    copies = [
        pltpu.make_async_copy(source, target, sems.at[i])
        for i, (source, target) in enumerate(zip(ins, held + (wqkv, wo)))
    ]
    for copy in copies:
        copy.start()
    for copy in copies[:11]:
        copy.wait()
    (
        mask_ref, x_ref, cot_ref, gain1, bias1, qv_bias, out_bias, gain2, bias2, down_bias, up_bias,
    ) = held
    piece = mask_ref.shape[1]
    diagonal = lax.broadcasted_iota(jnp.int32, (piece, piece), 0) == lax.broadcasted_iota(
        jnp.int32, (piece, piece), 1
    )
    rows = rows_ref[0, 0]

    def column(row):
        kept = mask_ref[pl.ds(row, 1), :].astype(SINGLE) * (row < rows).astype(SINGLE)
        return jnp.sum(jnp.where(diagonal, kept, 0.0), axis=1, keepdims=True), kept

    weight_send, kept_send = column(1 - place)
    c_send[...] = (cot_ref[1 - place].astype(SINGLE) * weight_send).astype(LOW)
    weight_mine, kept_mine = column(place)
    c_mine[...] = (cot_ref[place].astype(SINGLE) * weight_mine).astype(LOW)
    x_mine[...] = x_ref[place]
    count = jnp.sum(kept_mine + kept_send, axis=1, keepdims=True).astype(jnp.int32)
    lane = lax.broadcasted_iota(jnp.int32, count_ref.shape, 1) - core * DIGITS
    digit = lax.shift_right_logical(
        jnp.broadcast_to(count, count_ref.shape), jnp.clip(lane, 0, DIGITS - 1)
    )
    count_ref[...] = jnp.where((lane >= 0) & (lane < DIGITS), digit & 1, 0).astype(SINGLE)
    features = small.shape[1]
    small[12:16, :] = jnp.broadcast_to((place < rows).astype(SINGLE), (4, features))
    small[2:4, :] = qv_bias[...].astype(SINGLE)
    for line, value in ((0, gain1), (1, bias1), (4, out_bias), (5, gain2), (6, bias2), (7, down_bias)):
        small[line : line + 1, :] = value[...].astype(SINGLE)[None, :]
    ups = up_bias[...].astype(SINGLE)[None, :]
    for part in range(ups.shape[1] // features):
        small[8 + part : 9 + part, :] = ups[:, part * features : (part + 1) * features]
    for copy in copies[11:]:
        copy.wait()


def in_hbm(values):
    return [pltpu.with_memory_space_constraint(value, pltpu.HBM) for value in values]


def prepare(rows, mask, x, cot, vectors, weights):
    piece, features = cot.shape[1:]
    part = jax.ShapeDtypeStruct((piece, features), LOW)
    vmem = pl.BlockSpec(memory_space=pltpu.VMEM)
    held = (mask, x, cot, *vectors)
    return pl.pallas_call(
        prepare_kernel,
        in_specs=[pl.BlockSpec(memory_space=pltpu.SMEM)] + [pl.BlockSpec(memory_space=pl.ANY)] * 13,
        out_specs=[vmem] * 7,
        out_shape=[
            part,
            part,
            part,
            jax.ShapeDtypeStruct((1, 128), SINGLE),
            jax.ShapeDtypeStruct((16, features), SINGLE),
        ]
        + [jax.ShapeDtypeStruct(w.shape, w.dtype) for w in weights],
        scratch_shapes=[pltpu.VMEM(v.shape, v.dtype) for v in held]
        + [pltpu.SemaphoreType.DMA((13,))],
        compiler_params=pltpu.CompilerParams(vmem_limit_bytes=8 << 20),
        cost_estimate=pl.CostEstimate(flops=2 * 10**9, bytes_accessed=1, transcendentals=0),
    )(rows, *in_hbm(held), *in_hbm(weights))


def join_row(place, mine_ref, other_ref, row_ref):
    piece = mine_ref.shape[0]
    row_ref[rows_at(place * piece, piece), :] = mine_ref[...].astype(row_ref.dtype)
    row_ref[rows_at((1 - place) * piece, piece), :] = other_ref[...].astype(row_ref.dtype)


def attend_kernel(
    up_ref, down_ref, x_mine, x_other, small, wqkv, wo,
    up, down, n1, qkv, probs, mixed_low, middle, n2, heads_q, sems,
):
    _, _, place = where_am_i()
    copies = [
        pltpu.make_async_copy(up_ref, up, sems.at[0]),
        pltpu.make_async_copy(down_ref, down, sems.at[1]),
    ]
    for copy in copies:
        copy.start()
    length, features = n1.shape
    groups = features // GW
    join_row(place, x_mine, x_other, middle)
    normal, _ = normalize(middle[...])
    n1[...] = (normal * small[0:1, :] + small[1:2, :]).astype(LOW)
    for which in range(3):
        value = dot_nn(n1[...], wqkv[:, which * features : (which + 1) * features])
        if which != 1:
            line = 2 + which // 2
            value = value + small[line : line + 1, :]
        value = value.astype(LOW)
        for group in range(groups):
            qkv[which * groups + group] = value[:, group * GW : (group + 1) * GW]
    allowed = lax.broadcasted_iota(jnp.int32, (length, length), 0) >= lax.broadcasted_iota(
        jnp.int32, (length, length), 1
    )
    lanes = lax.broadcasted_iota(jnp.int32, (1, GW), 1)

    def one_group(group, carry):
        query, keys, values = (qkv[which * groups + group] for which in range(3))
        spread_heads(query, heads_q, HD**-0.5)
        parts = []
        for head in range(GROUP):
            cut = slice(head * length, (head + 1) * length)
            scores = jnp.where(allowed, dot_nt(heads_q[cut, :], keys), NEGATIVE)
            powers = jnp.exp(scores - jnp.max(scores, axis=-1, keepdims=True))
            low = (powers * (1.0 / jnp.sum(powers, axis=-1, keepdims=True))).astype(LOW)
            probs[group, cut, :] = low
            parts.append(low)
        mixed = dot_nn(parts[0], values)
        for head in range(1, GROUP):
            mixed = jnp.where(lanes >= head * HD, dot_nn(parts[head], values), mixed)
        mixed_low[:, rows_at(group * GW, GW)] = mixed.astype(LOW)
        return carry

    lax.fori_loop(0, groups, one_group, 0)
    middle[...] += dot_nn(mixed_low[...], wo[...]) + small[4:5, :]
    normal, _ = normalize(middle[...])
    n2[...] = (normal * small[5:6, :] + small[6:7, :]).astype(LOW)
    for copy in copies:
        copy.wait()


def attend(x_mine, x_other, small, qkv_weight, out_weight, up_weight, down_weight):
    piece, features = x_other.shape
    length = 2 * piece
    groups = features // GW
    act = ((length, features), LOW)
    return call(
        "attend",
        attend_kernel,
        (x_mine, x_other, small, qkv_weight, out_weight),
        [
            act,
            ((3 * groups, length, GW), LOW),
            ((groups, GROUP * length, length), LOW),
            act,
            ((length, features), SINGLE),
            act,
        ],
        [((GROUP * length, GW), LOW)],
        loaded=(up_weight, down_weight),
    )


def gelu_and_slope(u):
    c = math.sqrt(2 / math.pi)
    square = u * u
    bent = jnp.tanh(u * (c + (c * 0.044715) * square))
    half = 0.5 + 0.5 * bent
    slope = half + u * (0.5 - 0.5 * bent * bent) * (c + (3 * c * 0.044715) * square)
    return u * half, slope


def feed_tiles(side, n2, db2, small, up, down, g, du, vec, total):
    tiles, _, features = g.shape

    def one_tile(tile, carry):
        number = side * tiles + tile
        cut = rows_at(number * features, features)
        line = pl.ds(8 + number, 1)
        hidden = dot_nn(n2[...], up[:, cut]) + small[line, :]
        active, slope = gelu_and_slope(hidden)
        g[tile] = active.astype(LOW)
        grad = (dot_nt(db2[...], down[cut, :]) * slope).astype(LOW)
        du[tile] = grad
        vec[line, :] = jnp.sum(grad.astype(SINGLE), axis=0, keepdims=True)
        total[...] += dot_nt(grad, up[:, cut])
        return carry

    lax.fori_loop(0, tiles, one_tile, 0)


def feed_one_kernel(
    n2, c_mine, c_other, small, count, up, down, g, du, db2, theirs, dn, vec,
):
    core, _, place = where_am_i()
    half = theirs.shape[1]
    join_row(place, c_mine, c_other, db2)
    theirs[...] = db2[:, rows_at((1 - core) * half, half)]
    vec[...] = jnp.zeros_like(vec)
    vec[7:8, :] = jnp.sum(db2[...].astype(SINGLE), axis=0, keepdims=True)
    vec[12:13, 0:128] = count[...]
    dn[...] = jnp.zeros_like(dn)
    feed_tiles(1 - core, n2, db2, small, up, down, g, du, vec, dn)


def feed_one(n2, c_mine, c_other, small, count, up, down):
    length, features = n2.shape
    tiles = up.shape[1] // 2 // features
    hid = ((tiles, length, features), LOW)
    return call(
        "feed_one",
        feed_one_kernel,
        (n2, c_mine, c_other, small, count, up, down),
        [
            hid, hid, ((length, features), LOW), ((length, features // 2), LOW),
            ((length, features), SINGLE), ((16, features), SINGLE),
        ],
    )


def feed_two_kernel(
    n2, db2, small, up, down, middle, dn, vec_in, g, du, dm, db1, theirs, vec,
):
    core, _, _ = where_am_i()
    half = theirs.shape[1]
    vec[...] = vec_in[...]
    dm[...] = dn[...]
    feed_tiles(core, n2, db2, small, up, down, g, du, vec, dm)
    grad_n = dm[...]
    normal, inverse = normalize(middle[...])
    vec[5:6, :] = jnp.sum(grad_n * normal, axis=0, keepdims=True)
    vec[6:7, :] = jnp.sum(grad_n, axis=0, keepdims=True)
    grad = db2[...].astype(SINGLE) + norm_back(normal, inverse, grad_n, small[5:6, :])
    dm[...] = grad
    low = grad.astype(LOW)
    db1[...] = low
    theirs[...] = db1[:, rows_at((1 - core) * half, half)]
    vec[4:5, :] = jnp.sum(low.astype(SINGLE), axis=0, keepdims=True)


def feed_two(n2, db2, small, up, down, middle, dn, vec_in):
    length, features = n2.shape
    tiles = up.shape[1] // 2 // features
    hid = ((tiles, length, features), LOW)
    return call(
        "feed_two",
        feed_two_kernel,
        (n2, db2, small, up, down, middle, dn, vec_in),
        [
            hid, hid, ((length, features), SINGLE), ((length, features), LOW),
            ((length, features // 2), LOW), ((16, features), SINGLE),
        ],
    )


def result_kernel(g_mine, g_theirs, middle, small, down, x_grad_send, y_mine, send, total):
    core, _, place = where_am_i()
    tiles, _, features = g_mine.shape
    piece = y_mine.shape[0]
    total[...] = middle[...] + small[7:8, :]

    def one_tile(tile, carry):
        for side, active in ((core, g_mine), (1 - core, g_theirs)):
            cut = rows_at((side * tiles + tile) * features, features)
            total[...] += dot_nn(active[tile], down[cut, :])
        return carry

    lax.fori_loop(0, tiles, one_tile, 0)
    present = small[12:13, :]
    y_mine[...] = (total[rows_at(place * piece, piece), :] * present).astype(LOW)
    send[0] = (total[rows_at((1 - place) * piece, piece), :] * present).astype(LOW)
    send[1] = x_grad_send[...]


def result(g_mine, g_theirs, middle, small, down, x_grad_send):
    length, features = middle.shape
    piece = length // 2
    return call(
        "result",
        result_kernel,
        (g_mine, g_theirs, middle, small, down, x_grad_send),
        [((piece, features), LOW), ((2, piece, features), LOW)],
        [((length, features), SINGLE)],
    )


def back_kernel(
    qkv, probs, db1, wo, vec_in, theirs, mine, vec, dp, heads_q, heads_k, heads_g, side,
):
    core, _, _ = where_am_i()
    features = db1.shape[1]
    groups = features // GW
    vec[...] = vec_in[...]

    def one_group(group, carry):
        cut = rows_at(group * GW, GW)
        grad_mixed = dot_nt(db1[...], wo[cut, :]).astype(LOW)
        query, keys, values = (qkv[which * groups + group] for which in range(3))
        spread_heads(grad_mixed, heads_g)
        spread_heads(query, heads_q, HD**-0.5)
        spread_heads(keys, heads_k, HD**-0.5)
        weights = probs[group].astype(SINGLE)
        grad_probs = dot_nt(heads_g[...], values)
        inner = jnp.sum(weights * grad_probs, axis=-1, keepdims=True)
        grad_scores = (weights * (grad_probs - inner)).astype(LOW)
        side_by_side(grad_scores, side)
        dv = dot_tn(probs[group], heads_g[...])
        dk = dot_tn(grad_scores, heads_q[...])
        dq = dot_nn(side[...], heads_k[...])
        for which, value in enumerate((dq, dk, dv)):
            low = value.astype(LOW)
            dp[:, rows_at(which * features + group * GW, GW)] = low
            if which != 1:
                line = 2 + which // 2
                vec[line : line + 1, cut] = jnp.sum(low.astype(SINGLE), axis=0, keepdims=True)
        return carry

    lax.fori_loop(0, groups, one_group, 0)
    half = mine.shape[1]
    theirs[...] = dp[:, rows_at((1 - core) * half, half)]
    mine[...] = dp[:, rows_at(core * half, half)]


def back(qkv, probs, db1, out_weight, vec_in):
    length, features = db1.shape
    half = ((length, 3 * features // 2), LOW)
    return call(
        "back",
        back_kernel,
        (qkv, probs, db1, out_weight, vec_in),
        [half, half, ((16, features), SINGLE)],
        [((length, 3 * features), LOW)]
        + [((GROUP * length, GW), LOW)] * 3
        + [((length, GROUP * length), LOW)],
    )


def input_kernel(
    x_mine, x_other, small, dp_mine, dp_theirs, wqkv, dm, vec_in, mine, send, vec, row,
):
    core, _, place = where_am_i()
    half = dp_mine.shape[1]
    piece = mine.shape[0]
    grad_n = dot_nt(dp_mine[...], wqkv[:, rows_at(core * half, half)])
    grad_n = grad_n + dot_nt(dp_theirs[...], wqkv[:, rows_at((1 - core) * half, half)])
    join_row(place, x_mine, x_other, row)
    normal, inverse = normalize(row[...])
    vec[...] = vec_in[...]
    vec[0:1, :] = jnp.sum(grad_n * normal, axis=0, keepdims=True)
    vec[1:2, :] = jnp.sum(grad_n, axis=0, keepdims=True)
    row[...] = dm[...] + norm_back(normal, inverse, grad_n, small[0:1, :])
    mine[...] = row[rows_at(place * piece, piece), :].astype(LOW)
    send[...] = row[rows_at((1 - place) * piece, piece), :].astype(LOW)


def input_gradient(x_mine, x_other, small, dp_mine, dp_theirs, qkv_weight, dm, vec_in):
    piece, features = x_other.shape
    part = ((piece, features), LOW)
    return call(
        "input",
        input_kernel,
        (x_mine, x_other, small, dp_mine, dp_theirs, qkv_weight, dm, vec_in),
        [part, part, ((16, features), SINGLE)],
        [((2 * piece, features), SINGLE)],
    )


UNITS = 16


def unit_of(name, number):
    core, own, place = where_am_i()
    units = []
    for order in WAYS[name]:
        unit = 0
        for stage, axis in enumerate(order):
            if number >> (3 - stage) & 1:
                unit |= 1 if axis == "x" else BITS[axis] << 1
        units.append(unit)
    return jnp.where(core == 0, units[0], units[1]) ^ (own * 2 + place)


def lanes_kernel(
    g_mine, g_theirs, other_mine, other_theirs, right, right_other, send, keep, turned, whole, *, name
):
    core, _, _ = where_am_i()
    chunks, tall, wide = whole.shape
    tiles, length, features = g_mine.shape
    per_tile = features // wide
    half = tall // 2
    turned[:, :length] = right[:, rows_at(core * tall, tall)].T
    turned[:, length:] = right_other[...].T
    for side, one, two in ((core, g_mine, other_theirs), (1 - core, g_theirs, other_mine)):

        def one_tile(tile, carry, side=side, one=one, two=two):
            total = dot_nn(turned[:, :length], one[tile]) + dot_nn(turned[:, length:], two[tile])
            total = total.astype(LOW)
            for chunk in range(per_tile):
                whole[(side * tiles + tile) * per_tile + chunk] = total[:, chunk * wide : (chunk + 1) * wide]
            return carry

        lax.fori_loop(0, tiles, one_tile, 0)
    for number in range(UNITS):
        unit = unit_of(name, number)
        out = send if number >= UNITS // 2 else keep
        out[number % (UNITS // 2)] = whole[lax.div(unit, 2), rows_at(lax.rem(unit, 2) * half, half), :]


def grad_lanes(name, mine, theirs, other_mine, other_theirs, right, right_other):
    tiles, length, features = mine.shape
    tall = right_other.shape[1]
    chunks = UNITS // 2
    wide = 2 * tiles * features // chunks
    unit = ((UNITS // 2, tall // 2, wide), LOW)
    return call(
        "lanes",
        functools.partial(lanes_kernel, name=name),
        (mine, theirs, other_mine, other_theirs, right, right_other),
        [unit, unit],
        [((tall, 2 * length), LOW), ((chunks, tall, wide), LOW)],
    )


def rows_kernel(left, left_other, right, right_other, *rest, name, pick_core):
    if len(rest) > 4:
        vec, vec_other, send, keep, turned, whole, spread = rest
    else:
        send, keep, turned, whole = rest
        vec = None
    core, _, _ = where_am_i()
    length = left.shape[0]
    split = len(right_other.shape) == 2
    tiles, tile = (1, right_other.shape[1]) if split else (right_other.shape[0], right_other.shape[2])
    turned[:, :length] = left[...].T
    turned[:, length:] = left_other[...].T
    rows = turned.shape[0] // UNITS
    units = [unit_of(name, number) for number in range(UNITS)]
    if vec is not None:
        total = vec[...] + vec_other[...]
        features = total.shape[1]
        part = 2 * rows
        spread[...] = jnp.zeros_like(spread)
        for chunk in range(UNITS // 2):
            spread[2 * chunk, 0:8, :part] = total[0:8, chunk * part : (chunk + 1) * part]
            for piece in range(4):
                line, begin = divmod((4 * chunk + piece) * part, features)
                spread[2 * chunk + 1, piece : piece + 1, :part] = total[
                    8 + line : 9 + line, begin : begin + part
                ]
            spread[2 * chunk + 1, 4:5, : 2 * DIGITS] = total[12:13, : 2 * DIGITS]
        for out in (send, keep):
            out[:, rows:, :] = jnp.zeros_like(out[:, rows:, :])

    def one_tile(step, carry):
        if split:
            here = right[:, rows_at(core * tile, tile)] if pick_core else right[...]
            there = right_other[...]
        else:
            here, there = right[step], right_other[step]
        whole[...] = (dot_nn(turned[:, :length], here) + dot_nn(turned[:, length:], there)).astype(LOW)
        columns = rows_at(step * tile, tile)
        for number, unit in enumerate(units):
            out = send if number >= UNITS // 2 else keep
            out[number % (UNITS // 2), :rows, columns] = whole[rows_at(unit * rows, rows), :]
        return carry

    if tiles == 1:
        one_tile(0, 0)
    else:
        lax.fori_loop(0, tiles, one_tile, 0)
    if vec is not None:
        for number, unit in enumerate(units):
            out = send if number >= UNITS // 2 else keep
            out[number % (UNITS // 2), rows:, :128] = spread[unit].astype(LOW)


def grad_rows(name, left, left_other, right, right_other, pick_core=False, vecs=()):
    length, tall = left.shape
    rows = tall // UNITS
    tile = right_other.shape[-1]
    width = math.prod(right_other.shape) // length
    unit = ((UNITS // 2, rows + (16 if vecs else 0), width), LOW)
    return call(
        "rows_" + name,
        functools.partial(rows_kernel, name=name, pick_core=pick_core),
        (left, left_other, right, right_other, *vecs),
        [unit, unit],
        [((tall, 2 * length), LOW), ((tall, tile), LOW)] + [((UNITS, 16, 128), SINGLE)] * bool(vecs),
    )


FIRST = ("o", "q", "d", "u")


PACK = 384


def packed_rows(name, shape):
    tall, width = shape
    return (tall - 16 if name == "o" else tall) * (width // PACK)


def pack_kernel(*refs):
    out = refs[-1]
    first = 0
    for number, part in enumerate(refs[:-1]):
        name = FIRST[number // 2]
        tall = part.shape[0] - (16 if name == "o" else 0)
        for block in range(part.shape[1] // PACK):
            out[first : first + tall, :] = part[:tall, block * PACK : (block + 1) * PACK]
            first += tall


def pack(parts):
    operands = [p for name in FIRST for p in parts[name]]
    rows = sum(packed_rows(name, p.shape) for name in FIRST for p in parts[name])
    return call("result", pack_kernel, operands, [((rows, PACK), LOW)])[0]


def finale_kernel(*refs):
    homes, theirs, refs = refs[:3], refs[3], refs[4:]
    parts = {name: refs[2 * i : 2 * i + 2] for i, name in enumerate(FIRST)}
    refs = refs[2 * len(FIRST) :]
    count = (len(refs) - 3) // 2
    results, held = refs[:count], refs[count : 2 * count]
    vec, turned, sems = refs[2 * count :]
    core, _, place = where_am_i()
    copies = []

    def send(*numbers):
        for number in numbers:
            copies.append(pltpu.make_async_copy(held[number], results[number], sems.at[number]))
            copies[-1].start()

    for number in (0, 1):
        held[number][place] = homes[number][...]
        held[number][1 - place] = homes[2][number]
    send(0, 1)
    mine, other = parts["o"][:2]
    half = mine.shape[0] - 16
    vec[rows_at(place * 8, 8), :] = mine[half:, :128].astype(SINGLE)[:8]
    vec[rows_at((1 - place) * 8, 8), :] = other[half:, :128].astype(SINGLE)[:8]
    line = vec[12:13, :]
    lane = lax.broadcasted_iota(jnp.int32, line.shape, 1)
    worth = lax.shift_left(jnp.ones_like(lane), lax.rem(lane, DIGITS)).astype(SINGLE)
    first, second = (
        jnp.sum(jnp.where(lane // DIGITS == side, line * worth, 0.0), axis=1, keepdims=True)
        for side in (0, 1)
    )
    total = first + second
    share = 1.0 / total
    first_row = 0
    for number, name in enumerate(FIRST):
        out = held[2 + number]
        tall, width = parts[name][0].shape
        tall = tall - 16 if name == "o" else tall
        for spot in range(4):
            side, low = core ^ (spot >> 1), place ^ (spot & 1)
            for block in range(width // PACK):
                if spot < 2:
                    piece = parts[name][spot][:tall, block * PACK : (block + 1) * PACK]
                else:
                    piece = theirs[first_row : first_row + tall, :]
                    first_row += tall
                piece = piece.astype(SINGLE)
                if name == "d":
                    turned[rows_at((side * 2 + low) * tall, tall), :] = piece
                else:
                    column = pl.multiple_of(side * width + block * PACK, 128)
                    out[rows_at(low * tall, tall), pl.ds(column, PACK)] = piece * share
        if name == "d":
            out[...] = turned[...].T * share
        send(2 + number)
    counts, up, qv, *plain = held[2 + len(FIRST) :]
    spot = lax.broadcasted_iota(jnp.int32, (1, 128), 1)
    counts[...] = jnp.where(spot == 0, first, second).astype(jnp.int32)[0, : counts.shape[0]]
    width = qv.shape[1]
    scaled = vec[...] * share
    qv[...] = scaled[2:4, :width]
    for number, out in zip((0, 1, 4, 5, 6, 7), plain):
        out[...] = scaled[number, :width]
    up[...] = jnp.concatenate([scaled[8 + part : 9 + part, :width] for part in range(4)], axis=1)[0]
    send(*range(2 + len(FIRST), count))
    for copy in copies:
        copy.wait()


def finale(homes, theirs, parts, rows):
    piece, features = homes[0].shape
    home = jax.ShapeDtypeStruct((2, piece, features), LOW)
    results = [home, home]
    for name in FIRST:
        tall, width = parts[name][0].shape
        shape = (width, 4 * tall) if name == "d" else (2 * rows, 2 * width)
        results.append(jax.ShapeDtypeStruct(shape, SINGLE))
    chunk = 2 * rows
    results += [
        jax.ShapeDtypeStruct((2,), jnp.int32),
        jax.ShapeDtypeStruct((4 * chunk,), SINGLE),
        jax.ShapeDtypeStruct((2, chunk), SINGLE),
    ] + [jax.ShapeDtypeStruct((chunk,), SINGLE)] * 6
    vmem = pl.BlockSpec(memory_space=pltpu.VMEM)
    tall, width = parts["d"][0].shape
    operands = [*homes, theirs, *[p for name in FIRST for p in parts[name]]]
    return pl.pallas_call(
        finale_kernel,
        in_specs=[vmem] * len(operands),
        out_specs=[pl.BlockSpec(memory_space=pl.ANY)] * len(results),
        out_shape=results,
        scratch_shapes=[pltpu.VMEM(r.shape, r.dtype) for r in results]
        + [
            pltpu.VMEM((16, 128), SINGLE),
            pltpu.VMEM((4 * tall, width), SINGLE),
            pltpu.SemaphoreType.DMA((len(results),)),
        ],
        compiler_params=pltpu.CompilerParams(vmem_limit_bytes=16 << 20),
        cost_estimate=pl.CostEstimate(flops=1, bytes_accessed=1, transcendentals=0),
    )(*operands)


def swap_pairs(size, bit):
    return [(i, i ^ bit) for i in range(size)]


def partners(name, stage, groups):
    pairs = []
    for core in range(2):
        axis = WAYS[name][core][stage]
        for own in range(groups):
            for place in range(2):
                to = (own, place ^ 1) if axis == "x" else (own ^ BITS[axis], place)
                pairs.append(((core * groups + own) * 2 + place, (core * groups + to[0]) * 2 + to[1]))
    return pairs


def added(one, two):
    return (one.astype(SINGLE) + two.astype(SINGLE)).astype(LOW)


class Order:
    def __init__(self):
        self.last = None

    def tie(self, value):
        if self.last is not None:
            value, _ = lax.optimization_barrier((value, self.last))
        return value

    def mark(self, value):
        self.last = value


class Sum:
    def __init__(self, order, name, groups, send, keep):
        self.order, self.name, self.groups = order, name, groups
        self.keep = keep
        self.stage = 0
        self.whole_last = all(way[3] == "x" for way in WAYS[name])
        self.parts = None
        self.go(send)

    def go(self, send):
        self.flying = lax.ppermute(send, AXES, partners(self.name, self.stage, self.groups))

    def step(self):
        if self.parts is not None:
            return
        other = self.order.tie(self.flying)
        keep = self.keep
        self.stage += 1
        if self.stage == 5:
            self.order.mark(other)
            self.parts = [self.total, other]
        elif self.stage == 4 and self.whole_last:
            self.parts = [added(keep[0], other[1]), added(keep[1], other[0])]
            self.order.mark(self.parts[0])
        elif self.stage == 4:
            self.total = added(keep[0], other[0])
            self.order.mark(self.total)
            self.flying = lax.ppermute(self.total, "seq", swap_pairs(2, 1))
        elif self.stage == 3 and self.whole_last:
            self.keep = added(keep, other)
            self.order.mark(self.keep)
            self.go(self.keep)
        else:
            half = keep.shape[0] // 2
            send = added(keep[half:], other[half:])
            self.keep = added(keep[:half], other[:half])
            self.order.mark(send)
            self.go(send)


def body_fast(
    inputs,
    cotangent,
    row_counts,
    response_mask,
    norm1_gain,
    norm1_bias,
    qkv_weight,
    qv_bias,
    out_weight,
    out_bias,
    norm2_gain,
    norm2_bias,
    up_weight,
    up_bias,
    down_weight,
    down_bias,
):
    groups = lax.axis_size("dp")
    pair = swap_pairs(2, 1)
    core, own, place = (lax.axis_index(a) for a in ("src", "dp", "seq"))
    x_both = inputs[0, 0]
    x_other = lax.ppermute(
        lax.dynamic_index_in_dim(x_both, 1 - place, 0, keepdims=False), "seq", pair
    )
    x_mine, c_send, c_mine, count, small, qkv_weight, out_weight = prepare(
        row_counts,
        response_mask[0, 0],
        x_both,
        cotangent[0, 0],
        (norm1_gain, norm1_bias, qv_bias, out_bias, norm2_gain, norm2_bias, down_bias, up_bias),
        (qkv_weight, out_weight),
    )
    c_other = lax.ppermute(c_send, "seq", pair)
    order = Order()

    def from_core(value):
        return lax.ppermute(value, "src", pair)

    up_weight, down_weight, n1, qkv, probs, mixed, middle, n2 = attend(
        x_mine, x_other, small, qkv_weight, out_weight, up_weight, down_weight
    )
    g_theirs, du_theirs, db2, db2_theirs, dn, vec = feed_one(
        n2, c_mine, c_other, small, count, up_weight, down_weight
    )
    order.mark(vec)
    n2_other, n1_other, mixed_other = order.tie(
        (from_core(n2), from_core(n1), from_core(mixed))
    )
    here, n2_other, n1_other, mixed_other = lax.optimization_barrier(
        (n2, n2_other, n1_other, mixed_other)
    )
    g_mine, du_mine, dm, db1, db1_theirs, vec = feed_two(
        here, db2, small, up_weight, down_weight, middle, dn, vec
    )
    order.mark(vec)
    du_other, db2_other, other_theirs = order.tie(
        (from_core(du_theirs), from_core(db2_theirs), from_core(g_theirs))
    )
    here, du_other, db2_other, other_theirs = lax.optimization_barrier(
        (n2, du_other, db2_other, other_theirs)
    )
    other_mine, db1_other = from_core(g_mine), from_core(db1_theirs)

    sums = {}
    for event in EVENTS:
        if event == "h":
            homes = lax.ppermute(order.tie(home_send), "seq", pair)
            continue
        if event == "i":
            homes = order.tie(homes)
            order.mark(homes)
            continue
        if event.islower():
            sums[event].step()
            continue
        name = event.lower()
        if event == "U":
            parts = grad_rows(name, order.tie(here), n2_other, du_mine, du_other)
        elif event == "D":
            other_mine = order.tie(other_mine)
            here, other_mine = lax.optimization_barrier((g_mine, other_mine))
            parts = grad_lanes(name, here, g_theirs, other_mine, other_theirs, db2, db2_other)
        elif event == "C":
            here = order.tie(qkv)
            dp_theirs, dp_mine, vec = back(here, probs, db1, out_weight, vec)
            dp_other = from_core(dp_theirs)
            order.mark(vec)
            continue
        elif event == "I":
            x_grad_mine, x_grad_send, vec = input_gradient(
                order.tie(x_mine), x_other, small, dp_mine, dp_theirs, qkv_weight, dm, vec
            )
            vec_other = from_core(vec)
            order.mark(vec)
            continue
        elif event == "Y":
            y_mine, home_send = result(
                order.tie(g_mine), g_theirs, middle, small, down_weight, x_grad_send
            )
            order.mark(home_send)
            continue
        elif event == "O":
            parts = grad_rows(
                name, order.tie(mixed), mixed_other, db1, db1_other, True, (vec, vec_other)
            )
        else:
            dp_other, db1_other = order.tie((dp_other, db1_other))
            here, dp_other, db1_other = lax.optimization_barrier((n1, dp_other, db1_other))
            parts = grad_rows(name, here, n1_other, dp_mine, dp_other)
        order.mark(parts[0])
        sums[name] = Sum(order, name, groups, *parts)

    parts = order.tie({name: sums[name].parts for name in FIRST})
    rows = out_weight.shape[0] // groups // 2
    output, input_grad, out, qkv, down, up, counts, up_small, qv, *plain = finale(
        (y_mine, x_grad_mine, homes), from_core(pack(parts)), parts, rows
    )
    return (
        output[None, None],
        input_grad[None, None],
        counts,
        plain[0],
        plain[1],
        qkv,
        qv,
        out,
        plain[2],
        plain[3],
        plain[4],
        up,
        up_small,
        down,
        plain[5],
    )


def solution(mesh):
    placed = (
        P("src", "dp", None, "seq", None),
        P("src", "dp", None, "seq", None),
        P("src", "dp"),
        P("src", "dp", None, "seq"),
        P(),
        P(),
        P(),
        P(),
        P(),
        P(),
        P(),
        P(),
        P(),
        P(),
        P(),
        P(),
    )
    sizes = dict(mesh.shape)
    paired = sizes["src"] == 2 and sizes["seq"] == 2 and sizes["dp"] == 8
    return jax.shard_map(
        body_fast if paired else body_generic,
        mesh=mesh,
        in_specs=placed,
        out_specs=(
            P("src", "dp", None, "seq", None),
            P("src", "dp", None, "seq", None),
            P(),
            P("dp"),
            P("dp"),
            P("dp", None),
            P(None, "dp"),
            P("dp", None),
            P("dp"),
            P("dp"),
            P("dp"),
            P("dp", None),
            P("dp"),
            P("dp", None),
            P("dp"),
        ),
        check_vma=False,
    )
```

```python
import functools
import math

import jax
import jax.numpy as jnp
from jax import lax
from jax.experimental import pallas as pl
from jax.experimental.pallas import tpu as pltpu
from jax.sharding import PartitionSpec as P

H = 12
HD = 64


EPS = 1e-05
NEGATIVE = -1e30


def norm_apply(values, scaling, offset):
    centre = jnp.mean(values, axis=-1, keepdims=True)
    centered = values - centre
    spread = jnp.mean(centered * centered, axis=-1, keepdims=True)
    return centered * lax.rsqrt(spread + EPS) * scaling + offset


def causal_scores(query_part, keys_part, allowed):
    scores = jnp.einsum(
        "rqhd,rkhd->rhqk", query_part, keys_part, preferred_element_type=jnp.float32
    )
    scores = scores * HD ** (-0.5)
    return jnp.where(allowed, scores, NEGATIVE)


def attend_forward(query_part, keys_part, values_part, allowed):
    scores = causal_scores(query_part, keys_part, allowed)
    highest = jnp.max(scores, axis=-1, keepdims=True)
    powers = jnp.exp(scores - highest)
    totals = jnp.sum(powers, axis=-1, keepdims=True)
    probs_low = (powers / totals).astype(jnp.bfloat16)
    mixed = jnp.einsum(
        "rhqk,rkhd->rqhd", probs_low, values_part, preferred_element_type=jnp.float32
    )
    return (mixed, highest, totals)


def attend_backward(query_part, keys_part, values_part, grad_part, highest, totals, allowed):
    scores = causal_scores(query_part, keys_part, allowed)
    probs = jnp.exp(scores - highest) / totals
    probs_low = probs.astype(jnp.bfloat16)
    grad_probs = jnp.einsum(
        "rqhd,rkhd->rhqk", grad_part, values_part, preferred_element_type=jnp.float32
    )
    inner = jnp.sum(probs * grad_probs, axis=-1, keepdims=True)
    grad_scores = (probs * (grad_probs - inner)).astype(jnp.bfloat16)
    factor = HD ** (-0.5)
    grad_query = (
        jnp.einsum("rhqk,rkhd->rqhd", grad_scores, keys_part, preferred_element_type=jnp.float32)
        * factor
    )
    grad_keys = (
        jnp.einsum("rhqk,rqhd->rkhd", grad_scores, query_part, preferred_element_type=jnp.float32)
        * factor
    )
    grad_values = jnp.einsum(
        "rhqk,rqhd->rkhd", probs_low, grad_part, preferred_element_type=jnp.float32
    )
    return (grad_query, grad_keys, grad_values)


def body_generic(
    inputs,
    cotangent,
    row_counts,
    response_mask,
    norm1_gain,
    norm1_bias,
    qkv_weight,
    qv_bias,
    out_weight,
    out_bias,
    norm2_gain,
    norm2_bias,
    up_weight,
    up_bias,
    down_weight,
    down_bias,
):
    slots = inputs.shape[2]
    piece_len = inputs.shape[3]
    features = inputs.shape[4]
    tokens = slots * piece_len
    blocks_seq = lax.axis_size("seq")
    row_len = piece_len * blocks_seq
    group_heads = math.gcd(H, 4)
    bfloat = jnp.bfloat16
    single = jnp.float32
    present_int = (jnp.arange(slots) < row_counts[0, 0]).astype(jnp.int32)
    weight = (response_mask[0, 0] * present_int[:, None]).astype(single)
    local_count = jnp.sum(response_mask[0, 0] * present_int[:, None])
    picked = jnp.where(jnp.arange(lax.axis_size("src")) == lax.axis_index("src"), local_count, 0)
    source_counts = lax.psum(picked, ("src", "dp", "seq"))
    whole = jnp.sum(source_counts).astype(single)
    source = inputs.reshape(tokens, features).astype(single)
    normed, norm1_pull = jax.vjp(
        norm_apply, source, norm1_gain.astype(single), norm1_bias.astype(single)
    )
    normed_low = normed.astype(bfloat)
    bias_query = qv_bias[0].astype(single)
    joined = jnp.concatenate([bias_query, jnp.zeros_like(bias_query), qv_bias[1].astype(single)])
    projected = jnp.dot(normed_low, qkv_weight, preferred_element_type=single) + joined
    proj_low = projected.astype(bfloat)
    query = proj_low[:, :features].reshape(slots, piece_len, H, HD)
    keys_own = proj_low[:, features : 2 * features].reshape(slots, piece_len, features)
    values_own = proj_low[:, 2 * features :].reshape(slots, piece_len, features)
    keys_all, values_all = (
        lax.all_gather(keys_own, "seq", axis=1, tiled=True),
        lax.all_gather(values_own, "seq", axis=1, tiled=True),
    )
    query_pos = lax.axis_index("seq") * piece_len + jnp.arange(piece_len)
    allowed = query_pos[:, None] >= jnp.arange(row_len)[None, :]
    keys_heads = keys_all.reshape(slots, row_len, H, HD)
    values_heads = values_all.reshape(slots, row_len, H, HD)
    mixed_parts = []
    kept_stats = []
    for group in range(H // group_heads):
        first = group * group_heads
        last = first + group_heads
        mixed, highest, totals = attend_forward(
            query[:, :, first:last],
            keys_heads[:, :, first:last],
            values_heads[:, :, first:last],
            allowed,
        )
        mixed_parts.append(mixed)
        kept_stats.append((highest, totals))
    attended = jnp.concatenate(mixed_parts, axis=2).reshape(tokens, features)
    attended_low = attended.astype(bfloat)
    branch = jnp.dot(attended_low, out_weight, preferred_element_type=single) + out_bias.astype(
        single
    )
    middle = source + branch
    normed_two, norm2_pull = jax.vjp(
        norm_apply, middle, norm2_gain.astype(single), norm2_bias.astype(single)
    )
    normed_two_low = normed_two.astype(bfloat)
    hidden = jnp.dot(normed_two_low, up_weight, preferred_element_type=single) + up_bias.astype(
        single
    )
    active, gelu_pull = jax.vjp(functools.partial(jax.nn.gelu, approximate=True), hidden)
    active_low = active.astype(bfloat)
    branch_two = jnp.dot(active_low, down_weight, preferred_element_type=single) + down_bias.astype(
        single
    )
    result = middle + branch_two
    present_tok = jnp.repeat(present_int.astype(single), piece_len)
    output = (result * present_tok[:, None]).astype(bfloat).reshape(inputs.shape)
    incoming = cotangent.reshape(tokens, features).astype(single) * weight.reshape(tokens)[:, None]
    grad_branch_two = incoming.astype(bfloat)
    grad_down_weight = jnp.einsum(
        "tf,td->fd", active_low, grad_branch_two, preferred_element_type=single
    )
    grad_down_bias = jnp.sum(grad_branch_two.astype(single), axis=0)
    grad_active = jnp.einsum(
        "td,fd->tf", grad_branch_two, down_weight, preferred_element_type=single
    )
    grad_hidden = gelu_pull(grad_active)[0].astype(bfloat)
    grad_up_weight = jnp.einsum(
        "tm,tf->mf", normed_two_low, grad_hidden, preferred_element_type=single
    )
    grad_up_bias = jnp.sum(grad_hidden.astype(single), axis=0)
    grad_normed_two = jnp.einsum("tf,mf->tm", grad_hidden, up_weight, preferred_element_type=single)
    grad_mid_norm, grad_norm2_gain, grad_norm2_bias = norm2_pull(grad_normed_two)
    grad_middle = incoming + grad_mid_norm
    grad_branch = grad_middle.astype(bfloat)
    grad_out_weight = jnp.einsum(
        "tm,td->md", attended_low, grad_branch, preferred_element_type=single
    )
    grad_out_bias = jnp.sum(grad_branch.astype(single), axis=0)
    grad_attended = jnp.einsum("td,md->tm", grad_branch, out_weight, preferred_element_type=single)
    grad_heads = grad_attended.astype(bfloat).reshape(slots, piece_len, H, HD)
    query_grads = []
    key_grads = []
    value_grads = []
    for group in range(H // group_heads):
        first = group * group_heads
        last = first + group_heads
        highest, totals = kept_stats[group]
        grad_query, grad_keys, grad_values = attend_backward(
            query[:, :, first:last],
            keys_heads[:, :, first:last],
            values_heads[:, :, first:last],
            grad_heads[:, :, first:last],
            highest,
            totals,
            allowed,
        )
        query_grads.append(grad_query)
        key_grads.append(grad_keys)
        value_grads.append(grad_values)
    grad_query_all = jnp.concatenate(query_grads, axis=2).reshape(tokens, features)
    grad_keys_all = jnp.concatenate(key_grads, axis=2).reshape(slots, row_len, features)
    grad_values_all = jnp.concatenate(value_grads, axis=2).reshape(slots, row_len, features)
    grad_keys_own, grad_values_own = (
        lax.psum_scatter(
            grad_keys_all.astype(jnp.bfloat16), "seq", scatter_dimension=1, tiled=True
        ).astype(jnp.float32),
        lax.psum_scatter(
            grad_values_all.astype(jnp.bfloat16), "seq", scatter_dimension=1, tiled=True
        ).astype(jnp.float32),
    )
    grad_projected = jnp.concatenate(
        [
            grad_query_all,
            grad_keys_own.reshape(tokens, features),
            grad_values_own.reshape(tokens, features),
        ],
        axis=1,
    ).astype(bfloat)
    grad_qkv_weight = jnp.einsum(
        "tm,tn->mn", normed_low, grad_projected, preferred_element_type=single
    )
    column_sums = jnp.sum(grad_projected.astype(single), axis=0)
    grad_qv_bias = jnp.stack([column_sums[:features], column_sums[2 * features :]])
    grad_normed = jnp.einsum("tn,mn->tm", grad_projected, qkv_weight, preferred_element_type=single)
    grad_src_norm, grad_norm1_gain, grad_norm1_bias = norm1_pull(grad_normed)
    input_grad = (grad_middle + grad_src_norm).astype(bfloat).reshape(inputs.shape)
    grads = (
        grad_norm1_gain,
        grad_norm1_bias,
        grad_qkv_weight,
        grad_qv_bias,
        grad_out_weight,
        grad_out_bias,
        grad_norm2_gain,
        grad_norm2_bias,
        grad_up_weight,
        grad_up_bias,
        grad_down_weight,
        grad_down_bias,
    )
    summed = (
        lax.psum_scatter(
            grads[0].astype(jnp.bfloat16), "dp", scatter_dimension=0, tiled=True
        ).astype(jnp.float32),
        lax.psum_scatter(
            grads[1].astype(jnp.bfloat16), "dp", scatter_dimension=0, tiled=True
        ).astype(jnp.float32),
        lax.psum_scatter(
            grads[2].astype(jnp.bfloat16), "dp", scatter_dimension=0, tiled=True
        ).astype(jnp.float32),
        lax.psum_scatter(
            grads[3].astype(jnp.bfloat16), "dp", scatter_dimension=1, tiled=True
        ).astype(jnp.float32),
        lax.psum_scatter(
            grads[4].astype(jnp.bfloat16), "dp", scatter_dimension=0, tiled=True
        ).astype(jnp.float32),
        lax.psum_scatter(
            grads[5].astype(jnp.bfloat16), "dp", scatter_dimension=0, tiled=True
        ).astype(jnp.float32),
        lax.psum_scatter(
            grads[6].astype(jnp.bfloat16), "dp", scatter_dimension=0, tiled=True
        ).astype(jnp.float32),
        lax.psum_scatter(
            grads[7].astype(jnp.bfloat16), "dp", scatter_dimension=0, tiled=True
        ).astype(jnp.float32),
        lax.psum_scatter(
            grads[8].astype(jnp.bfloat16), "dp", scatter_dimension=0, tiled=True
        ).astype(jnp.float32),
        lax.psum_scatter(
            grads[9].astype(jnp.bfloat16), "dp", scatter_dimension=0, tiled=True
        ).astype(jnp.float32),
        lax.psum_scatter(
            grads[10].astype(jnp.bfloat16), "dp", scatter_dimension=0, tiled=True
        ).astype(jnp.float32),
        lax.psum_scatter(
            grads[11].astype(jnp.bfloat16), "dp", scatter_dimension=0, tiled=True
        ).astype(jnp.float32),
    )
    summed = (
        lax.psum(summed[0].astype(jnp.bfloat16), ("src", "seq")).astype(jnp.float32),
        lax.psum(summed[1].astype(jnp.bfloat16), ("src", "seq")).astype(jnp.float32),
        lax.psum(summed[2].astype(jnp.bfloat16), ("src", "seq")).astype(jnp.float32),
        lax.psum(summed[3].astype(jnp.bfloat16), ("src", "seq")).astype(jnp.float32),
        lax.psum(summed[4].astype(jnp.bfloat16), ("src", "seq")).astype(jnp.float32),
        lax.psum(summed[5].astype(jnp.bfloat16), ("src", "seq")).astype(jnp.float32),
        lax.psum(summed[6].astype(jnp.bfloat16), ("src", "seq")).astype(jnp.float32),
        lax.psum(summed[7].astype(jnp.bfloat16), ("src", "seq")).astype(jnp.float32),
        lax.psum(summed[8].astype(jnp.bfloat16), ("src", "seq")).astype(jnp.float32),
        lax.psum(summed[9].astype(jnp.bfloat16), ("src", "seq")).astype(jnp.float32),
        lax.psum(summed[10].astype(jnp.bfloat16), ("src", "seq")).astype(jnp.float32),
        lax.psum(summed[11].astype(jnp.bfloat16), ("src", "seq")).astype(jnp.float32),
    )
    final = [g / whole for g in summed]
    return (
        output,
        input_grad,
        source_counts,
        final[0],
        final[1],
        final[2],
        final[3],
        final[4],
        final[5],
        final[6],
        final[7],
        final[8],
        final[9],
        final[10],
        final[11],
    )


WAYS = {
    "u": ("yx12", "12yx"),
    "d": ("xy12", "1yx2"),
    "o": ("yx12", "yx12"),
    "q": ("x1y2", "yx12"),
}
EVENTS = "UDCIOQYudoqudqohudqoduoqiduoq"
BITS = {"y": 1, "1": 2, "2": 4}


COSTS = {"prepare": 2, "load": 4, "attend": 8, "feed_one": 5, "feed_two": 5, "back": 0, "input": 0, "lanes": 0, "rows_u": 4, "rows_q": 0, "rows_o": 0, "result": 0}
AXES = ("src", "dp", "seq")
SINGLE = jnp.float32
LOW = jnp.bfloat16
GROUP = 4
GW = GROUP * HD
DIGITS = 16


def dot_nt(left, right):
    return lax.dot_general(left, right, (((1,), (1,)), ((), ())), preferred_element_type=SINGLE)


def dot_tn(left, right):
    return lax.dot_general(left, right, (((0,), (0,)), ((), ())), preferred_element_type=SINGLE)


def dot_nn(left, right):
    return jnp.dot(left, right, preferred_element_type=SINGLE)


def normalize(values):
    centered = values - jnp.mean(values, axis=-1, keepdims=True)
    inverse = lax.rsqrt(jnp.mean(centered * centered, axis=-1, keepdims=True) + EPS)
    return centered * inverse, inverse


def norm_back(normal, inverse, grad, gain):
    scaled = grad * gain
    return inverse * (
        scaled
        - jnp.mean(scaled, axis=-1, keepdims=True)
        - normal * jnp.mean(scaled * normal, axis=-1, keepdims=True)
    )


def spread_heads(value, out, scale=1.0):
    length = value.shape[0]
    lanes = lax.broadcasted_iota(jnp.int32, (1, GW), 1)
    for head in range(GROUP):
        keep = jnp.where((lanes >= head * HD) & (lanes < (head + 1) * HD), scale, 0.0).astype(LOW)
        out[head * length : (head + 1) * length, :] = value * keep


def side_by_side(stacked, out):
    length = out.shape[0]
    for head in range(GROUP):
        out[:, head * length : (head + 1) * length] = stacked[head * length : (head + 1) * length, :]


def rows_at(first, count):
    return pl.ds(pl.multiple_of(first, count), count)


def where_am_i():
    return tuple(lax.axis_index(axis) for axis in AXES)


def call(name, kernel, operands, outs, scratch=(), loaded=()):
    vmem = pl.BlockSpec(memory_space=pltpu.VMEM)
    return pl.pallas_call(
        kernel,
        in_specs=[pl.BlockSpec(memory_space=pl.ANY)] * len(loaded) + [vmem] * len(operands),
        out_specs=[vmem] * (len(loaded) + len(outs)),
        out_shape=[jax.ShapeDtypeStruct(v.shape, v.dtype) for v in loaded]
        + [jax.ShapeDtypeStruct(*o) for o in outs],
        scratch_shapes=[pltpu.VMEM(*s) for s in scratch]
        + [pltpu.SemaphoreType.DMA((len(loaded),))] * bool(loaded),
        compiler_params=pltpu.CompilerParams(vmem_limit_bytes=16 << 20),
        cost_estimate=pl.CostEstimate(
            flops=int(COSTS[name] * 10**9) + 1, bytes_accessed=1, transcendentals=0
        ),
    )(*in_hbm(loaded), *operands)


def prepare_kernel(*refs):
    rows_ref, ins, refs = refs[0], refs[1:14], refs[14:]
    x_mine, c_send, c_mine, count_ref, small, wqkv, wo = refs[:7]
    held, sems = refs[7:18], refs[18]
    core, _, place = where_am_i()
    copies = [
        pltpu.make_async_copy(source, target, sems.at[i])
        for i, (source, target) in enumerate(zip(ins, held + (wqkv, wo)))
    ]
    for copy in copies:
        copy.start()
    for copy in copies[:11]:
        copy.wait()
    (
        mask_ref, x_ref, cot_ref, gain1, bias1, qv_bias, out_bias, gain2, bias2, down_bias, up_bias,
    ) = held
    piece = mask_ref.shape[1]
    diagonal = lax.broadcasted_iota(jnp.int32, (piece, piece), 0) == lax.broadcasted_iota(
        jnp.int32, (piece, piece), 1
    )
    rows = rows_ref[0, 0]

    def column(row):
        kept = mask_ref[pl.ds(row, 1), :].astype(SINGLE) * (row < rows).astype(SINGLE)
        return jnp.sum(jnp.where(diagonal, kept, 0.0), axis=1, keepdims=True), kept

    weight_send, kept_send = column(1 - place)
    c_send[...] = (cot_ref[1 - place].astype(SINGLE) * weight_send).astype(LOW)
    weight_mine, kept_mine = column(place)
    c_mine[...] = (cot_ref[place].astype(SINGLE) * weight_mine).astype(LOW)
    x_mine[...] = x_ref[place]
    count = jnp.sum(kept_mine + kept_send, axis=1, keepdims=True).astype(jnp.int32)
    lane = lax.broadcasted_iota(jnp.int32, count_ref.shape, 1) - core * DIGITS
    digit = lax.shift_right_logical(
        jnp.broadcast_to(count, count_ref.shape), jnp.clip(lane, 0, DIGITS - 1)
    )
    count_ref[...] = jnp.where((lane >= 0) & (lane < DIGITS), digit & 1, 0).astype(SINGLE)
    features = small.shape[1]
    small[12:16, :] = jnp.broadcast_to((place < rows).astype(SINGLE), (4, features))
    small[2:4, :] = qv_bias[...].astype(SINGLE)
    for line, value in ((0, gain1), (1, bias1), (4, out_bias), (5, gain2), (6, bias2), (7, down_bias)):
        small[line : line + 1, :] = value[...].astype(SINGLE)[None, :]
    ups = up_bias[...].astype(SINGLE)[None, :]
    for part in range(ups.shape[1] // features):
        small[8 + part : 9 + part, :] = ups[:, part * features : (part + 1) * features]
    for copy in copies[11:]:
        copy.wait()


def in_hbm(values):
    return [pltpu.with_memory_space_constraint(value, pltpu.HBM) for value in values]


def prepare(rows, mask, x, cot, vectors, weights):
    piece, features = cot.shape[1:]
    part = jax.ShapeDtypeStruct((piece, features), LOW)
    vmem = pl.BlockSpec(memory_space=pltpu.VMEM)
    held = (mask, x, cot, *vectors)
    return pl.pallas_call(
        prepare_kernel,
        in_specs=[pl.BlockSpec(memory_space=pltpu.SMEM)] + [pl.BlockSpec(memory_space=pl.ANY)] * 13,
        out_specs=[vmem] * 7,
        out_shape=[
            part,
            part,
            part,
            jax.ShapeDtypeStruct((1, 128), SINGLE),
            jax.ShapeDtypeStruct((16, features), SINGLE),
        ]
        + [jax.ShapeDtypeStruct(w.shape, w.dtype) for w in weights],
        scratch_shapes=[pltpu.VMEM(v.shape, v.dtype) for v in held]
        + [pltpu.SemaphoreType.DMA((13,))],
        compiler_params=pltpu.CompilerParams(vmem_limit_bytes=8 << 20),
        cost_estimate=pl.CostEstimate(flops=2 * 10**9, bytes_accessed=1, transcendentals=0),
    )(rows, *in_hbm(held), *in_hbm(weights))


def join_row(place, mine_ref, other_ref, row_ref):
    piece = mine_ref.shape[0]
    row_ref[rows_at(place * piece, piece), :] = mine_ref[...].astype(row_ref.dtype)
    row_ref[rows_at((1 - place) * piece, piece), :] = other_ref[...].astype(row_ref.dtype)


def attend_kernel(
    up_ref, down_ref, x_mine, x_other, small, wqkv, wo,
    up, down, n1, qkv, probs, mixed_low, middle, n2, heads_q, sems,
):
    _, _, place = where_am_i()
    copies = [
        pltpu.make_async_copy(up_ref, up, sems.at[0]),
        pltpu.make_async_copy(down_ref, down, sems.at[1]),
    ]
    for copy in copies:
        copy.start()
    length, features = n1.shape
    groups = features // GW
    join_row(place, x_mine, x_other, middle)
    normal, _ = normalize(middle[...])
    n1[...] = (normal * small[0:1, :] + small[1:2, :]).astype(LOW)
    for which in range(3):
        value = dot_nn(n1[...], wqkv[:, which * features : (which + 1) * features])
        if which != 1:
            line = 2 + which // 2
            value = value + small[line : line + 1, :]
        value = value.astype(LOW)
        for group in range(groups):
            qkv[which * groups + group] = value[:, group * GW : (group + 1) * GW]
    allowed = lax.broadcasted_iota(jnp.int32, (length, length), 0) >= lax.broadcasted_iota(
        jnp.int32, (length, length), 1
    )
    lanes = lax.broadcasted_iota(jnp.int32, (1, GW), 1)

    def one_group(group, carry):
        query, keys, values = (qkv[which * groups + group] for which in range(3))
        spread_heads(query, heads_q, HD**-0.5)
        parts = []
        for head in range(GROUP):
            cut = slice(head * length, (head + 1) * length)
            scores = jnp.where(allowed, dot_nt(heads_q[cut, :], keys), NEGATIVE)
            powers = jnp.exp(scores - jnp.max(scores, axis=-1, keepdims=True))
            low = (powers * (1.0 / jnp.sum(powers, axis=-1, keepdims=True))).astype(LOW)
            probs[group, cut, :] = low
            parts.append(low)
        mixed = dot_nn(parts[0], values)
        for head in range(1, GROUP):
            mixed = jnp.where(lanes >= head * HD, dot_nn(parts[head], values), mixed)
        mixed_low[:, rows_at(group * GW, GW)] = mixed.astype(LOW)
        return carry

    lax.fori_loop(0, groups, one_group, 0)
    middle[...] += dot_nn(mixed_low[...], wo[...]) + small[4:5, :]
    normal, _ = normalize(middle[...])
    n2[...] = (normal * small[5:6, :] + small[6:7, :]).astype(LOW)
    for copy in copies:
        copy.wait()


def attend(x_mine, x_other, small, qkv_weight, out_weight, up_weight, down_weight):
    piece, features = x_other.shape
    length = 2 * piece
    groups = features // GW
    act = ((length, features), LOW)
    return call(
        "attend",
        attend_kernel,
        (x_mine, x_other, small, qkv_weight, out_weight),
        [
            act,
            ((3 * groups, length, GW), LOW),
            ((groups, GROUP * length, length), LOW),
            act,
            ((length, features), SINGLE),
            act,
        ],
        [((GROUP * length, GW), LOW)],
        loaded=(up_weight, down_weight),
    )


def gelu_and_slope(u):
    c = math.sqrt(2 / math.pi)
    square = u * u
    bent = jnp.tanh(u * (c + (c * 0.044715) * square))
    half = 0.5 + 0.5 * bent
    slope = half + u * (0.5 - 0.5 * bent * bent) * (c + (3 * c * 0.044715) * square)
    return u * half, slope


def feed_tiles(side, n2, db2, small, up, down, g, du, vec, total):
    tiles, _, features = g.shape

    def one_tile(tile, carry):
        number = side * tiles + tile
        cut = rows_at(number * features, features)
        line = pl.ds(8 + number, 1)
        hidden = dot_nn(n2[...], up[:, cut]) + small[line, :]
        active, slope = gelu_and_slope(hidden)
        g[tile] = active.astype(LOW)
        grad = (dot_nt(db2[...], down[cut, :]) * slope).astype(LOW)
        du[tile] = grad
        vec[line, :] = jnp.sum(grad.astype(SINGLE), axis=0, keepdims=True)
        total[...] += dot_nt(grad, up[:, cut])
        return carry

    lax.fori_loop(0, tiles, one_tile, 0)


def feed_one_kernel(
    n2, c_mine, c_other, small, count, up, down, g, du, db2, theirs, dn, vec,
):
    core, _, place = where_am_i()
    half = theirs.shape[1]
    join_row(place, c_mine, c_other, db2)
    theirs[...] = db2[:, rows_at((1 - core) * half, half)]
    vec[...] = jnp.zeros_like(vec)
    vec[7:8, :] = jnp.sum(db2[...].astype(SINGLE), axis=0, keepdims=True)
    vec[12:13, 0:128] = count[...]
    dn[...] = jnp.zeros_like(dn)
    feed_tiles(1 - core, n2, db2, small, up, down, g, du, vec, dn)


def feed_one(n2, c_mine, c_other, small, count, up, down):
    length, features = n2.shape
    tiles = up.shape[1] // 2 // features
    hid = ((tiles, length, features), LOW)
    return call(
        "feed_one",
        feed_one_kernel,
        (n2, c_mine, c_other, small, count, up, down),
        [
            hid, hid, ((length, features), LOW), ((length, features // 2), LOW),
            ((length, features), SINGLE), ((16, features), SINGLE),
        ],
    )


def feed_two_kernel(
    n2, db2, small, up, down, middle, dn, vec_in, g, du, dm, db1, theirs, vec,
):
    core, _, _ = where_am_i()
    half = theirs.shape[1]
    vec[...] = vec_in[...]
    dm[...] = dn[...]
    feed_tiles(core, n2, db2, small, up, down, g, du, vec, dm)
    grad_n = dm[...]
    normal, inverse = normalize(middle[...])
    vec[5:6, :] = jnp.sum(grad_n * normal, axis=0, keepdims=True)
    vec[6:7, :] = jnp.sum(grad_n, axis=0, keepdims=True)
    grad = db2[...].astype(SINGLE) + norm_back(normal, inverse, grad_n, small[5:6, :])
    dm[...] = grad
    low = grad.astype(LOW)
    db1[...] = low
    theirs[...] = db1[:, rows_at((1 - core) * half, half)]
    vec[4:5, :] = jnp.sum(low.astype(SINGLE), axis=0, keepdims=True)


def feed_two(n2, db2, small, up, down, middle, dn, vec_in):
    length, features = n2.shape
    tiles = up.shape[1] // 2 // features
    hid = ((tiles, length, features), LOW)
    return call(
        "feed_two",
        feed_two_kernel,
        (n2, db2, small, up, down, middle, dn, vec_in),
        [
            hid, hid, ((length, features), SINGLE), ((length, features), LOW),
            ((length, features // 2), LOW), ((16, features), SINGLE),
        ],
    )


def result_kernel(g_mine, g_theirs, middle, small, down, x_grad_send, y_mine, send, total):
    core, _, place = where_am_i()
    tiles, _, features = g_mine.shape
    piece = y_mine.shape[0]
    total[...] = middle[...] + small[7:8, :]

    def one_tile(tile, carry):
        for side, active in ((core, g_mine), (1 - core, g_theirs)):
            cut = rows_at((side * tiles + tile) * features, features)
            total[...] += dot_nn(active[tile], down[cut, :])
        return carry

    lax.fori_loop(0, tiles, one_tile, 0)
    present = small[12:13, :]
    y_mine[...] = (total[rows_at(place * piece, piece), :] * present).astype(LOW)
    send[0] = (total[rows_at((1 - place) * piece, piece), :] * present).astype(LOW)
    send[1] = x_grad_send[...]


def result(g_mine, g_theirs, middle, small, down, x_grad_send):
    length, features = middle.shape
    piece = length // 2
    return call(
        "result",
        result_kernel,
        (g_mine, g_theirs, middle, small, down, x_grad_send),
        [((piece, features), LOW), ((2, piece, features), LOW)],
        [((length, features), SINGLE)],
    )


def back_kernel(
    qkv, probs, db1, wo, vec_in, theirs, mine, vec, dp, heads_q, heads_k, heads_g, side,
):
    core, _, _ = where_am_i()
    features = db1.shape[1]
    groups = features // GW
    vec[...] = vec_in[...]

    def one_group(group, carry):
        cut = rows_at(group * GW, GW)
        grad_mixed = dot_nt(db1[...], wo[cut, :]).astype(LOW)
        query, keys, values = (qkv[which * groups + group] for which in range(3))
        spread_heads(grad_mixed, heads_g)
        spread_heads(query, heads_q, HD**-0.5)
        spread_heads(keys, heads_k, HD**-0.5)
        weights = probs[group].astype(SINGLE)
        grad_probs = dot_nt(heads_g[...], values)
        inner = jnp.sum(weights * grad_probs, axis=-1, keepdims=True)
        grad_scores = (weights * (grad_probs - inner)).astype(LOW)
        side_by_side(grad_scores, side)
        dv = dot_tn(probs[group], heads_g[...])
        dk = dot_tn(grad_scores, heads_q[...])
        dq = dot_nn(side[...], heads_k[...])
        for which, value in enumerate((dq, dk, dv)):
            low = value.astype(LOW)
            dp[:, rows_at(which * features + group * GW, GW)] = low
            if which != 1:
                line = 2 + which // 2
                vec[line : line + 1, cut] = jnp.sum(low.astype(SINGLE), axis=0, keepdims=True)
        return carry

    lax.fori_loop(0, groups, one_group, 0)
    half = mine.shape[1]
    theirs[...] = dp[:, rows_at((1 - core) * half, half)]
    mine[...] = dp[:, rows_at(core * half, half)]


def back(qkv, probs, db1, out_weight, vec_in):
    length, features = db1.shape
    half = ((length, 3 * features // 2), LOW)
    return call(
        "back",
        back_kernel,
        (qkv, probs, db1, out_weight, vec_in),
        [half, half, ((16, features), SINGLE)],
        [((length, 3 * features), LOW)]
        + [((GROUP * length, GW), LOW)] * 3
        + [((length, GROUP * length), LOW)],
    )


def input_kernel(
    x_mine, x_other, small, dp_mine, dp_theirs, wqkv, dm, vec_in, mine, send, vec, row,
):
    core, _, place = where_am_i()
    half = dp_mine.shape[1]
    piece = mine.shape[0]
    grad_n = dot_nt(dp_mine[...], wqkv[:, rows_at(core * half, half)])
    grad_n = grad_n + dot_nt(dp_theirs[...], wqkv[:, rows_at((1 - core) * half, half)])
    join_row(place, x_mine, x_other, row)
    normal, inverse = normalize(row[...])
    vec[...] = vec_in[...]
    vec[0:1, :] = jnp.sum(grad_n * normal, axis=0, keepdims=True)
    vec[1:2, :] = jnp.sum(grad_n, axis=0, keepdims=True)
    row[...] = dm[...] + norm_back(normal, inverse, grad_n, small[0:1, :])
    mine[...] = row[rows_at(place * piece, piece), :].astype(LOW)
    send[...] = row[rows_at((1 - place) * piece, piece), :].astype(LOW)


def input_gradient(x_mine, x_other, small, dp_mine, dp_theirs, qkv_weight, dm, vec_in):
    piece, features = x_other.shape
    part = ((piece, features), LOW)
    return call(
        "input",
        input_kernel,
        (x_mine, x_other, small, dp_mine, dp_theirs, qkv_weight, dm, vec_in),
        [part, part, ((16, features), SINGLE)],
        [((2 * piece, features), SINGLE)],
    )


UNITS = 16


def unit_of(name, number):
    core, own, place = where_am_i()
    units = []
    for order in WAYS[name]:
        unit = 0
        for stage, axis in enumerate(order):
            if number >> (3 - stage) & 1:
                unit |= 1 if axis == "x" else BITS[axis] << 1
        units.append(unit)
    return jnp.where(core == 0, units[0], units[1]) ^ (own * 2 + place)


def lanes_kernel(
    g_mine, g_theirs, other_mine, other_theirs, right, right_other, send, keep, turned, whole, *, name
):
    core, _, _ = where_am_i()
    chunks, tall, wide = whole.shape
    tiles, length, features = g_mine.shape
    per_tile = features // wide
    half = tall // 2
    turned[:, :length] = right[:, rows_at(core * tall, tall)].T
    turned[:, length:] = right_other[...].T
    for side, one, two in ((core, g_mine, other_theirs), (1 - core, g_theirs, other_mine)):

        def one_tile(tile, carry, side=side, one=one, two=two):
            total = dot_nn(turned[:, :length], one[tile]) + dot_nn(turned[:, length:], two[tile])
            total = total.astype(LOW)
            for chunk in range(per_tile):
                whole[(side * tiles + tile) * per_tile + chunk] = total[:, chunk * wide : (chunk + 1) * wide]
            return carry

        lax.fori_loop(0, tiles, one_tile, 0)
    for number in range(UNITS):
        unit = unit_of(name, number)
        out = send if number >= UNITS // 2 else keep
        out[number % (UNITS // 2)] = whole[lax.div(unit, 2), rows_at(lax.rem(unit, 2) * half, half), :]


def grad_lanes(name, mine, theirs, other_mine, other_theirs, right, right_other):
    tiles, length, features = mine.shape
    tall = right_other.shape[1]
    chunks = UNITS // 2
    wide = 2 * tiles * features // chunks
    unit = ((UNITS // 2, tall // 2, wide), LOW)
    return call(
        "lanes",
        functools.partial(lanes_kernel, name=name),
        (mine, theirs, other_mine, other_theirs, right, right_other),
        [unit, unit],
        [((tall, 2 * length), LOW), ((chunks, tall, wide), LOW)],
    )


def rows_kernel(left, left_other, right, right_other, *rest, name, pick_core):
    if len(rest) > 4:
        vec, vec_other, send, keep, turned, whole, spread = rest
    else:
        send, keep, turned, whole = rest
        vec = None
    core, _, _ = where_am_i()
    length = left.shape[0]
    split = len(right_other.shape) == 2
    tiles, tile = (1, right_other.shape[1]) if split else (right_other.shape[0], right_other.shape[2])
    turned[:, :length] = left[...].T
    turned[:, length:] = left_other[...].T
    rows = turned.shape[0] // UNITS
    units = [unit_of(name, number) for number in range(UNITS)]
    if vec is not None:
        total = vec[...] + vec_other[...]
        features = total.shape[1]
        part = 2 * rows
        spread[...] = jnp.zeros_like(spread)
        for chunk in range(UNITS // 2):
            spread[2 * chunk, 0:8, :part] = total[0:8, chunk * part : (chunk + 1) * part]
            for piece in range(4):
                line, begin = divmod((4 * chunk + piece) * part, features)
                spread[2 * chunk + 1, piece : piece + 1, :part] = total[
                    8 + line : 9 + line, begin : begin + part
                ]
            spread[2 * chunk + 1, 4:5, : 2 * DIGITS] = total[12:13, : 2 * DIGITS]
        for out in (send, keep):
            out[:, rows:, :] = jnp.zeros_like(out[:, rows:, :])

    def one_tile(step, carry):
        if split:
            here = right[:, rows_at(core * tile, tile)] if pick_core else right[...]
            there = right_other[...]
        else:
            here, there = right[step], right_other[step]
        whole[...] = (dot_nn(turned[:, :length], here) + dot_nn(turned[:, length:], there)).astype(LOW)
        columns = rows_at(step * tile, tile)
        for number, unit in enumerate(units):
            out = send if number >= UNITS // 2 else keep
            out[number % (UNITS // 2), :rows, columns] = whole[rows_at(unit * rows, rows), :]
        return carry

    if tiles == 1:
        one_tile(0, 0)
    else:
        lax.fori_loop(0, tiles, one_tile, 0)
    if vec is not None:
        for number, unit in enumerate(units):
            out = send if number >= UNITS // 2 else keep
            out[number % (UNITS // 2), rows:, :128] = spread[unit].astype(LOW)


def grad_rows(name, left, left_other, right, right_other, pick_core=False, vecs=()):
    length, tall = left.shape
    rows = tall // UNITS
    tile = right_other.shape[-1]
    width = math.prod(right_other.shape) // length
    unit = ((UNITS // 2, rows + (16 if vecs else 0), width), LOW)
    return call(
        "rows_" + name,
        functools.partial(rows_kernel, name=name, pick_core=pick_core),
        (left, left_other, right, right_other, *vecs),
        [unit, unit],
        [((tall, 2 * length), LOW), ((tall, tile), LOW)] + [((UNITS, 16, 128), SINGLE)] * bool(vecs),
    )


FIRST = ("o", "q", "d", "u")


PACK = 384


def packed_rows(name, shape):
    tall, width = shape
    return (tall - 16 if name == "o" else tall) * (width // PACK)


def pack_kernel(*refs):
    out = refs[-1]
    first = 0
    for number, part in enumerate(refs[:-1]):
        name = FIRST[number // 2]
        tall = part.shape[0] - (16 if name == "o" else 0)
        for block in range(part.shape[1] // PACK):
            out[first : first + tall, :] = part[:tall, block * PACK : (block + 1) * PACK]
            first += tall


def pack(parts):
    operands = [p for name in FIRST for p in parts[name]]
    rows = sum(packed_rows(name, p.shape) for name in FIRST for p in parts[name])
    return call("result", pack_kernel, operands, [((rows, PACK), LOW)])[0]


def finish_side(side, parts, share, out, turned, scratch, sems, copies):
    _, _, place = where_am_i()
    for number, name in enumerate(FIRST):
        tall, width = 0, 0
        for spot in (0, 1):
            low = place ^ spot
            blocks = parts(name, spot)
            tall, width = blocks[0].shape[0], PACK * len(blocks)
            for block, value in enumerate(blocks):
                value = value.astype(SINGLE)
                if name == "d":
                    turned[rows_at(low * tall, tall), :] = value
                else:
                    scratch[number][rows_at(low * tall, tall), block * PACK : (block + 1) * PACK] = (
                        value * share
                    )
        if name == "d":
            scratch[number][...] = turned[...].T * share
            width = scratch[number].shape[1]
        target = out[number].at[:, rows_at(side * width, width)]
        copies.append(pltpu.make_async_copy(scratch[number], target, sems.at[number]))
        copies[-1].start()


def own_kernel(*refs):
    homes, refs = refs[:3], refs[3:]
    given = {name: refs[2 * i : 2 * i + 2] for i, name in enumerate(FIRST)}
    refs = refs[2 * len(FIRST) :]
    grads, refs = refs[: len(FIRST)], refs[len(FIRST) :]
    count = (len(refs) - 4 - len(FIRST)) // 2
    results, share_out, refs = refs[:count], refs[count], refs[count + 1 :]
    scratch, held = refs[: len(FIRST)], refs[len(FIRST) : len(FIRST) + count]
    vec, turned, sems = refs[len(FIRST) + count :]
    core, _, place = where_am_i()
    copies = []

    def send(*numbers):
        for number in numbers:
            copies.append(
                pltpu.make_async_copy(held[number], results[number], sems.at[len(FIRST) + number])
            )
            copies[-1].start()

    for number in (0, 1):
        held[number][place] = homes[number][...]
        held[number][1 - place] = homes[2][number]
    send(0, 1)
    mine, other = given["o"]
    half = mine.shape[0] - 16
    vec[rows_at(place * 8, 8), :] = mine[half:, :128].astype(SINGLE)[:8]
    vec[rows_at((1 - place) * 8, 8), :] = other[half:, :128].astype(SINGLE)[:8]
    line = vec[12:13, :]
    lane = lax.broadcasted_iota(jnp.int32, line.shape, 1)
    worth = lax.shift_left(jnp.ones_like(lane), lax.rem(lane, DIGITS)).astype(SINGLE)
    first, second = (
        jnp.sum(jnp.where(lane // DIGITS == side, line * worth, 0.0), axis=1, keepdims=True)
        for side in (0, 1)
    )
    share = 1.0 / (first + second)
    share_out[...] = jnp.broadcast_to(share, share_out.shape)

    def parts(name, spot):
        part = given[name][spot]
        tall = part.shape[0] - (16 if name == "o" else 0)
        return [part[:tall, at : at + PACK] for at in range(0, part.shape[1], PACK)]

    finish_side(core, parts, share, grads, turned, scratch, sems, copies)
    counts, up, qv, *plain = held[2:]
    spot = lax.broadcasted_iota(jnp.int32, (1, 128), 1)
    counts[...] = jnp.where(spot == 0, first, second).astype(jnp.int32)[0, : counts.shape[0]]
    width = qv.shape[1]
    scaled = vec[...] * share
    qv[...] = scaled[2:4, :width]
    for number, out in zip((0, 1, 4, 5, 6, 7), plain):
        out[...] = scaled[number, :width]
    up[...] = jnp.concatenate([scaled[8 + part : 9 + part, :width] for part in range(4)], axis=1)[0]
    send(*range(2, count))
    for copy in copies:
        copy.wait()


def other_kernel(theirs, share, *refs):
    refs = refs[len(FIRST) :]
    grads, refs = refs[: len(FIRST)], refs[len(FIRST) :]
    scratch, (turned, sems) = refs[: len(FIRST)], refs[len(FIRST) :]
    core, _, _ = where_am_i()
    first = [0]

    def parts(name, spot):
        place = FIRST.index(name)
        tall, width = scratch[place].shape
        if name == "d":
            tall, width = turned.shape
        blocks = []
        for _ in range(width // PACK):
            blocks.append(theirs[first[0] : first[0] + tall // 2, :])
            first[0] += tall // 2
        return blocks

    copies = []
    finish_side(1 - core, parts, share[0:1, 0:1], grads, turned, scratch, sems, copies)
    for copy in copies:
        copy.wait()


def finale(homes, theirs, parts, rows):
    piece, features = homes[0].shape
    shapes, halves = [], []
    for name in FIRST:
        tall, width = parts[name][0].shape
        shapes.append((width, 4 * tall) if name == "d" else (2 * rows, 2 * width))
        halves.append(pltpu.VMEM((shapes[-1][0], shapes[-1][1] // 2), SINGLE))
    grads = [jax.ShapeDtypeStruct(s, SINGLE) for s in shapes]
    chunk = 2 * rows
    home = jax.ShapeDtypeStruct((2, piece, features), LOW)
    results = [
        home,
        home,
        jax.ShapeDtypeStruct((2,), jnp.int32),
        jax.ShapeDtypeStruct((4 * chunk,), SINGLE),
        jax.ShapeDtypeStruct((2, chunk), SINGLE),
    ] + [jax.ShapeDtypeStruct((chunk,), SINGLE)] * 6
    vmem = pl.BlockSpec(memory_space=pltpu.VMEM)
    anywhere = pl.BlockSpec(memory_space=pl.ANY)
    tall, width = parts["d"][0].shape
    turned = pltpu.VMEM((2 * tall, width), SINGLE)
    operands = [*homes, *[p for name in FIRST for p in parts[name]]]
    params = pltpu.CompilerParams(vmem_limit_bytes=16 << 20)
    own = pl.pallas_call(
        own_kernel,
        in_specs=[vmem] * len(operands),
        out_specs=[anywhere] * (len(grads) + len(results)) + [vmem],
        out_shape=grads + results + [jax.ShapeDtypeStruct((8, 128), SINGLE)],
        scratch_shapes=halves
        + [pltpu.VMEM(r.shape, r.dtype) for r in results]
        + [
            pltpu.VMEM((16, 128), SINGLE),
            turned,
            pltpu.SemaphoreType.DMA((len(grads) + len(results),)),
        ],
        compiler_params=params,
        cost_estimate=pl.CostEstimate(flops=40 * 10**9, bytes_accessed=1, transcendentals=0),
    )(*operands)
    grads_own, rest, share = own[: len(grads)], own[len(grads) : -1], own[-1]
    whole = pl.pallas_call(
        other_kernel,
        in_specs=[vmem, vmem] + [anywhere] * len(grads),
        out_specs=[anywhere] * len(grads),
        out_shape=grads,
        scratch_shapes=halves + [turned, pltpu.SemaphoreType.DMA((len(grads),))],
        input_output_aliases={2 + i: i for i in range(len(grads))},
        compiler_params=params,
        cost_estimate=pl.CostEstimate(flops=1, bytes_accessed=1, transcendentals=0),
    )(theirs, share, *grads_own)
    return [*rest[:2], *whole, *rest[2:]]


def swap_pairs(size, bit):
    return [(i, i ^ bit) for i in range(size)]


def partners(name, stage, groups):
    pairs = []
    for core in range(2):
        axis = WAYS[name][core][stage]
        for own in range(groups):
            for place in range(2):
                to = (own, place ^ 1) if axis == "x" else (own ^ BITS[axis], place)
                pairs.append(((core * groups + own) * 2 + place, (core * groups + to[0]) * 2 + to[1]))
    return pairs


def added(one, two):
    return (one.astype(SINGLE) + two.astype(SINGLE)).astype(LOW)


class Order:
    def __init__(self):
        self.last = None

    def tie(self, value):
        if self.last is not None:
            value, _ = lax.optimization_barrier((value, self.last))
        return value

    def mark(self, value):
        self.last = value


class Sum:
    def __init__(self, order, name, groups, send, keep):
        self.order, self.name, self.groups = order, name, groups
        self.keep = keep
        self.stage = 0
        self.whole_last = all(way[3] == "x" for way in WAYS[name])
        self.parts = None
        self.go(send)

    def go(self, send):
        self.flying = lax.ppermute(send, AXES, partners(self.name, self.stage, self.groups))

    def step(self):
        if self.parts is not None:
            return
        other = self.order.tie(self.flying)
        keep = self.keep
        self.stage += 1
        if self.stage == 5:
            self.order.mark(other)
            self.parts = [self.total, other]
        elif self.stage == 4 and self.whole_last:
            self.parts = [added(keep[0], other[1]), added(keep[1], other[0])]
            self.order.mark(self.parts[0])
        elif self.stage == 4:
            self.total = added(keep[0], other[0])
            self.order.mark(self.total)
            self.flying = lax.ppermute(self.total, "seq", swap_pairs(2, 1))
        elif self.stage == 3 and self.whole_last:
            self.keep = added(keep, other)
            self.order.mark(self.keep)
            self.go(self.keep)
        else:
            half = keep.shape[0] // 2
            send = added(keep[half:], other[half:])
            self.keep = added(keep[:half], other[:half])
            self.order.mark(send)
            self.go(send)


def body_fast(
    inputs,
    cotangent,
    row_counts,
    response_mask,
    norm1_gain,
    norm1_bias,
    qkv_weight,
    qv_bias,
    out_weight,
    out_bias,
    norm2_gain,
    norm2_bias,
    up_weight,
    up_bias,
    down_weight,
    down_bias,
):
    groups = lax.axis_size("dp")
    pair = swap_pairs(2, 1)
    core, own, place = (lax.axis_index(a) for a in ("src", "dp", "seq"))
    x_both = inputs[0, 0]
    x_other = lax.ppermute(
        lax.dynamic_index_in_dim(x_both, 1 - place, 0, keepdims=False), "seq", pair
    )
    x_mine, c_send, c_mine, count, small, qkv_weight, out_weight = prepare(
        row_counts,
        response_mask[0, 0],
        x_both,
        cotangent[0, 0],
        (norm1_gain, norm1_bias, qv_bias, out_bias, norm2_gain, norm2_bias, down_bias, up_bias),
        (qkv_weight, out_weight),
    )
    c_other = lax.ppermute(c_send, "seq", pair)
    order = Order()

    def from_core(value):
        return lax.ppermute(value, "src", pair)

    up_weight, down_weight, n1, qkv, probs, mixed, middle, n2 = attend(
        x_mine, x_other, small, qkv_weight, out_weight, up_weight, down_weight
    )
    g_theirs, du_theirs, db2, db2_theirs, dn, vec = feed_one(
        n2, c_mine, c_other, small, count, up_weight, down_weight
    )
    order.mark(vec)
    n2_other, n1_other, mixed_other = order.tie(
        (from_core(n2), from_core(n1), from_core(mixed))
    )
    here, n2_other, n1_other, mixed_other = lax.optimization_barrier(
        (n2, n2_other, n1_other, mixed_other)
    )
    g_mine, du_mine, dm, db1, db1_theirs, vec = feed_two(
        here, db2, small, up_weight, down_weight, middle, dn, vec
    )
    order.mark(vec)
    du_other, db2_other, other_theirs = order.tie(
        (from_core(du_theirs), from_core(db2_theirs), from_core(g_theirs))
    )
    here, du_other, db2_other, other_theirs = lax.optimization_barrier(
        (n2, du_other, db2_other, other_theirs)
    )
    other_mine, db1_other = from_core(g_mine), from_core(db1_theirs)

    sums = {}
    for event in EVENTS:
        if event == "h":
            homes = lax.ppermute(order.tie(home_send), "seq", pair)
            continue
        if event == "i":
            homes = order.tie(homes)
            order.mark(homes)
            continue
        if event.islower():
            sums[event].step()
            continue
        name = event.lower()
        if event == "U":
            parts = grad_rows(name, order.tie(here), n2_other, du_mine, du_other)
        elif event == "D":
            other_mine = order.tie(other_mine)
            here, other_mine = lax.optimization_barrier((g_mine, other_mine))
            parts = grad_lanes(name, here, g_theirs, other_mine, other_theirs, db2, db2_other)
        elif event == "C":
            here = order.tie(qkv)
            dp_theirs, dp_mine, vec = back(here, probs, db1, out_weight, vec)
            dp_other = from_core(dp_theirs)
            order.mark(vec)
            continue
        elif event == "I":
            x_grad_mine, x_grad_send, vec = input_gradient(
                order.tie(x_mine), x_other, small, dp_mine, dp_theirs, qkv_weight, dm, vec
            )
            vec_other = from_core(vec)
            order.mark(vec)
            continue
        elif event == "Y":
            y_mine, home_send = result(
                order.tie(g_mine), g_theirs, middle, small, down_weight, x_grad_send
            )
            order.mark(home_send)
            continue
        elif event == "O":
            parts = grad_rows(
                name, order.tie(mixed), mixed_other, db1, db1_other, True, (vec, vec_other)
            )
        else:
            dp_other, db1_other = order.tie((dp_other, db1_other))
            here, dp_other, db1_other = lax.optimization_barrier((n1, dp_other, db1_other))
            parts = grad_rows(name, here, n1_other, dp_mine, dp_other)
        order.mark(parts[0])
        sums[name] = Sum(order, name, groups, *parts)

    parts = order.tie({name: sums[name].parts for name in FIRST})
    rows = out_weight.shape[0] // groups // 2
    output, input_grad, out, qkv, down, up, counts, up_small, qv, *plain = finale(
        (y_mine, x_grad_mine, homes), from_core(pack(parts)), parts, rows
    )
    return (
        output[None, None],
        input_grad[None, None],
        counts,
        plain[0],
        plain[1],
        qkv,
        qv,
        out,
        plain[2],
        plain[3],
        plain[4],
        up,
        up_small,
        down,
        plain[5],
    )


def solution(mesh):
    placed = (
        P("src", "dp", None, "seq", None),
        P("src", "dp", None, "seq", None),
        P("src", "dp"),
        P("src", "dp", None, "seq"),
        P(),
        P(),
        P(),
        P(),
        P(),
        P(),
        P(),
        P(),
        P(),
        P(),
        P(),
        P(),
    )
    sizes = dict(mesh.shape)
    paired = sizes["src"] == 2 and sizes["seq"] == 2 and sizes["dp"] == 8
    return jax.shard_map(
        body_fast if paired else body_generic,
        mesh=mesh,
        in_specs=placed,
        out_specs=(
            P("src", "dp", None, "seq", None),
            P("src", "dp", None, "seq", None),
            P(),
            P("dp"),
            P("dp"),
            P("dp", None),
            P(None, "dp"),
            P("dp", None),
            P("dp"),
            P("dp"),
            P("dp"),
            P("dp", None),
            P("dp"),
            P("dp", None),
            P("dp"),
        ),
        check_vma=False,
    )
```

```python
import functools
import math

import jax
import jax.numpy as jnp
from jax import lax
from jax.experimental import pallas as pl
from jax.experimental.pallas import tpu as pltpu
from jax.sharding import PartitionSpec as P

H = 12
HD = 64


EPS = 1e-05
NEGATIVE = -1e30


def norm_apply(values, scaling, offset):
    centre = jnp.mean(values, axis=-1, keepdims=True)
    centered = values - centre
    spread = jnp.mean(centered * centered, axis=-1, keepdims=True)
    return centered * lax.rsqrt(spread + EPS) * scaling + offset


def causal_scores(query_part, keys_part, allowed):
    scores = jnp.einsum(
        "rqhd,rkhd->rhqk", query_part, keys_part, preferred_element_type=jnp.float32
    )
    scores = scores * HD ** (-0.5)
    return jnp.where(allowed, scores, NEGATIVE)


def attend_forward(query_part, keys_part, values_part, allowed):
    scores = causal_scores(query_part, keys_part, allowed)
    highest = jnp.max(scores, axis=-1, keepdims=True)
    powers = jnp.exp(scores - highest)
    totals = jnp.sum(powers, axis=-1, keepdims=True)
    probs_low = (powers / totals).astype(jnp.bfloat16)
    mixed = jnp.einsum(
        "rhqk,rkhd->rqhd", probs_low, values_part, preferred_element_type=jnp.float32
    )
    return (mixed, highest, totals)


def attend_backward(query_part, keys_part, values_part, grad_part, highest, totals, allowed):
    scores = causal_scores(query_part, keys_part, allowed)
    probs = jnp.exp(scores - highest) / totals
    probs_low = probs.astype(jnp.bfloat16)
    grad_probs = jnp.einsum(
        "rqhd,rkhd->rhqk", grad_part, values_part, preferred_element_type=jnp.float32
    )
    inner = jnp.sum(probs * grad_probs, axis=-1, keepdims=True)
    grad_scores = (probs * (grad_probs - inner)).astype(jnp.bfloat16)
    factor = HD ** (-0.5)
    grad_query = (
        jnp.einsum("rhqk,rkhd->rqhd", grad_scores, keys_part, preferred_element_type=jnp.float32)
        * factor
    )
    grad_keys = (
        jnp.einsum("rhqk,rqhd->rkhd", grad_scores, query_part, preferred_element_type=jnp.float32)
        * factor
    )
    grad_values = jnp.einsum(
        "rhqk,rqhd->rkhd", probs_low, grad_part, preferred_element_type=jnp.float32
    )
    return (grad_query, grad_keys, grad_values)


def body_generic(
    inputs,
    cotangent,
    row_counts,
    response_mask,
    norm1_gain,
    norm1_bias,
    qkv_weight,
    qv_bias,
    out_weight,
    out_bias,
    norm2_gain,
    norm2_bias,
    up_weight,
    up_bias,
    down_weight,
    down_bias,
):
    slots = inputs.shape[2]
    piece_len = inputs.shape[3]
    features = inputs.shape[4]
    tokens = slots * piece_len
    blocks_seq = lax.axis_size("seq")
    row_len = piece_len * blocks_seq
    group_heads = math.gcd(H, 4)
    bfloat = jnp.bfloat16
    single = jnp.float32
    present_int = (jnp.arange(slots) < row_counts[0, 0]).astype(jnp.int32)
    weight = (response_mask[0, 0] * present_int[:, None]).astype(single)
    local_count = jnp.sum(response_mask[0, 0] * present_int[:, None])
    picked = jnp.where(jnp.arange(lax.axis_size("src")) == lax.axis_index("src"), local_count, 0)
    source_counts = lax.psum(picked, ("src", "dp", "seq"))
    whole = jnp.sum(source_counts).astype(single)
    source = inputs.reshape(tokens, features).astype(single)
    normed, norm1_pull = jax.vjp(
        norm_apply, source, norm1_gain.astype(single), norm1_bias.astype(single)
    )
    normed_low = normed.astype(bfloat)
    bias_query = qv_bias[0].astype(single)
    joined = jnp.concatenate([bias_query, jnp.zeros_like(bias_query), qv_bias[1].astype(single)])
    projected = jnp.dot(normed_low, qkv_weight, preferred_element_type=single) + joined
    proj_low = projected.astype(bfloat)
    query = proj_low[:, :features].reshape(slots, piece_len, H, HD)
    keys_own = proj_low[:, features : 2 * features].reshape(slots, piece_len, features)
    values_own = proj_low[:, 2 * features :].reshape(slots, piece_len, features)
    keys_all, values_all = (
        lax.all_gather(keys_own, "seq", axis=1, tiled=True),
        lax.all_gather(values_own, "seq", axis=1, tiled=True),
    )
    query_pos = lax.axis_index("seq") * piece_len + jnp.arange(piece_len)
    allowed = query_pos[:, None] >= jnp.arange(row_len)[None, :]
    keys_heads = keys_all.reshape(slots, row_len, H, HD)
    values_heads = values_all.reshape(slots, row_len, H, HD)
    mixed_parts = []
    kept_stats = []
    for group in range(H // group_heads):
        first = group * group_heads
        last = first + group_heads
        mixed, highest, totals = attend_forward(
            query[:, :, first:last],
            keys_heads[:, :, first:last],
            values_heads[:, :, first:last],
            allowed,
        )
        mixed_parts.append(mixed)
        kept_stats.append((highest, totals))
    attended = jnp.concatenate(mixed_parts, axis=2).reshape(tokens, features)
    attended_low = attended.astype(bfloat)
    branch = jnp.dot(attended_low, out_weight, preferred_element_type=single) + out_bias.astype(
        single
    )
    middle = source + branch
    normed_two, norm2_pull = jax.vjp(
        norm_apply, middle, norm2_gain.astype(single), norm2_bias.astype(single)
    )
    normed_two_low = normed_two.astype(bfloat)
    hidden = jnp.dot(normed_two_low, up_weight, preferred_element_type=single) + up_bias.astype(
        single
    )
    active, gelu_pull = jax.vjp(functools.partial(jax.nn.gelu, approximate=True), hidden)
    active_low = active.astype(bfloat)
    branch_two = jnp.dot(active_low, down_weight, preferred_element_type=single) + down_bias.astype(
        single
    )
    result = middle + branch_two
    present_tok = jnp.repeat(present_int.astype(single), piece_len)
    output = (result * present_tok[:, None]).astype(bfloat).reshape(inputs.shape)
    incoming = cotangent.reshape(tokens, features).astype(single) * weight.reshape(tokens)[:, None]
    grad_branch_two = incoming.astype(bfloat)
    grad_down_weight = jnp.einsum(
        "tf,td->fd", active_low, grad_branch_two, preferred_element_type=single
    )
    grad_down_bias = jnp.sum(grad_branch_two.astype(single), axis=0)
    grad_active = jnp.einsum(
        "td,fd->tf", grad_branch_two, down_weight, preferred_element_type=single
    )
    grad_hidden = gelu_pull(grad_active)[0].astype(bfloat)
    grad_up_weight = jnp.einsum(
        "tm,tf->mf", normed_two_low, grad_hidden, preferred_element_type=single
    )
    grad_up_bias = jnp.sum(grad_hidden.astype(single), axis=0)
    grad_normed_two = jnp.einsum("tf,mf->tm", grad_hidden, up_weight, preferred_element_type=single)
    grad_mid_norm, grad_norm2_gain, grad_norm2_bias = norm2_pull(grad_normed_two)
    grad_middle = incoming + grad_mid_norm
    grad_branch = grad_middle.astype(bfloat)
    grad_out_weight = jnp.einsum(
        "tm,td->md", attended_low, grad_branch, preferred_element_type=single
    )
    grad_out_bias = jnp.sum(grad_branch.astype(single), axis=0)
    grad_attended = jnp.einsum("td,md->tm", grad_branch, out_weight, preferred_element_type=single)
    grad_heads = grad_attended.astype(bfloat).reshape(slots, piece_len, H, HD)
    query_grads = []
    key_grads = []
    value_grads = []
    for group in range(H // group_heads):
        first = group * group_heads
        last = first + group_heads
        highest, totals = kept_stats[group]
        grad_query, grad_keys, grad_values = attend_backward(
            query[:, :, first:last],
            keys_heads[:, :, first:last],
            values_heads[:, :, first:last],
            grad_heads[:, :, first:last],
            highest,
            totals,
            allowed,
        )
        query_grads.append(grad_query)
        key_grads.append(grad_keys)
        value_grads.append(grad_values)
    grad_query_all = jnp.concatenate(query_grads, axis=2).reshape(tokens, features)
    grad_keys_all = jnp.concatenate(key_grads, axis=2).reshape(slots, row_len, features)
    grad_values_all = jnp.concatenate(value_grads, axis=2).reshape(slots, row_len, features)
    grad_keys_own, grad_values_own = (
        lax.psum_scatter(
            grad_keys_all.astype(jnp.bfloat16), "seq", scatter_dimension=1, tiled=True
        ).astype(jnp.float32),
        lax.psum_scatter(
            grad_values_all.astype(jnp.bfloat16), "seq", scatter_dimension=1, tiled=True
        ).astype(jnp.float32),
    )
    grad_projected = jnp.concatenate(
        [
            grad_query_all,
            grad_keys_own.reshape(tokens, features),
            grad_values_own.reshape(tokens, features),
        ],
        axis=1,
    ).astype(bfloat)
    grad_qkv_weight = jnp.einsum(
        "tm,tn->mn", normed_low, grad_projected, preferred_element_type=single
    )
    column_sums = jnp.sum(grad_projected.astype(single), axis=0)
    grad_qv_bias = jnp.stack([column_sums[:features], column_sums[2 * features :]])
    grad_normed = jnp.einsum("tn,mn->tm", grad_projected, qkv_weight, preferred_element_type=single)
    grad_src_norm, grad_norm1_gain, grad_norm1_bias = norm1_pull(grad_normed)
    input_grad = (grad_middle + grad_src_norm).astype(bfloat).reshape(inputs.shape)
    grads = (
        grad_norm1_gain,
        grad_norm1_bias,
        grad_qkv_weight,
        grad_qv_bias,
        grad_out_weight,
        grad_out_bias,
        grad_norm2_gain,
        grad_norm2_bias,
        grad_up_weight,
        grad_up_bias,
        grad_down_weight,
        grad_down_bias,
    )
    summed = (
        lax.psum_scatter(
            grads[0].astype(jnp.bfloat16), "dp", scatter_dimension=0, tiled=True
        ).astype(jnp.float32),
        lax.psum_scatter(
            grads[1].astype(jnp.bfloat16), "dp", scatter_dimension=0, tiled=True
        ).astype(jnp.float32),
        lax.psum_scatter(
            grads[2].astype(jnp.bfloat16), "dp", scatter_dimension=0, tiled=True
        ).astype(jnp.float32),
        lax.psum_scatter(
            grads[3].astype(jnp.bfloat16), "dp", scatter_dimension=1, tiled=True
        ).astype(jnp.float32),
        lax.psum_scatter(
            grads[4].astype(jnp.bfloat16), "dp", scatter_dimension=0, tiled=True
        ).astype(jnp.float32),
        lax.psum_scatter(
            grads[5].astype(jnp.bfloat16), "dp", scatter_dimension=0, tiled=True
        ).astype(jnp.float32),
        lax.psum_scatter(
            grads[6].astype(jnp.bfloat16), "dp", scatter_dimension=0, tiled=True
        ).astype(jnp.float32),
        lax.psum_scatter(
            grads[7].astype(jnp.bfloat16), "dp", scatter_dimension=0, tiled=True
        ).astype(jnp.float32),
        lax.psum_scatter(
            grads[8].astype(jnp.bfloat16), "dp", scatter_dimension=0, tiled=True
        ).astype(jnp.float32),
        lax.psum_scatter(
            grads[9].astype(jnp.bfloat16), "dp", scatter_dimension=0, tiled=True
        ).astype(jnp.float32),
        lax.psum_scatter(
            grads[10].astype(jnp.bfloat16), "dp", scatter_dimension=0, tiled=True
        ).astype(jnp.float32),
        lax.psum_scatter(
            grads[11].astype(jnp.bfloat16), "dp", scatter_dimension=0, tiled=True
        ).astype(jnp.float32),
    )
    summed = (
        lax.psum(summed[0].astype(jnp.bfloat16), ("src", "seq")).astype(jnp.float32),
        lax.psum(summed[1].astype(jnp.bfloat16), ("src", "seq")).astype(jnp.float32),
        lax.psum(summed[2].astype(jnp.bfloat16), ("src", "seq")).astype(jnp.float32),
        lax.psum(summed[3].astype(jnp.bfloat16), ("src", "seq")).astype(jnp.float32),
        lax.psum(summed[4].astype(jnp.bfloat16), ("src", "seq")).astype(jnp.float32),
        lax.psum(summed[5].astype(jnp.bfloat16), ("src", "seq")).astype(jnp.float32),
        lax.psum(summed[6].astype(jnp.bfloat16), ("src", "seq")).astype(jnp.float32),
        lax.psum(summed[7].astype(jnp.bfloat16), ("src", "seq")).astype(jnp.float32),
        lax.psum(summed[8].astype(jnp.bfloat16), ("src", "seq")).astype(jnp.float32),
        lax.psum(summed[9].astype(jnp.bfloat16), ("src", "seq")).astype(jnp.float32),
        lax.psum(summed[10].astype(jnp.bfloat16), ("src", "seq")).astype(jnp.float32),
        lax.psum(summed[11].astype(jnp.bfloat16), ("src", "seq")).astype(jnp.float32),
    )
    final = [g / whole for g in summed]
    return (
        output,
        input_grad,
        source_counts,
        final[0],
        final[1],
        final[2],
        final[3],
        final[4],
        final[5],
        final[6],
        final[7],
        final[8],
        final[9],
        final[10],
        final[11],
    )


WAYS = {
    "u": ("yx12", "12yx"),
    "d": ("xy12", "1yx2"),
    "o": ("yx12", "yx12"),
    "q": ("x1y2", "yx12"),
}
EVENTS = "UDCIOQYudoqudqohudqoduoqiduoq"
BITS = {"y": 1, "1": 2, "2": 4}


COSTS = {"attend": 8, "feed_one": 5, "feed_two": 5, "back": 0, "input": 0, "lanes": 0, "rows_u": 4, "rows_q": 0, "rows_o": 0, "result": 0}
AXES = ("src", "dp", "seq")
SINGLE = jnp.float32
LOW = jnp.bfloat16
GROUP = 4
GW = GROUP * HD
DIGITS = 16


def dot_nt(left, right):
    return lax.dot_general(left, right, (((1,), (1,)), ((), ())), preferred_element_type=SINGLE)


def dot_tn(left, right):
    return lax.dot_general(left, right, (((0,), (0,)), ((), ())), preferred_element_type=SINGLE)


def dot_nn(left, right):
    return jnp.dot(left, right, preferred_element_type=SINGLE)


def normalize(values):
    centered = values - jnp.mean(values, axis=-1, keepdims=True)
    inverse = lax.rsqrt(jnp.mean(centered * centered, axis=-1, keepdims=True) + EPS)
    return centered * inverse, inverse


def norm_back(normal, inverse, grad, gain):
    scaled = grad * gain
    return inverse * (
        scaled
        - jnp.mean(scaled, axis=-1, keepdims=True)
        - normal * jnp.mean(scaled * normal, axis=-1, keepdims=True)
    )


def spread_heads(value, out, scale=1.0):
    length = value.shape[0]
    lanes = lax.broadcasted_iota(jnp.int32, (1, GW), 1)
    for head in range(GROUP):
        keep = jnp.where((lanes >= head * HD) & (lanes < (head + 1) * HD), scale, 0.0).astype(LOW)
        out[head * length : (head + 1) * length, :] = value * keep


def side_by_side(stacked, out):
    length = out.shape[0]
    for head in range(GROUP):
        out[:, head * length : (head + 1) * length] = stacked[head * length : (head + 1) * length, :]


def rows_at(first, count):
    return pl.ds(pl.multiple_of(first, count), count)


def where_am_i():
    return tuple(lax.axis_index(axis) for axis in AXES)


def call(name, kernel, operands, outs, scratch=(), loaded=()):
    vmem = pl.BlockSpec(memory_space=pltpu.VMEM)
    return pl.pallas_call(
        kernel,
        in_specs=[pl.BlockSpec(memory_space=pl.ANY)] * len(loaded) + [vmem] * len(operands),
        out_specs=[vmem] * (len(loaded) + len(outs)),
        out_shape=[jax.ShapeDtypeStruct(v.shape, v.dtype) for v in loaded]
        + [jax.ShapeDtypeStruct(*o) for o in outs],
        scratch_shapes=[pltpu.VMEM(*s) for s in scratch]
        + [pltpu.SemaphoreType.DMA((len(loaded),))] * bool(loaded),
        compiler_params=pltpu.CompilerParams(vmem_limit_bytes=16 << 20),
        cost_estimate=pl.CostEstimate(
            flops=int(COSTS[name] * 10**9) + 1, bytes_accessed=1, transcendentals=0
        ),
    )(*in_hbm(loaded), *operands)


def prepare_kernel(*refs):
    rows_ref, ins, refs = refs[0], refs[1:14], refs[14:]
    x_mine, c_send, c_mine, count_ref, small, wqkv, wo = refs[:7]
    held, sems = refs[7:18], refs[18]
    core, _, place = where_am_i()
    copies = [
        pltpu.make_async_copy(source, target, sems.at[i])
        for i, (source, target) in enumerate(zip(ins, held + (wqkv, wo)))
    ]
    for copy in copies:
        copy.start()
    for copy in copies[:11]:
        copy.wait()
    (
        mask_ref, x_ref, cot_ref, gain1, bias1, qv_bias, out_bias, gain2, bias2, down_bias, up_bias,
    ) = held
    piece = mask_ref.shape[1]
    diagonal = lax.broadcasted_iota(jnp.int32, (piece, piece), 0) == lax.broadcasted_iota(
        jnp.int32, (piece, piece), 1
    )
    rows = rows_ref[0, 0]

    def column(row):
        kept = mask_ref[pl.ds(row, 1), :].astype(SINGLE) * (row < rows).astype(SINGLE)
        return jnp.sum(jnp.where(diagonal, kept, 0.0), axis=1, keepdims=True), kept

    weight_send, kept_send = column(1 - place)
    c_send[...] = (cot_ref[1 - place].astype(SINGLE) * weight_send).astype(LOW)
    weight_mine, kept_mine = column(place)
    c_mine[...] = (cot_ref[place].astype(SINGLE) * weight_mine).astype(LOW)
    x_mine[...] = x_ref[place]
    count = jnp.sum(kept_mine + kept_send, axis=1, keepdims=True).astype(jnp.int32)
    lane = lax.broadcasted_iota(jnp.int32, count_ref.shape, 1) - core * DIGITS
    digit = lax.shift_right_logical(
        jnp.broadcast_to(count, count_ref.shape), jnp.clip(lane, 0, DIGITS - 1)
    )
    count_ref[...] = jnp.where((lane >= 0) & (lane < DIGITS), digit & 1, 0).astype(SINGLE)
    features = small.shape[1]
    small[12:16, :] = jnp.broadcast_to((place < rows).astype(SINGLE), (4, features))
    small[2:4, :] = qv_bias[...].astype(SINGLE)
    for line, value in ((0, gain1), (1, bias1), (4, out_bias), (5, gain2), (6, bias2), (7, down_bias)):
        small[line : line + 1, :] = value[...].astype(SINGLE)[None, :]
    ups = up_bias[...].astype(SINGLE)[None, :]
    for part in range(ups.shape[1] // features):
        small[8 + part : 9 + part, :] = ups[:, part * features : (part + 1) * features]
    for copy in copies[11:]:
        copy.wait()


def in_hbm(values):
    return [pltpu.with_memory_space_constraint(value, pltpu.HBM) for value in values]


def prepare(rows, mask, x, cot, vectors, weights):
    piece, features = cot.shape[1:]
    part = jax.ShapeDtypeStruct((piece, features), LOW)
    vmem = pl.BlockSpec(memory_space=pltpu.VMEM)
    held = (mask, x, cot, *vectors)
    return pl.pallas_call(
        prepare_kernel,
        in_specs=[pl.BlockSpec(memory_space=pltpu.SMEM)] + [pl.BlockSpec(memory_space=pl.ANY)] * 13,
        out_specs=[vmem] * 7,
        out_shape=[
            part,
            part,
            part,
            jax.ShapeDtypeStruct((1, 128), SINGLE),
            jax.ShapeDtypeStruct((16, features), SINGLE),
        ]
        + [jax.ShapeDtypeStruct(w.shape, w.dtype) for w in weights],
        scratch_shapes=[pltpu.VMEM(v.shape, v.dtype) for v in held]
        + [pltpu.SemaphoreType.DMA((13,))],
        compiler_params=pltpu.CompilerParams(vmem_limit_bytes=8 << 20),
        cost_estimate=pl.CostEstimate(flops=2 * 10**9, bytes_accessed=1, transcendentals=0),
    )(rows, *in_hbm(held), *in_hbm(weights))


def join_row(place, mine_ref, other_ref, row_ref):
    piece = mine_ref.shape[0]
    row_ref[rows_at(place * piece, piece), :] = mine_ref[...].astype(row_ref.dtype)
    row_ref[rows_at((1 - place) * piece, piece), :] = other_ref[...].astype(row_ref.dtype)


def attend_kernel(
    up_ref, down_ref, x_mine, x_other, small, wqkv, wo,
    up, down, n1, qkv, probs, mixed_low, middle, n2, heads_q, sems,
):
    _, _, place = where_am_i()
    copies = [
        pltpu.make_async_copy(up_ref, up, sems.at[0]),
        pltpu.make_async_copy(down_ref, down, sems.at[1]),
    ]
    for copy in copies:
        copy.start()
    length, features = n1.shape
    groups = features // GW
    join_row(place, x_mine, x_other, middle)
    normal, _ = normalize(middle[...])
    n1[...] = (normal * small[0:1, :] + small[1:2, :]).astype(LOW)
    for which in range(3):
        value = dot_nn(n1[...], wqkv[:, which * features : (which + 1) * features])
        if which != 1:
            line = 2 + which // 2
            value = value + small[line : line + 1, :]
        value = value.astype(LOW)
        for group in range(groups):
            qkv[which * groups + group] = value[:, group * GW : (group + 1) * GW]
    allowed = lax.broadcasted_iota(jnp.int32, (length, length), 0) >= lax.broadcasted_iota(
        jnp.int32, (length, length), 1
    )
    lanes = lax.broadcasted_iota(jnp.int32, (1, GW), 1)

    def one_group(group, carry):
        query, keys, values = (qkv[which * groups + group] for which in range(3))
        spread_heads(query, heads_q, HD**-0.5)
        parts = []
        for head in range(GROUP):
            cut = slice(head * length, (head + 1) * length)
            scores = jnp.where(allowed, dot_nt(heads_q[cut, :], keys), NEGATIVE)
            powers = jnp.exp(scores - jnp.max(scores, axis=-1, keepdims=True))
            low = (powers * (1.0 / jnp.sum(powers, axis=-1, keepdims=True))).astype(LOW)
            probs[group, cut, :] = low
            parts.append(low)
        mixed = dot_nn(parts[0], values)
        for head in range(1, GROUP):
            mixed = jnp.where(lanes >= head * HD, dot_nn(parts[head], values), mixed)
        mixed_low[:, rows_at(group * GW, GW)] = mixed.astype(LOW)
        return carry

    lax.fori_loop(0, groups, one_group, 0)
    middle[...] += dot_nn(mixed_low[...], wo[...]) + small[4:5, :]
    normal, _ = normalize(middle[...])
    n2[...] = (normal * small[5:6, :] + small[6:7, :]).astype(LOW)
    for copy in copies:
        copy.wait()


def attend(x_mine, x_other, small, qkv_weight, out_weight, up_weight, down_weight):
    piece, features = x_other.shape
    length = 2 * piece
    groups = features // GW
    act = ((length, features), LOW)
    return call(
        "attend",
        attend_kernel,
        (x_mine, x_other, small, qkv_weight, out_weight),
        [
            act,
            ((3 * groups, length, GW), LOW),
            ((groups, GROUP * length, length), LOW),
            act,
            ((length, features), SINGLE),
            act,
        ],
        [((GROUP * length, GW), LOW)],
        loaded=(up_weight, down_weight),
    )


def gelu_and_slope(u):
    c = math.sqrt(2 / math.pi)
    square = u * u
    bent = jnp.tanh(u * (c + (c * 0.044715) * square))
    half = 0.5 + 0.5 * bent
    slope = half + u * (0.5 - 0.5 * bent * bent) * (c + (3 * c * 0.044715) * square)
    return u * half, slope


def feed_tiles(side, n2, db2, small, up, down, g, du, vec, total):
    tiles, _, features = g.shape

    def one_tile(tile, carry):
        number = side * tiles + tile
        cut = rows_at(number * features, features)
        line = pl.ds(8 + number, 1)
        hidden = dot_nn(n2[...], up[:, cut]) + small[line, :]
        active, slope = gelu_and_slope(hidden)
        g[tile] = active.astype(LOW)
        grad = (dot_nt(db2[...], down[cut, :]) * slope).astype(LOW)
        du[tile] = grad
        vec[line, :] = jnp.sum(grad.astype(SINGLE), axis=0, keepdims=True)
        total[...] += dot_nt(grad, up[:, cut])
        return carry

    lax.fori_loop(0, tiles, one_tile, 0)


def feed_one_kernel(
    n2, c_mine, c_other, small, count, up, down, g, du, db2, theirs, dn, vec,
):
    core, _, place = where_am_i()
    half = theirs.shape[1]
    join_row(place, c_mine, c_other, db2)
    theirs[...] = db2[:, rows_at((1 - core) * half, half)]
    vec[...] = jnp.zeros_like(vec)
    vec[7:8, :] = jnp.sum(db2[...].astype(SINGLE), axis=0, keepdims=True)
    vec[12:13, 0:128] = count[...]
    dn[...] = jnp.zeros_like(dn)
    feed_tiles(1 - core, n2, db2, small, up, down, g, du, vec, dn)


def feed_one(n2, c_mine, c_other, small, count, up, down):
    length, features = n2.shape
    tiles = up.shape[1] // 2 // features
    hid = ((tiles, length, features), LOW)
    return call(
        "feed_one",
        feed_one_kernel,
        (n2, c_mine, c_other, small, count, up, down),
        [
            hid, hid, ((length, features), LOW), ((length, features // 2), LOW),
            ((length, features), SINGLE), ((16, features), SINGLE),
        ],
    )


def feed_two_kernel(
    n2, db2, small, up, down, middle, dn, vec_in, g, du, dm, db1, theirs, vec,
):
    core, _, _ = where_am_i()
    half = theirs.shape[1]
    vec[...] = vec_in[...]
    dm[...] = dn[...]
    feed_tiles(core, n2, db2, small, up, down, g, du, vec, dm)
    grad_n = dm[...]
    normal, inverse = normalize(middle[...])
    vec[5:6, :] = jnp.sum(grad_n * normal, axis=0, keepdims=True)
    vec[6:7, :] = jnp.sum(grad_n, axis=0, keepdims=True)
    grad = db2[...].astype(SINGLE) + norm_back(normal, inverse, grad_n, small[5:6, :])
    dm[...] = grad
    low = grad.astype(LOW)
    db1[...] = low
    theirs[...] = db1[:, rows_at((1 - core) * half, half)]
    vec[4:5, :] = jnp.sum(low.astype(SINGLE), axis=0, keepdims=True)


def feed_two(n2, db2, small, up, down, middle, dn, vec_in):
    length, features = n2.shape
    tiles = up.shape[1] // 2 // features
    hid = ((tiles, length, features), LOW)
    return call(
        "feed_two",
        feed_two_kernel,
        (n2, db2, small, up, down, middle, dn, vec_in),
        [
            hid, hid, ((length, features), SINGLE), ((length, features), LOW),
            ((length, features // 2), LOW), ((16, features), SINGLE),
        ],
    )


def result_kernel(g_mine, g_theirs, middle, small, down, x_grad_send, y_mine, send, total):
    core, _, place = where_am_i()
    tiles, _, features = g_mine.shape
    piece = y_mine.shape[0]
    total[...] = middle[...] + small[7:8, :]

    def one_tile(tile, carry):
        for side, active in ((core, g_mine), (1 - core, g_theirs)):
            cut = rows_at((side * tiles + tile) * features, features)
            total[...] += dot_nn(active[tile], down[cut, :])
        return carry

    lax.fori_loop(0, tiles, one_tile, 0)
    present = small[12:13, :]
    y_mine[...] = (total[rows_at(place * piece, piece), :] * present).astype(LOW)
    send[0] = (total[rows_at((1 - place) * piece, piece), :] * present).astype(LOW)
    send[1] = x_grad_send[...]


def result(g_mine, g_theirs, middle, small, down, x_grad_send):
    length, features = middle.shape
    piece = length // 2
    return call(
        "result",
        result_kernel,
        (g_mine, g_theirs, middle, small, down, x_grad_send),
        [((piece, features), LOW), ((2, piece, features), LOW)],
        [((length, features), SINGLE)],
    )


def back_kernel(
    qkv, probs, db1, wo, vec_in, theirs, mine, vec, dp, heads_q, heads_k, heads_g, side,
):
    core, _, _ = where_am_i()
    features = db1.shape[1]
    groups = features // GW
    vec[...] = vec_in[...]

    def one_group(group, carry):
        cut = rows_at(group * GW, GW)
        grad_mixed = dot_nt(db1[...], wo[cut, :]).astype(LOW)
        query, keys, values = (qkv[which * groups + group] for which in range(3))
        spread_heads(grad_mixed, heads_g)
        spread_heads(query, heads_q, HD**-0.5)
        spread_heads(keys, heads_k, HD**-0.5)
        weights = probs[group].astype(SINGLE)
        grad_probs = dot_nt(heads_g[...], values)
        inner = jnp.sum(weights * grad_probs, axis=-1, keepdims=True)
        grad_scores = (weights * (grad_probs - inner)).astype(LOW)
        side_by_side(grad_scores, side)
        dv = dot_tn(probs[group], heads_g[...])
        dk = dot_tn(grad_scores, heads_q[...])
        dq = dot_nn(side[...], heads_k[...])
        for which, value in enumerate((dq, dk, dv)):
            low = value.astype(LOW)
            dp[:, rows_at(which * features + group * GW, GW)] = low
            if which != 1:
                line = 2 + which // 2
                vec[line : line + 1, cut] = jnp.sum(low.astype(SINGLE), axis=0, keepdims=True)
        return carry

    lax.fori_loop(0, groups, one_group, 0)
    half = mine.shape[1]
    theirs[...] = dp[:, rows_at((1 - core) * half, half)]
    mine[...] = dp[:, rows_at(core * half, half)]


def back(qkv, probs, db1, out_weight, vec_in):
    length, features = db1.shape
    half = ((length, 3 * features // 2), LOW)
    return call(
        "back",
        back_kernel,
        (qkv, probs, db1, out_weight, vec_in),
        [half, half, ((16, features), SINGLE)],
        [((length, 3 * features), LOW)]
        + [((GROUP * length, GW), LOW)] * 3
        + [((length, GROUP * length), LOW)],
    )


def input_kernel(
    x_mine, x_other, small, dp_mine, dp_theirs, wqkv, dm, vec_in, mine, send, vec, row,
):
    core, _, place = where_am_i()
    half = dp_mine.shape[1]
    piece = mine.shape[0]
    grad_n = dot_nt(dp_mine[...], wqkv[:, rows_at(core * half, half)])
    grad_n = grad_n + dot_nt(dp_theirs[...], wqkv[:, rows_at((1 - core) * half, half)])
    join_row(place, x_mine, x_other, row)
    normal, inverse = normalize(row[...])
    vec[...] = vec_in[...]
    vec[0:1, :] = jnp.sum(grad_n * normal, axis=0, keepdims=True)
    vec[1:2, :] = jnp.sum(grad_n, axis=0, keepdims=True)
    row[...] = dm[...] + norm_back(normal, inverse, grad_n, small[0:1, :])
    mine[...] = row[rows_at(place * piece, piece), :].astype(LOW)
    send[...] = row[rows_at((1 - place) * piece, piece), :].astype(LOW)


def input_gradient(x_mine, x_other, small, dp_mine, dp_theirs, qkv_weight, dm, vec_in):
    piece, features = x_other.shape
    part = ((piece, features), LOW)
    return call(
        "input",
        input_kernel,
        (x_mine, x_other, small, dp_mine, dp_theirs, qkv_weight, dm, vec_in),
        [part, part, ((16, features), SINGLE)],
        [((2 * piece, features), SINGLE)],
    )


UNITS = 16


def unit_of(name, number):
    core, own, place = where_am_i()
    units = []
    for order in WAYS[name]:
        unit = 0
        for stage, axis in enumerate(order):
            if number >> (3 - stage) & 1:
                unit |= 1 if axis == "x" else BITS[axis] << 1
        units.append(unit)
    return jnp.where(core == 0, units[0], units[1]) ^ (own * 2 + place)


def lanes_kernel(
    g_mine, g_theirs, other_mine, other_theirs, right, right_other, send, keep, turned, whole, *, name
):
    core, _, _ = where_am_i()
    chunks, tall, wide = whole.shape
    tiles, length, features = g_mine.shape
    per_tile = features // wide
    half = tall // 2
    turned[:, :length] = right[:, rows_at(core * tall, tall)].T
    turned[:, length:] = right_other[...].T
    for side, one, two in ((core, g_mine, other_theirs), (1 - core, g_theirs, other_mine)):

        def one_tile(tile, carry, side=side, one=one, two=two):
            total = dot_nn(turned[:, :length], one[tile]) + dot_nn(turned[:, length:], two[tile])
            total = total.astype(LOW)
            for chunk in range(per_tile):
                whole[(side * tiles + tile) * per_tile + chunk] = total[:, chunk * wide : (chunk + 1) * wide]
            return carry

        lax.fori_loop(0, tiles, one_tile, 0)
    for number in range(UNITS):
        unit = unit_of(name, number)
        out = send if number >= UNITS // 2 else keep
        out[number % (UNITS // 2)] = whole[lax.div(unit, 2), rows_at(lax.rem(unit, 2) * half, half), :]


def grad_lanes(name, mine, theirs, other_mine, other_theirs, right, right_other):
    tiles, length, features = mine.shape
    tall = right_other.shape[1]
    chunks = UNITS // 2
    wide = 2 * tiles * features // chunks
    unit = ((UNITS // 2, tall // 2, wide), LOW)
    return call(
        "lanes",
        functools.partial(lanes_kernel, name=name),
        (mine, theirs, other_mine, other_theirs, right, right_other),
        [unit, unit],
        [((tall, 2 * length), LOW), ((chunks, tall, wide), LOW)],
    )


def rows_kernel(left, left_other, right, right_other, *rest, name, pick_core):
    if len(rest) > 4:
        vec, vec_other, send, keep, turned, whole, spread = rest
    else:
        send, keep, turned, whole = rest
        vec = None
    core, _, _ = where_am_i()
    length = left.shape[0]
    split = len(right_other.shape) == 2
    tiles, tile = (1, right_other.shape[1]) if split else (right_other.shape[0], right_other.shape[2])
    turned[:, :length] = left[...].T
    turned[:, length:] = left_other[...].T
    rows = turned.shape[0] // UNITS
    units = [unit_of(name, number) for number in range(UNITS)]
    if vec is not None:
        total = vec[...] + vec_other[...]
        features = total.shape[1]
        part = 2 * rows
        spread[...] = jnp.zeros_like(spread)
        for chunk in range(UNITS // 2):
            spread[2 * chunk, 0:8, :part] = total[0:8, chunk * part : (chunk + 1) * part]
            for piece in range(4):
                line, begin = divmod((4 * chunk + piece) * part, features)
                spread[2 * chunk + 1, piece : piece + 1, :part] = total[
                    8 + line : 9 + line, begin : begin + part
                ]
            spread[2 * chunk + 1, 4:5, : 2 * DIGITS] = total[12:13, : 2 * DIGITS]
        for out in (send, keep):
            out[:, rows:, :] = jnp.zeros_like(out[:, rows:, :])

    def one_tile(step, carry):
        if split:
            here = right[:, rows_at(core * tile, tile)] if pick_core else right[...]
            there = right_other[...]
        else:
            here, there = right[step], right_other[step]
        whole[...] = (dot_nn(turned[:, :length], here) + dot_nn(turned[:, length:], there)).astype(LOW)
        columns = rows_at(step * tile, tile)
        for number, unit in enumerate(units):
            out = send if number >= UNITS // 2 else keep
            out[number % (UNITS // 2), :rows, columns] = whole[rows_at(unit * rows, rows), :]
        return carry

    if tiles == 1:
        one_tile(0, 0)
    else:
        lax.fori_loop(0, tiles, one_tile, 0)
    if vec is not None:
        for number, unit in enumerate(units):
            out = send if number >= UNITS // 2 else keep
            out[number % (UNITS // 2), rows:, :128] = spread[unit].astype(LOW)


def grad_rows(name, left, left_other, right, right_other, pick_core=False, vecs=()):
    length, tall = left.shape
    rows = tall // UNITS
    tile = right_other.shape[-1]
    width = math.prod(right_other.shape) // length
    unit = ((UNITS // 2, rows + (16 if vecs else 0), width), LOW)
    return call(
        "rows_" + name,
        functools.partial(rows_kernel, name=name, pick_core=pick_core),
        (left, left_other, right, right_other, *vecs),
        [unit, unit],
        [((tall, 2 * length), LOW), ((tall, tile), LOW)] + [((UNITS, 16, 128), SINGLE)] * bool(vecs),
    )


FIRST = ("o", "q", "d", "u")


PACK = 384


def packed_rows(name, shape):
    tall, width = shape
    return (tall - 16 if name == "o" else tall) * (width // PACK)


def pack_kernel(*refs):
    out = refs[-1]
    first = 0
    for number, part in enumerate(refs[:-1]):
        name = FIRST[number // 2]
        tall = part.shape[0] - (16 if name == "o" else 0)
        for block in range(part.shape[1] // PACK):
            out[first : first + tall, :] = part[:tall, block * PACK : (block + 1) * PACK]
            first += tall


def pack(parts):
    operands = [p for name in FIRST for p in parts[name]]
    rows = sum(packed_rows(name, p.shape) for name in FIRST for p in parts[name])
    return call("result", pack_kernel, operands, [((rows, PACK), LOW)])[0]


def finish_side(side, parts, share, out, turned, scratch, sems, copies):
    _, _, place = where_am_i()
    for number, name in enumerate(FIRST):
        tall, width = 0, 0
        for spot in (0, 1):
            low = place ^ spot
            blocks = parts(name, spot)
            tall, width = blocks[0].shape[0], PACK * len(blocks)
            for block, value in enumerate(blocks):
                value = value.astype(SINGLE)
                if name == "d":
                    turned[rows_at(low * tall, tall), :] = value
                else:
                    scratch[number][rows_at(low * tall, tall), block * PACK : (block + 1) * PACK] = (
                        value * share
                    )
        if name == "d":
            scratch[number][...] = turned[...].T * share
            width = scratch[number].shape[1]
        target = out[number].at[:, rows_at(side * width, width)]
        copies.append(pltpu.make_async_copy(scratch[number], target, sems.at[number]))
        copies[-1].start()


def own_kernel(*refs):
    homes, refs = refs[:3], refs[3:]
    given = {name: refs[2 * i : 2 * i + 2] for i, name in enumerate(FIRST)}
    refs = refs[2 * len(FIRST) :]
    grads, refs = refs[: len(FIRST)], refs[len(FIRST) :]
    count = (len(refs) - 4 - len(FIRST)) // 2
    results, share_out, refs = refs[:count], refs[count], refs[count + 1 :]
    scratch, held = refs[: len(FIRST)], refs[len(FIRST) : len(FIRST) + count]
    vec, turned, sems = refs[len(FIRST) + count :]
    core, _, place = where_am_i()
    copies = []

    def send(*numbers):
        for number in numbers:
            copies.append(
                pltpu.make_async_copy(held[number], results[number], sems.at[len(FIRST) + number])
            )
            copies[-1].start()

    for number in (0, 1):
        held[number][place] = homes[number][...]
        held[number][1 - place] = homes[2][number]
    send(0, 1)
    mine, other = given["o"]
    half = mine.shape[0] - 16
    vec[rows_at(place * 8, 8), :] = mine[half:, :128].astype(SINGLE)[:8]
    vec[rows_at((1 - place) * 8, 8), :] = other[half:, :128].astype(SINGLE)[:8]
    line = vec[12:13, :]
    lane = lax.broadcasted_iota(jnp.int32, line.shape, 1)
    worth = lax.shift_left(jnp.ones_like(lane), lax.rem(lane, DIGITS)).astype(SINGLE)
    first, second = (
        jnp.sum(jnp.where(lane // DIGITS == side, line * worth, 0.0), axis=1, keepdims=True)
        for side in (0, 1)
    )
    share = 1.0 / (first + second)
    share_out[...] = jnp.broadcast_to(share, share_out.shape)

    def parts(name, spot):
        part = given[name][spot]
        tall = part.shape[0] - (16 if name == "o" else 0)
        return [part[:tall, at : at + PACK] for at in range(0, part.shape[1], PACK)]

    finish_side(core, parts, share, grads, turned, scratch, sems, copies)
    counts, up, qv, *plain = held[2:]
    spot = lax.broadcasted_iota(jnp.int32, (1, 128), 1)
    counts[...] = jnp.where(spot == 0, first, second).astype(jnp.int32)[0, : counts.shape[0]]
    width = qv.shape[1]
    scaled = vec[...] * share
    qv[...] = scaled[2:4, :width]
    for number, out in zip((0, 1, 4, 5, 6, 7), plain):
        out[...] = scaled[number, :width]
    up[...] = jnp.concatenate([scaled[8 + part : 9 + part, :width] for part in range(4)], axis=1)[0]
    send(*range(2, count))
    for copy in copies:
        copy.wait()


def other_kernel(theirs, share, *refs):
    refs = refs[len(FIRST) :]
    grads, refs = refs[: len(FIRST)], refs[len(FIRST) :]
    scratch, (turned, sems) = refs[: len(FIRST)], refs[len(FIRST) :]
    core, _, _ = where_am_i()
    first = [0]

    def parts(name, spot):
        place = FIRST.index(name)
        tall, width = scratch[place].shape
        if name == "d":
            tall, width = turned.shape
        blocks = []
        for _ in range(width // PACK):
            blocks.append(theirs[first[0] : first[0] + tall // 2, :])
            first[0] += tall // 2
        return blocks

    copies = []
    finish_side(1 - core, parts, share[0:1, 0:1], grads, turned, scratch, sems, copies)
    for copy in copies:
        copy.wait()


def finale(homes, theirs, parts, rows):
    piece, features = homes[0].shape
    shapes, halves = [], []
    for name in FIRST:
        tall, width = parts[name][0].shape
        shapes.append((width, 4 * tall) if name == "d" else (2 * rows, 2 * width))
        halves.append(pltpu.VMEM((shapes[-1][0], shapes[-1][1] // 2), SINGLE))
    grads = [jax.ShapeDtypeStruct(s, SINGLE) for s in shapes]
    chunk = 2 * rows
    home = jax.ShapeDtypeStruct((2, piece, features), LOW)
    results = [
        home,
        home,
        jax.ShapeDtypeStruct((2,), jnp.int32),
        jax.ShapeDtypeStruct((4 * chunk,), SINGLE),
        jax.ShapeDtypeStruct((2, chunk), SINGLE),
    ] + [jax.ShapeDtypeStruct((chunk,), SINGLE)] * 6
    vmem = pl.BlockSpec(memory_space=pltpu.VMEM)
    anywhere = pl.BlockSpec(memory_space=pl.ANY)
    tall, width = parts["d"][0].shape
    turned = pltpu.VMEM((2 * tall, width), SINGLE)
    operands = [*homes, *[p for name in FIRST for p in parts[name]]]
    params = pltpu.CompilerParams(vmem_limit_bytes=16 << 20)
    own = pl.pallas_call(
        own_kernel,
        in_specs=[vmem] * len(operands),
        out_specs=[anywhere] * (len(grads) + len(results)) + [vmem],
        out_shape=grads + results + [jax.ShapeDtypeStruct((8, 128), SINGLE)],
        scratch_shapes=halves
        + [pltpu.VMEM(r.shape, r.dtype) for r in results]
        + [
            pltpu.VMEM((16, 128), SINGLE),
            turned,
            pltpu.SemaphoreType.DMA((len(grads) + len(results),)),
        ],
        compiler_params=params,
        cost_estimate=pl.CostEstimate(flops=40 * 10**9, bytes_accessed=1, transcendentals=0),
    )(*operands)
    grads_own, rest, share = own[: len(grads)], own[len(grads) : -1], own[-1]
    whole = pl.pallas_call(
        other_kernel,
        in_specs=[vmem, vmem] + [anywhere] * len(grads),
        out_specs=[anywhere] * len(grads),
        out_shape=grads,
        scratch_shapes=halves + [turned, pltpu.SemaphoreType.DMA((len(grads),))],
        input_output_aliases={2 + i: i for i in range(len(grads))},
        compiler_params=params,
        cost_estimate=pl.CostEstimate(flops=1, bytes_accessed=1, transcendentals=0),
    )(theirs, share, *grads_own)
    return [*rest[:2], *whole, *rest[2:]]


def swap_pairs(size, bit):
    return [(i, i ^ bit) for i in range(size)]


def partners(name, stage, groups):
    pairs = []
    for core in range(2):
        axis = WAYS[name][core][stage]
        for own in range(groups):
            for place in range(2):
                to = (own, place ^ 1) if axis == "x" else (own ^ BITS[axis], place)
                pairs.append(((core * groups + own) * 2 + place, (core * groups + to[0]) * 2 + to[1]))
    return pairs


def added(one, two):
    return (one.astype(SINGLE) + two.astype(SINGLE)).astype(LOW)


class Order:
    def __init__(self):
        self.last = None

    def tie(self, value):
        if self.last is not None:
            value, _ = lax.optimization_barrier((value, self.last))
        return value

    def mark(self, value):
        self.last = value


class Sum:
    def __init__(self, order, name, groups, send, keep):
        self.order, self.name, self.groups = order, name, groups
        self.keep = keep
        self.stage = 0
        self.whole_last = all(way[3] == "x" for way in WAYS[name])
        self.parts = None
        self.go(send)

    def go(self, send):
        self.flying = lax.ppermute(send, AXES, partners(self.name, self.stage, self.groups))

    def step(self):
        if self.parts is not None:
            return
        other = self.order.tie(self.flying)
        keep = self.keep
        self.stage += 1
        if self.stage == 5:
            self.order.mark(other)
            self.parts = [self.total, other]
        elif self.stage == 4 and self.whole_last:
            self.parts = [added(keep[0], other[1]), added(keep[1], other[0])]
            self.order.mark(self.parts[0])
        elif self.stage == 4:
            self.total = added(keep[0], other[0])
            self.order.mark(self.total)
            self.flying = lax.ppermute(self.total, "seq", swap_pairs(2, 1))
        elif self.stage == 3 and self.whole_last:
            self.keep = added(keep, other)
            self.order.mark(self.keep)
            self.go(self.keep)
        else:
            half = keep.shape[0] // 2
            send = added(keep[half:], other[half:])
            self.keep = added(keep[:half], other[:half])
            self.order.mark(send)
            self.go(send)


def body_fast(
    inputs,
    cotangent,
    row_counts,
    response_mask,
    norm1_gain,
    norm1_bias,
    qkv_weight,
    qv_bias,
    out_weight,
    out_bias,
    norm2_gain,
    norm2_bias,
    up_weight,
    up_bias,
    down_weight,
    down_bias,
):
    groups = lax.axis_size("dp")
    pair = swap_pairs(2, 1)
    core, own, place = (lax.axis_index(a) for a in ("src", "dp", "seq"))
    x_both = inputs[0, 0]
    x_other = lax.ppermute(
        lax.dynamic_index_in_dim(x_both, 1 - place, 0, keepdims=False), "seq", pair
    )
    x_mine, c_send, c_mine, count, small, qkv_weight, out_weight = prepare(
        row_counts,
        response_mask[0, 0],
        x_both,
        cotangent[0, 0],
        (norm1_gain, norm1_bias, qv_bias, out_bias, norm2_gain, norm2_bias, down_bias, up_bias),
        (qkv_weight, out_weight),
    )
    c_other = lax.ppermute(c_send, "seq", pair)
    order = Order()

    def from_core(value):
        return lax.ppermute(value, "src", pair)

    up_weight, down_weight, n1, qkv, probs, mixed, middle, n2 = attend(
        x_mine, x_other, small, qkv_weight, out_weight, up_weight, down_weight
    )
    g_theirs, du_theirs, db2, db2_theirs, dn, vec = feed_one(
        n2, c_mine, c_other, small, count, up_weight, down_weight
    )
    order.mark(vec)
    n2_other, n1_other, mixed_other = order.tie(
        (from_core(n2), from_core(n1), from_core(mixed))
    )
    here, n2_other, n1_other, mixed_other = lax.optimization_barrier(
        (n2, n2_other, n1_other, mixed_other)
    )
    g_mine, du_mine, dm, db1, db1_theirs, vec = feed_two(
        here, db2, small, up_weight, down_weight, middle, dn, vec
    )
    order.mark(vec)
    du_other, db2_other, other_theirs = order.tie(
        (from_core(du_theirs), from_core(db2_theirs), from_core(g_theirs))
    )
    here, du_other, db2_other, other_theirs = lax.optimization_barrier(
        (n2, du_other, db2_other, other_theirs)
    )
    other_mine, db1_other = from_core(g_mine), from_core(db1_theirs)

    sums = {}
    for event in EVENTS:
        if event == "h":
            homes = lax.ppermute(order.tie(home_send), "seq", pair)
            continue
        if event == "i":
            homes = order.tie(homes)
            order.mark(homes)
            continue
        if event.islower():
            sums[event].step()
            continue
        name = event.lower()
        if event == "U":
            parts = grad_rows(name, order.tie(here), n2_other, du_mine, du_other)
        elif event == "D":
            other_mine = order.tie(other_mine)
            here, other_mine = lax.optimization_barrier((g_mine, other_mine))
            parts = grad_lanes(name, here, g_theirs, other_mine, other_theirs, db2, db2_other)
        elif event == "C":
            here = order.tie(qkv)
            dp_theirs, dp_mine, vec = back(here, probs, db1, out_weight, vec)
            dp_other = from_core(dp_theirs)
            order.mark(vec)
            continue
        elif event == "I":
            x_grad_mine, x_grad_send, vec = input_gradient(
                order.tie(x_mine), x_other, small, dp_mine, dp_theirs, qkv_weight, dm, vec
            )
            vec_other = from_core(vec)
            order.mark(vec)
            continue
        elif event == "Y":
            y_mine, home_send = result(
                order.tie(g_mine), g_theirs, middle, small, down_weight, x_grad_send
            )
            order.mark(home_send)
            continue
        elif event == "O":
            parts = grad_rows(
                name, order.tie(mixed), mixed_other, db1, db1_other, True, (vec, vec_other)
            )
        else:
            dp_other, db1_other = order.tie((dp_other, db1_other))
            here, dp_other, db1_other = lax.optimization_barrier((n1, dp_other, db1_other))
            parts = grad_rows(name, here, n1_other, dp_mine, dp_other)
        order.mark(parts[0])
        sums[name] = Sum(order, name, groups, *parts)

    parts = order.tie({name: sums[name].parts for name in FIRST})
    rows = out_weight.shape[0] // groups // 2
    output, input_grad, out, qkv, down, up, counts, up_small, qv, *plain = finale(
        (y_mine, x_grad_mine, homes), from_core(pack(parts)), parts, rows
    )
    return (
        output[None, None],
        input_grad[None, None],
        counts,
        plain[0],
        plain[1],
        qkv,
        qv,
        out,
        plain[2],
        plain[3],
        plain[4],
        up,
        up_small,
        down,
        plain[5],
    )


def solution(mesh):
    placed = (
        P("src", "dp", None, "seq", None),
        P("src", "dp", None, "seq", None),
        P("src", "dp"),
        P("src", "dp", None, "seq"),
        P(),
        P(),
        P(),
        P(),
        P(),
        P(),
        P(),
        P(),
        P(),
        P(),
        P(),
        P(),
    )
    sizes = dict(mesh.shape)
    paired = sizes["src"] == 2 and sizes["seq"] == 2 and sizes["dp"] == 8
    return jax.shard_map(
        body_fast if paired else body_generic,
        mesh=mesh,
        in_specs=placed,
        out_specs=(
            P("src", "dp", None, "seq", None),
            P("src", "dp", None, "seq", None),
            P(),
            P("dp"),
            P("dp"),
            P("dp", None),
            P(None, "dp"),
            P("dp", None),
            P("dp"),
            P("dp"),
            P("dp"),
            P("dp", None),
            P("dp"),
            P("dp", None),
            P("dp"),
        ),
        check_vma=False,
    )
```
